32 devices in a mesh: ctx: 4 (over z), fsdp: 8 (over y, x, core).
Axes of the slice: x: 2, y: 2, z: 4, core: 2. Of those that a mesh axis runs over, the one named last changes fastest.
Arguments:
- tokens: bfloat16 [4096, 2048], P(('ctx', 'fsdp')), may hold values from -6 to 6
- pair_index: int32 [4], replicated, may hold values from 0 to 3, each once
- gain_attn: bfloat16 [2048], P(('ctx', 'fsdp')), may hold values from 0.5 to 1.5
- w_query: bfloat16 [2048, 2048], P(('ctx', 'fsdp')), may hold values from -0.125 to 0.125
- w_key: bfloat16 [2048, 2048], P(('ctx', 'fsdp')), may hold values from -0.125 to 0.125
- w_value: bfloat16 [2048, 2048], P(('ctx', 'fsdp')), may hold values from -0.125 to 0.125
- w_out: bfloat16 [2048, 2048], P(('ctx', 'fsdp')), may hold values from -0.5 to 0.5
- gain_ffn: bfloat16 [2048], P(('ctx', 'fsdp')), may hold values from 0.5 to 1.5
- w_gate: bfloat16 [8192, 2048], P(('ctx', 'fsdp')), may hold values from -0.125 to 0.125
- w_up: bfloat16 [8192, 2048], P(('ctx', 'fsdp')), may hold values from -0.125 to 0.125
- w_down: bfloat16 [8192, 2048], P(('ctx', 'fsdp')), may hold values from -0.0625 to 0.0625
- cotangent: bfloat16 [4096, 2048], P(('ctx', 'fsdp')), may hold values from -6 to 6
Outputs:
- block_out: bfloat16 [4096, 2048], P(('ctx', 'fsdp'))
- input_grad: float32 [4096, 2048], P(('ctx', 'fsdp'))
- gain_attn_grad: float32 [2048], P(('ctx', 'fsdp'))
- query_grad: float32 [2048, 2048], P(('ctx', 'fsdp'))
- key_grad: float32 [2048, 2048], P(('ctx', 'fsdp'))
- value_grad: float32 [2048, 2048], P(('ctx', 'fsdp'))
- out_grad: float32 [2048, 2048], P(('ctx', 'fsdp'))
- gain_ffn_grad: float32 [2048], P(('ctx', 'fsdp'))
- gate_grad: float32 [8192, 2048], P(('ctx', 'fsdp'))
- up_grad: float32 [8192, 2048], P(('ctx', 'fsdp'))
- down_grad: float32 [8192, 2048], P(('ctx', 'fsdp'))
The draws below stay inside these ranges and needn't reach their ends.
Inputs may be any that keep to these rules, and one draw needn't show every extreme that they name: Ctx group c holds sequence blocks pair_index[c] and 7 - pair_index[c] of 512 tokens each, rows of the lower block first; every value occurs once.
All inputs are finite; a program needn't handle non-finite values.
Results may differ from the reference program's by a relative error of at most 0.019.
Values may be sent and summed in bfloat16 or wider, within the bound.
No kernel may reach another device: no remote copies, remote signals or barrier semaphores. Data moves between devices by JAX's collectives and lax.ppermute only.
A program may use at most 256 MiB of HBM per device.

```python
import math
import jax
import jax.numpy as jnp
from jax import lax

D = 2048
H = 32
HD = 64
FF = 8192
TOKENS = 4096
BLK = 512
N_CTX = 4


def shard_levels(own_key, extent, cuts, least, largest):
    level = 1.0
    for dim, blocks in cuts:
        heights = jax.random.uniform(jax.random.fold_in(jax.random.fold_in(own_key, 6), dim), (blocks,), jnp.float32, least / len(cuts), largest / len(cuts))
        level = level * jnp.repeat(jnp.exp(heights), extent[dim] // blocks).reshape((-1,) + (1,) * (len(extent) - 1 - dim))
    return level


def centred(own_key, shape, scale, reach, shards=(), kind=jnp.bfloat16):
    values = jax.random.normal(own_key, shape, jnp.float32) * scale
    if len(shards) > 0:
        values = shard_levels(own_key, shape, shards, -0.22, 0.18) * values
    return jnp.clip(values, min=-reach, max=reach).astype(kind)


def setup_inputs(seed: int = 0) -> dict:
    streams_of = jax.random.split(jax.random.key(seed), 13)
    return {
        "tokens": centred(streams_of[0], (TOKENS, D), 1.0, 6.0, ((0, 32),)),
        "pair_index": jax.random.permutation(streams_of[1], N_CTX).astype(jnp.int32),
        "gain_attn": jnp.clip(1.0 + 0.1 * jax.random.normal(streams_of[2], (D,), jnp.float32), 0.5, 1.5).astype(jnp.bfloat16),
        "w_query": centred(streams_of[3], (D, D), D ** -0.5, 0.125, ((0, 32),)),
        "w_key": centred(streams_of[4], (D, D), D ** -0.5, 0.125, ((0, 32),)),
        "w_value": centred(streams_of[5], (D, D), D ** -0.5, 0.125, ((0, 32),)),
        "w_out": centred(streams_of[6], (D, D), (max(1, D * 256 // TOKENS)) ** -0.5, 0.5, ((0, 32),)),
        "gain_ffn": jnp.clip(1.0 + 0.1 * jax.random.normal(streams_of[7], (D,), jnp.float32), 0.5, 1.5).astype(jnp.bfloat16),
        "w_gate": centred(streams_of[8], (FF, D), D ** -0.5, 0.125, ((0, 32),)),
        "w_up": centred(streams_of[9], (FF, D), D ** -0.5, 0.125, ((0, 32),)),
        "w_down": centred(streams_of[10], (FF, D), FF ** -0.5, 0.0625, ((0, 32),)),
        "cotangent": centred(streams_of[11], (TOKENS, D), 1.0, 6.0, ((0, 32),)),
    }


@jax.custom_vjp
def low(v):
    return lax.optimization_barrier(v.astype(jnp.bfloat16)).astype(jnp.float32)

@jax.custom_vjp
def low_back(v):
    return v

def low_keep(v):
    return (low(v), None)

def low_pass(kept, grad):
    return (grad,)

def back_keep(v):
    return (v, None)

def back_low(kept, grad):
    return (low(grad),)
low.defvjp(low_keep, low_pass)
low_back.defvjp(back_keep, back_low)
EPS = 1e-05
THETA = 130000.0
HIGH = lax.Precision.HIGHEST

def positions_of(pair_index):
    rows = jnp.arange(TOKENS, dtype=jnp.int32)
    group = rows // (2 * BLK)
    within = rows % (2 * BLK)
    match = group[:, None] == jnp.arange(N_CTX, dtype=jnp.int32)[None, :]
    pair = lax.optimization_barrier(jnp.sum(jnp.where(match, pair_index[None, :], 0), axis=1)).astype(jnp.int32)
    block = jnp.where(within < BLK, pair, 2 * N_CTX - 1 - pair)
    return (block * BLK + within % BLK).astype(jnp.int32)

def rotate(flat, cosine, sine):
    rows = flat.shape[0]
    split = flat.reshape(rows, H, HD)
    half = HD // 2
    first = split[..., :half]
    second = split[..., half:]
    cos_b = cosine[:, None, :]
    sin_b = sine[:, None, :]
    out = jnp.concatenate([first * cos_b - second * sin_b, second * cos_b + first * sin_b], axis=-1)
    return out.reshape(rows, H * HD)

def rms_norm(value, gain):
    return value * lax.rsqrt(lax.optimization_barrier(jnp.mean(value * value, axis=-1, keepdims=True)) + EPS) * gain

def attend(query, key, value, places):
    scale = HD ** (-0.5)
    step = math.gcd(TOKENS, 256)
    count = TOKENS // step
    keys = key.reshape(TOKENS, H, HD)
    values = value.reshape(TOKENS, H, HD)
    qblocks = query.reshape(count, step, H, HD)
    pblocks = places.reshape(count, step)

    def one_block(args):
        qblock, qplace = args
        raw = jnp.einsum('qhd,khd->hqk', qblock, keys, precision=HIGH) * scale
        scores = low_back(raw)
        keep = places[None, None, :] <= qplace[None, :, None]
        scores = jnp.where(keep, scores, -1e+30)
        top = lax.optimization_barrier(jnp.max(scores, axis=-1, keepdims=True))
        expo = jnp.exp(scores - top)
        prob = expo / lax.optimization_barrier(jnp.sum(expo, axis=-1, keepdims=True))
        return jnp.einsum('hqk,khd->qhd', low(prob), values, precision=HIGH)
    out = lax.map(jax.checkpoint(one_block), (qblocks, pblocks))
    return out.reshape(TOKENS, H * HD)

def reference(tokens, pair_index, gain_attn, w_query, w_key, w_value, w_out, gain_ffn, w_gate, w_up, w_down, cotangent):
    places = positions_of(pair_index)
    freq = jnp.exp(jnp.arange(HD // 2, dtype=jnp.float32) * (-2.0 * math.log(THETA) / HD))
    angle = places.astype(jnp.float32)[:, None] * freq[None, :]
    cosine = jnp.cos(angle)
    sine = jnp.sin(angle)

    def forward(x, g_one, wq, wk, wv, wo, g_two, wg, wu, wd):
        normed_one = low(rms_norm(x, g_one))
        query = low(rotate(low_back(jnp.dot(normed_one, wq, precision=HIGH)), cosine, sine))
        key = low(rotate(low_back(jnp.dot(normed_one, wk, precision=HIGH)), cosine, sine))
        value = low(low_back(jnp.dot(normed_one, wv, precision=HIGH)))
        attn = low(low_back(attend(query, key, value, places)))
        mid = x + low_back(jnp.dot(attn, wo, precision=HIGH))
        normed_two = low(rms_norm(mid, g_two))
        gate = low_back(jnp.dot(normed_two, wg.T, precision=HIGH))
        upper = low_back(jnp.dot(normed_two, wu.T, precision=HIGH))
        hidden = low(jax.nn.silu(gate) * upper)
        return mid + low_back(jnp.dot(hidden, wd, precision=HIGH))
    inputs = [a.astype(jnp.float32) for a in (tokens, gain_attn, w_query, w_key, w_value, w_out, gain_ffn, w_gate, w_up, w_down)]
    result, pullback = jax.vjp(forward, *inputs)
    grads = pullback(cotangent.astype(jnp.float32))
    return (result.astype(jnp.bfloat16), grads[0], grads[1], grads[2], grads[3], grads[4], grads[5], grads[6], grads[7], grads[8], grads[9])
```

```python
import functools
import math

import jax
import jax.numpy as jnp
import numpy as np
from jax import lax
from jax.experimental import pallas as pl
from jax.experimental.pallas import tpu as pltpu
from jax.sharding import Mesh
from jax.sharding import PartitionSpec as P

HD = 64


EPS = 1e-05
THETA = 130000.0


def place_of(rows, pair_index, n_groups, blk):
    group = rows // (2 * blk)
    within = rows % (2 * blk)
    match = group[:, None] == jnp.arange(n_groups, dtype=jnp.int32)[None, :]
    pair = jnp.sum(jnp.where(match, pair_index[None, :], 0), axis=1)
    block = jnp.where(within < blk, pair, 2 * n_groups - 1 - pair)
    return block * blk + within % blk


def tables(places, head_dim):
    freq = jnp.exp(
        jnp.arange(head_dim // 2, dtype=jnp.float32) * (-2.0 * math.log(THETA) / head_dim)
    )
    angle = places.astype(jnp.float32)[:, None] * freq[None, :]
    return (jnp.cos(angle), jnp.sin(angle))


def rotate(flat, cosine, sine, head_dim):
    rows = flat.shape[0]
    split = flat.reshape(rows, -1, head_dim)
    half = head_dim // 2
    first = split[..., :half]
    second = split[..., half:]
    cos_b = cosine[:, None, :]
    sin_b = sine[:, None, :]
    out = jnp.concatenate([first * cos_b - second * sin_b, second * cos_b + first * sin_b], axis=-1)
    return out.reshape(rows, -1)


def silu_parts(gate):
    sig = jax.nn.sigmoid(gate)
    return (gate * sig, sig * (1.0 + gate * (1.0 - sig)))


def rows_by(left, right):
    return jnp.einsum("td,fd->tf", left, right, preferred_element_type=jnp.float32)


def outer_sum(left, right):
    return jnp.einsum("tf,td->fd", left, right, preferred_element_type=jnp.float32)


def per_device_any(
    tokens,
    pair_index,
    gain_attn,
    w_query,
    w_key,
    w_value,
    w_out,
    gain_ffn,
    w_gate,
    w_up,
    w_down,
    cotangent,
):
    f32 = jnp.float32
    bf16 = jnp.bfloat16
    n_ctx = lax.axis_size("ctx")
    n_fsdp = lax.axis_size("fsdp")
    tok = tokens.shape[0]
    group_rows = tok * n_fsdp
    blk = group_rows // 2
    total = group_rows * n_ctx
    ctx_index = lax.axis_index("ctx")
    fsdp_index = lax.axis_index("fsdp")
    local_rows = (ctx_index * n_fsdp + fsdp_index) * tok + jnp.arange(tok, dtype=jnp.int32)
    local_places = place_of(local_rows, pair_index, n_ctx, blk)
    group_places = place_of(
        ctx_index * group_rows + jnp.arange(group_rows, dtype=jnp.int32), pair_index, n_ctx, blk
    )
    key_places = place_of(jnp.arange(total, dtype=jnp.int32), pair_index, n_ctx, blk)
    group_cos, group_sin = tables(group_places, HD)
    query_full, key_full, value_full, out_full, gain_one, gain_two = (
        lax.all_gather(w_query, ("ctx", "fsdp"), axis=0, tiled=True),
        lax.all_gather(w_key, ("ctx", "fsdp"), axis=0, tiled=True),
        lax.all_gather(w_value, ("ctx", "fsdp"), axis=0, tiled=True),
        lax.all_gather(w_out, ("ctx", "fsdp"), axis=0, tiled=True),
        lax.all_gather(gain_attn, ("ctx", "fsdp"), axis=0, tiled=True),
        lax.all_gather(gain_ffn, ("ctx", "fsdp"), axis=0, tiled=True),
    )
    gain_one = gain_one.astype(f32)
    gain_two = gain_two.astype(f32)
    x32 = tokens.astype(f32)
    scale_one = lax.rsqrt(jnp.mean(x32 * x32, axis=-1, keepdims=True) + EPS)
    normed_one = (x32 * scale_one * gain_one).astype(bf16)
    cosine, sine = tables(local_places, HD)
    query = rotate(
        jnp.dot(normed_one, query_full, preferred_element_type=f32), cosine, sine, HD
    ).astype(bf16)
    key = rotate(
        jnp.dot(normed_one, key_full, preferred_element_type=f32), cosine, sine, HD
    ).astype(bf16)
    value = jnp.dot(normed_one, value_full, preferred_element_type=f32).astype(bf16)
    query_heads, key_heads, value_heads = (
        lax.all_to_all(query, "fsdp", split_axis=1, concat_axis=0, tiled=True),
        lax.all_to_all(key, "fsdp", split_axis=1, concat_axis=0, tiled=True),
        lax.all_to_all(value, "fsdp", split_axis=1, concat_axis=0, tiled=True),
    )
    key_all, value_all = (
        lax.all_gather(key_heads, "ctx", axis=0, tiled=True),
        lax.all_gather(value_heads, "ctx", axis=0, tiled=True),
    )
    local_width = query_heads.shape[1]
    heads_here = local_width // HD
    scale = HD ** (-0.5)
    query_parts = query_heads.reshape(2, blk, heads_here, HD)
    query_place_tiles = group_places.reshape(2, blk)
    key_tiles = key_all.reshape(2 * n_ctx, blk, heads_here, HD)
    value_tiles = value_all.reshape(2 * n_ctx, blk, heads_here, HD)
    key_place_tiles = key_places.reshape(2 * n_ctx, blk)

    def tile_scores(slot, keys, k_place):
        raw = (
            jnp.einsum("qhd,khd->hqk", query_parts[slot], keys, preferred_element_type=f32) * scale
        )
        keep = k_place[None, None, :] <= query_place_tiles[slot][None, :, None]
        return jnp.where(keep, raw, -1e30)

    def is_live(slot, k_place):
        return jnp.min(k_place) <= jnp.max(query_place_tiles[slot])

    def first_pass(carry, tile):
        keys, k_place = tile
        highs, totals = carry
        new_highs = []
        new_totals = []
        for slot in range(2):

            def first_update(high, summed):
                masked = tile_scores(slot, keys, k_place)
                fresh = jnp.maximum(high, jnp.max(masked, axis=-1))
                summed = summed * jnp.exp(high - fresh) + jnp.sum(
                    jnp.exp(masked - fresh[..., None]), axis=-1
                )
                return (fresh, summed)

            def first_leave(high, summed):
                return (high, summed)

            high, summed = lax.cond(
                is_live(slot, k_place), first_update, first_leave, highs[slot], totals[slot]
            )
            new_highs.append(high)
            new_totals.append(summed)
        return ((jnp.stack(new_highs), jnp.stack(new_totals)), None)

    start_high = jnp.full((2, heads_here, blk), -1e30, f32)
    start_total = jnp.zeros((2, heads_here, blk), f32)
    (highs, totals), unused = lax.scan(
        first_pass, (start_high, start_total), (key_tiles, key_place_tiles)
    )
    log_total = highs + jnp.log(totals)

    def second_pass(carry, tile):
        keys, values, k_place = tile
        outs = []
        for slot in range(2):

            def second_update(acc):
                masked = tile_scores(slot, keys, k_place)
                prob_low = jnp.exp(masked - log_total[slot][..., None]).astype(bf16)
                return acc + jnp.einsum(
                    "hqk,khd->qhd", prob_low, values, preferred_element_type=f32
                )

            def second_leave(acc):
                return acc

            outs.append(lax.cond(is_live(slot, k_place), second_update, second_leave, carry[slot]))
        return (jnp.stack(outs), None)

    acc_start = jnp.zeros((2, blk, heads_here, HD), f32)
    attn_acc, unused = lax.scan(second_pass, acc_start, (key_tiles, value_tiles, key_place_tiles))
    attn32 = attn_acc.reshape(group_rows, local_width)
    attn_tokens = lax.all_to_all(
        attn32.astype(bf16), "fsdp", split_axis=0, concat_axis=1, tiled=True
    )
    mid = x32 + jnp.dot(attn_tokens, out_full, preferred_element_type=f32)
    scale_two = lax.rsqrt(jnp.mean(mid * mid, axis=-1, keepdims=True) + EPS)
    normed_two = (mid * scale_two * gain_two).astype(bf16)
    dy = cotangent.astype(f32)
    dy_low = dy.astype(bf16)
    gate_local, up_local, down_local = (
        lax.all_gather(w_gate, "ctx", axis=0, tiled=True),
        lax.all_gather(w_up, "ctx", axis=0, tiled=True),
        lax.all_gather(w_down, "ctx", axis=0, tiled=True),
    )
    rows_all = lax.all_gather(normed_two, "fsdp", axis=0, tiled=True)
    gate_all = rows_by(rows_all, gate_local)
    up_all = rows_by(rows_all, up_local)
    silu_all, unused_slope = silu_parts(gate_all)
    hidden_all = (silu_all * up_all).astype(bf16)
    branch = lax.psum_scatter(
        jnp.dot(hidden_all, down_local, preferred_element_type=f32).astype(jnp.bfloat16),
        "fsdp",
        scatter_dimension=0,
        tiled=True,
    ).astype(jnp.float32)
    block_out = (mid + branch).astype(bf16)
    grad_rows_all = lax.all_gather(dy_low, "fsdp", axis=0, tiled=True)
    dhidden = rows_by(grad_rows_all, down_local)
    silu_val, slope = silu_parts(gate_all)
    dgate = (dhidden * up_all * slope).astype(bf16)
    dup = (dhidden * silu_val).astype(bf16)
    gate_term = outer_sum(dgate, rows_all)
    up_term = outer_sum(dup, rows_all)
    down_term = outer_sum(hidden_all, grad_rows_all)
    gate_grad, up_grad, down_grad = (
        lax.psum_scatter(
            gate_term.astype(jnp.bfloat16), "ctx", scatter_dimension=0, tiled=True
        ).astype(jnp.float32),
        lax.psum_scatter(
            up_term.astype(jnp.bfloat16), "ctx", scatter_dimension=0, tiled=True
        ).astype(jnp.float32),
        lax.psum_scatter(
            down_term.astype(jnp.bfloat16), "ctx", scatter_dimension=0, tiled=True
        ).astype(jnp.float32),
    )
    dnormed_two = lax.psum_scatter(
        (
            jnp.dot(dgate, gate_local, preferred_element_type=f32)
            + jnp.dot(dup, up_local, preferred_element_type=f32)
        ).astype(jnp.bfloat16),
        "fsdp",
        scatter_dimension=0,
        tiled=True,
    ).astype(jnp.float32)
    gain_two_term = jnp.sum(dnormed_two * mid * scale_two, axis=0)
    scaled_two = gain_two * dnormed_two
    dmid = (
        dy
        + scale_two * scaled_two
        - mid * scale_two**3 * jnp.mean(scaled_two * mid, axis=-1, keepdims=True)
    )
    dmid_low = dmid.astype(bf16)
    out_term = jnp.einsum("td,te->de", attn_tokens, dmid_low, preferred_element_type=f32)
    dattn = jnp.einsum("te,de->td", dmid_low, out_full, preferred_element_type=f32).astype(bf16)
    dattn_heads = lax.all_to_all(dattn, "fsdp", split_axis=1, concat_axis=0, tiled=True)
    delta = jnp.sum((dattn_heads.astype(f32) * attn32).reshape(group_rows, heads_here, HD), axis=-1)
    delta_tiles = delta.reshape(2, blk, heads_here).transpose(0, 2, 1)
    grad_parts = dattn_heads.reshape(2, blk, heads_here, HD)

    def back_pass(carry, tile):
        keys, values, k_place = tile
        key_acc = jnp.zeros((blk, heads_here, HD), f32)
        value_acc = jnp.zeros((blk, heads_here, HD), f32)
        new_query = []
        for slot in range(2):

            def back_update(q_acc, k_acc, v_acc):
                masked = tile_scores(slot, keys, k_place)
                prob = jnp.exp(masked - log_total[slot][..., None])
                prob_low = prob.astype(bf16)
                dprob = jnp.einsum(
                    "qhd,khd->hqk", grad_parts[slot], values, preferred_element_type=f32
                )
                dscore = (prob * (dprob - delta_tiles[slot][..., None])).astype(bf16)
                q_acc = (
                    q_acc
                    + jnp.einsum("hqk,khd->qhd", dscore, keys, preferred_element_type=f32) * scale
                )
                k_acc = (
                    k_acc
                    + jnp.einsum(
                        "hqk,qhd->khd", dscore, query_parts[slot], preferred_element_type=f32
                    )
                    * scale
                )
                v_acc = v_acc + jnp.einsum(
                    "hqk,qhd->khd", prob_low, grad_parts[slot], preferred_element_type=f32
                )
                return (q_acc, k_acc, v_acc)

            def back_leave(q_acc, k_acc, v_acc):
                return (q_acc, k_acc, v_acc)

            q_acc, key_acc, value_acc = lax.cond(
                is_live(slot, k_place), back_update, back_leave, carry[slot], key_acc, value_acc
            )
            new_query.append(q_acc)
        return (jnp.stack(new_query), (key_acc, value_acc))

    dquery_start = jnp.zeros((2, blk, heads_here, HD), f32)
    dquery_acc, (dkey_tiles, dvalue_tiles) = lax.scan(
        back_pass, dquery_start, (key_tiles, value_tiles, key_place_tiles)
    )
    dkey_all = dkey_tiles.reshape(total, local_width)
    dvalue_all = dvalue_tiles.reshape(total, local_width)
    dkey_own, dvalue_own = (
        lax.psum_scatter(
            dkey_all.astype(jnp.bfloat16), "ctx", scatter_dimension=0, tiled=True
        ).astype(jnp.float32),
        lax.psum_scatter(
            dvalue_all.astype(jnp.bfloat16), "ctx", scatter_dimension=0, tiled=True
        ).astype(jnp.float32),
    )
    dquery_low = rotate(
        dquery_acc.reshape(group_rows, local_width), group_cos, -group_sin, HD
    ).astype(bf16)
    dkey_low = rotate(dkey_own, group_cos, -group_sin, HD).astype(bf16)
    dvalue_low = dvalue_own.astype(bf16)
    dquery_tok, dkey_tok, dvalue_tok = (
        lax.all_to_all(dquery_low, "fsdp", split_axis=0, concat_axis=1, tiled=True),
        lax.all_to_all(dkey_low, "fsdp", split_axis=0, concat_axis=1, tiled=True),
        lax.all_to_all(dvalue_low, "fsdp", split_axis=0, concat_axis=1, tiled=True),
    )
    dnormed_one = (
        jnp.einsum("te,de->td", dquery_tok, query_full, preferred_element_type=f32)
        + jnp.einsum("te,de->td", dkey_tok, key_full, preferred_element_type=f32)
        + jnp.einsum("te,de->td", dvalue_tok, value_full, preferred_element_type=f32)
    )
    query_term = jnp.einsum("td,te->de", normed_one, dquery_tok, preferred_element_type=f32)
    key_term = jnp.einsum("td,te->de", normed_one, dkey_tok, preferred_element_type=f32)
    value_term = jnp.einsum("td,te->de", normed_one, dvalue_tok, preferred_element_type=f32)
    gain_one_term = jnp.sum(dnormed_one * x32 * scale_one, axis=0)
    scaled_one = gain_one * dnormed_one
    input_grad = (
        dmid
        + scale_one * scaled_one
        - x32 * scale_one**3 * jnp.mean(scaled_one * x32, axis=-1, keepdims=True)
    )
    query_grad, key_grad, value_grad, out_grad, gain_attn_grad, gain_ffn_grad = (
        lax.psum_scatter(query_term, ("ctx", "fsdp"), scatter_dimension=0, tiled=True),
        lax.psum_scatter(key_term, ("ctx", "fsdp"), scatter_dimension=0, tiled=True),
        lax.psum_scatter(value_term, ("ctx", "fsdp"), scatter_dimension=0, tiled=True),
        lax.psum_scatter(out_term, ("ctx", "fsdp"), scatter_dimension=0, tiled=True),
        lax.psum_scatter(gain_one_term, ("ctx", "fsdp"), scatter_dimension=0, tiled=True),
        lax.psum_scatter(gain_two_term, ("ctx", "fsdp"), scatter_dimension=0, tiled=True),
    )
    return (
        block_out,
        input_grad,
        gain_attn_grad,
        query_grad,
        key_grad,
        value_grad,
        out_grad,
        gain_ffn_grad,
        gate_grad,
        up_grad,
        down_grad,
    )


BF16 = jnp.bfloat16
F32 = jnp.float32
LOG2E = math.log2(math.e)
VMEM = pl.BlockSpec(memory_space=pltpu.VMEM)


def mxu(a, b):
    return jnp.dot(a, b, preferred_element_type=F32)


def causal(blk):
    row = lax.broadcasted_iota(jnp.int32, (blk, blk), 0)
    col = lax.broadcasted_iota(jnp.int32, (blk, blk), 1)
    return row <= col


def attn_fwd_kernel(
    slot_ref, qkv_ref, out_ref, o32_ref, lse_ref, seq_ref, k_scr, m_scr, l_scr, acc_scr, *, blocks, width
):
    pieces = qkv_ref.shape[0]
    blk = pieces * width
    coef = LOG2E * HD**-0.5
    for s in range(blocks):
        at = pl.multiple_of(slot_ref[s] * width, width)
        for j in range(pieces):
            lo = s * blk + j * width
            piece = qkv_ref[j, :, pl.ds(at, width)]
            seq_ref[:, lo : lo + width] = piece
            k_scr[lo : lo + width, :] = piece[HD : 2 * HD].T

    def tile(kb, q_t, masked):
        at = pl.multiple_of(kb * blk, blk)
        score = mxu(k_scr[pl.ds(at, blk), :], q_t) * coef
        if masked:
            score = jnp.where(causal(blk), score, -1e30)
        old = m_scr[...]
        new = jnp.maximum(old, jnp.max(score, axis=0, keepdims=True))
        p = jnp.exp2(score - new)
        fade = jnp.exp2(old - new)
        m_scr[...] = new
        l_scr[...] = l_scr[...] * fade + jnp.sum(p, axis=0, keepdims=True)
        acc_scr[...] = acc_scr[...] * fade + mxu(seq_ref[2 * HD :, pl.ds(at, blk)], p.astype(BF16))

    for qb in range(blocks):
        lo = qb * blk
        q_t = seq_ref[:HD, lo : lo + blk]
        m_scr[...] = jnp.full_like(m_scr, -1e30)
        l_scr[...] = jnp.zeros_like(l_scr)
        acc_scr[...] = jnp.zeros_like(acc_scr)
        tile(qb, q_t, True)
        if qb > 0:

            @pl.loop(0, qb)
            def _(kb):
                tile(kb, q_t, False)

        o = acc_scr[...] / l_scr[...]
        o32_ref[:, lo : lo + blk] = o
        lse_ref[:, lo : lo + blk] = m_scr[...] + jnp.log2(l_scr[...])
        at = pl.multiple_of(slot_ref[qb] * width, width)
        low = o.astype(BF16)
        for j in range(pieces):
            out_ref[j, :, pl.ds(at, width)] = low[:, j * width : (j + 1) * width]


def attn_fwd(slot, qkv, blocks):
    pieces, _, cols = qkv.shape
    total = pieces * cols
    blk = total // blocks
    return pl.pallas_call(
        functools.partial(attn_fwd_kernel, blocks=blocks, width=cols // blocks),
        out_shape=(
            jax.ShapeDtypeStruct((pieces, HD, cols), BF16),
            jax.ShapeDtypeStruct((HD, total), F32),
            jax.ShapeDtypeStruct((1, total), F32),
            jax.ShapeDtypeStruct((3 * HD, total), BF16),
        ),
        in_specs=[pl.BlockSpec(memory_space=pltpu.SMEM), VMEM],
        out_specs=(VMEM,) * 4,
        scratch_shapes=[
            pltpu.VMEM((total, HD), BF16),
            pltpu.VMEM((1, blk), F32),
            pltpu.VMEM((1, blk), F32),
            pltpu.VMEM((HD, blk), F32),
        ],
        compiler_params=pltpu.CompilerParams(vmem_limit_bytes=40 << 20),
        cost_estimate=pl.CostEstimate(
            flops=8 * total * total * HD, bytes_accessed=8 << 20, transcendentals=total * total // 2
        ),
        name="attn_fwd",
    )(slot, qkv)


def attn_bwd_kernel(
    slot_ref,
    seq_ref,
    o32_ref,
    lse_ref,
    do_ref,
    cos_ref,
    sin_ref,
    out_ref,
    q_scr,
    k_scr,
    v_scr,
    do_scr,
    dot_scr,
    delta_scr,
    dq_scr,
    dk_scr,
    dv_scr,
    *,
    blocks,
    width,
):
    pieces = do_ref.shape[0]
    blk = pieces * width
    scale = HD**-0.5
    coef = LOG2E * scale
    half = HD // 2
    for s in range(blocks):
        at = pl.multiple_of(slot_ref[s] * width, width)
        for j in range(pieces):
            lo = s * blk + j * width
            piece = do_ref[j, :, pl.ds(at, width)]
            dot_scr[:, lo : lo + width] = piece
            do_scr[lo : lo + width, :] = piece.T
            delta_scr[:, lo : lo + width] = jnp.sum(
                piece.astype(F32) * o32_ref[:, lo : lo + width], axis=0, keepdims=True
            )
            q_scr[lo : lo + width, :] = seq_ref[:HD, lo : lo + width].T
            k_scr[lo : lo + width, :] = seq_ref[HD : 2 * HD, lo : lo + width].T
            v_scr[lo : lo + width, :] = seq_ref[2 * HD :, lo : lo + width].T
    dq_scr[...] = jnp.zeros_like(dq_scr)

    def turn_back(v, s):
        c = cos_ref[:, s * blk : (s + 1) * blk]
        n = sin_ref[:, s * blk : (s + 1) * blk]
        a, b = v[:half], v[half:]
        return jnp.concatenate([a * c + b * n, b * c - a * n], axis=0).astype(BF16)

    def put(v, s, row):
        at = pl.multiple_of(slot_ref[s] * width, width)
        for j in range(pieces):
            out_ref[j, row * HD : (row + 1) * HD, pl.ds(at, width)] = v[:, j * width : (j + 1) * width]

    for kb in range(blocks):
        lo = kb * blk
        k = k_scr[lo : lo + blk, :]
        v = v_scr[lo : lo + blk, :]
        k_t = seq_ref[HD : 2 * HD, lo : lo + blk]

        def tile(qb, masked):
            here = pl.ds(pl.multiple_of(qb * blk, blk), blk)
            p = jnp.exp2(mxu(k, seq_ref[:HD, here]) * coef - lse_ref[:, here])
            if masked:
                p = jnp.where(causal(blk), p, 0.0)
            dp = mxu(v, dot_scr[:, here])
            ds = (p * (dp - delta_scr[:, here])).astype(BF16)
            dq_scr[:, here] += mxu(k_t, ds)
            return mxu(ds, q_scr[here, :]), mxu(p.astype(BF16), do_scr[here, :])

        dk_scr[...], dv_scr[...] = tile(kb, True)
        if kb < blocks - 1:

            @pl.loop(kb + 1, blocks)
            def _(qb):
                dk, dv = tile(qb, False)
                dk_scr[...] += dk
                dv_scr[...] += dv

        put(turn_back(dq_scr[:, lo : lo + blk] * scale, kb), kb, 0)
        put(turn_back((dk_scr[...] * scale).T, kb), kb, 1)
        put(dv_scr[...].T.astype(BF16), kb, 2)


def attn_bwd(slot, seq, o32, lse, do, cos, sin, blocks):
    pieces, _, cols = do.shape
    total = pieces * cols
    blk = total // blocks
    return pl.pallas_call(
        functools.partial(attn_bwd_kernel, blocks=blocks, width=cols // blocks),
        out_shape=jax.ShapeDtypeStruct((pieces, 3 * HD, cols), BF16),
        in_specs=[pl.BlockSpec(memory_space=pltpu.SMEM)] + [VMEM] * 6,
        out_specs=VMEM,
        scratch_shapes=[pltpu.VMEM((total, HD), BF16)] * 4
        + [
            pltpu.VMEM((HD, total), BF16),
            pltpu.VMEM((1, total), F32),
            pltpu.VMEM((HD, total), F32),
            pltpu.VMEM((blk, HD), F32),
            pltpu.VMEM((blk, HD), F32),
        ],
        compiler_params=pltpu.CompilerParams(vmem_limit_bytes=48 << 20),
        cost_estimate=pl.CostEstimate(
            flops=20 * total * total * HD, bytes_accessed=8 << 20, transcendentals=total * total // 2
        ),
        name="attn_bwd",
    )(slot, seq, o32, lse, do, cos, sin)


FAR = ("ctx", "row")
NEAR = ("col", "core")


def swap(v, axis):
    return lax.ppermute(v, axis, [(0, 1), (1, 0)])


def shift(v, by):
    n = lax.axis_size("ctx")
    return lax.ppermute(v, "ctx", [(i, (i + by) % n) for i in range(n)])


def spread(v):
    parts = [v]
    for _ in range(lax.axis_size("ctx") - 1):
        parts.append(shift(parts[-1], 1))
    return jnp.concatenate(parts + [swap(p, "row") for p in parts], axis=0)


def collect(terms, tok):
    n = lax.axis_size("ctx")
    other = terms(1).astype(BF16).reshape(n, tok, -1)
    crossed = [swap(other[c], "row") for c in reversed(range(n))][::-1]
    own = terms(0).reshape(n, tok, -1)
    total = None
    for c in reversed(range(n)):
        part = own[c] + crossed[c].astype(F32)
        if total is not None:
            part = part + shift(total.astype(BF16), -1).astype(F32)
        total = part
    return total


def by_side(index, mine, theirs):
    return jnp.where(index == 0, mine, theirs), jnp.where(index == 0, theirs, mine)


def per_device_split(
    tokens,
    pair_index,
    gain_attn,
    w_query,
    w_key,
    w_value,
    w_out,
    gain_ffn,
    w_gate,
    w_up,
    w_down,
    cotangent,
):
    n_ctx = lax.axis_size("ctx")
    near = lax.axis_size("col") * lax.axis_size("core")
    far = 2 * n_ctx
    tok, width = tokens.shape
    own_in = w_query.shape[0]
    ctx_at, row_at, col_at, core_at = (lax.axis_index(a) for a in ("ctx", "row", "col", "core"))
    near_at = col_at * lax.axis_size("core") + core_at
    blk = near * tok
    rows_here = far * tok
    group = near * HD

    slots = jnp.arange(far, dtype=jnp.int32)
    slot_ctx = (ctx_at - slots % n_ctx + n_ctx) % n_ctx
    slot_row = row_at ^ (slots // n_ctx)
    pair = jnp.sum(
        jnp.where(
            slot_ctx[:, None] == jnp.arange(n_ctx, dtype=jnp.int32)[None, :], pair_index[None, :], 0
        ),
        axis=1,
    )
    slot_block = jnp.where(slot_row == 0, pair, far - 1 - pair)
    block_slot = jnp.sum(jnp.where(slot_block[None, :] == slots[:, None], slots[None, :], 0), axis=1)
    freq = jnp.exp(jnp.arange(HD // 2, dtype=F32) * (-2.0 * math.log(THETA) / HD))
    places = (
        slot_block[:, None] * blk + near_at * tok + jnp.arange(tok, dtype=jnp.int32)[None, :]
    ).reshape(rows_here)
    angle = freq[:, None] * places.astype(F32)[None, :]
    cosine, sine = jnp.cos(angle), jnp.sin(angle)
    seq_angle = freq[:, None] * jnp.arange(far * blk, dtype=jnp.int32).astype(F32)[None, :]
    seq_cos, seq_sin = jnp.cos(seq_angle), jnp.sin(seq_angle)

    gain_one = gain_attn.astype(F32)[:, None]
    send = jnp.concatenate(
        [
            (w.astype(F32) * gain_one).astype(BF16).reshape(own_in, far, group)
            for w in (w_query, w_key, w_value)
        ]
        + [jnp.broadcast_to(gain_ffn[:, None, None], (own_in, far, 128))],
        axis=2,
    ).transpose(1, 0, 2)
    x32 = tokens.astype(F32)
    scale_one = lax.rsqrt(jnp.mean(x32 * x32, axis=-1, keepdims=True) + EPS)
    rows_one = spread((x32 * scale_one).astype(BF16))
    mine = lax.all_to_all(send, FAR, split_axis=0, concat_axis=0, tiled=True)
    other = swap(mine, "col")
    mine_pair = by_side(core_at, mine, swap(mine, "core"))
    other_pair = by_side(core_at, other, swap(other, "core"))
    halves = [by_side(col_at, a, b) for a, b in zip(mine_pair, other_pair, strict=True)]
    w_ext = jnp.stack(
        [halves[0][0], halves[1][0], halves[0][1], halves[1][1]], axis=1
    ).reshape(width, 3 * group + 128)
    w_heads = w_ext[:, : 3 * group]
    gain_two = w_ext[:, 3 * group].astype(F32)[None, :]

    out_rows = lax.all_gather(w_out, NEAR, axis=0, tiled=True)
    gate_w, up_w, down_w = (
        lax.all_gather(w, NEAR, axis=0, tiled=True) for w in (w_gate, w_up, w_down)
    )

    half = HD // 2
    flat = jnp.einsum("de,td->et", w_heads, rows_one, preferred_element_type=F32)
    qkv = flat.reshape(3, near, 2, half, rows_here)
    first, second = qkv[:2, :, 0], qkv[:2, :, 1]
    turned = jnp.stack([first * cosine - second * sine, second * cosine + first * sine], axis=2)
    qkv = jnp.concatenate([turned, qkv[2:]], axis=0).astype(BF16)
    qkv = qkv.transpose(1, 0, 2, 3, 4).reshape(near, 3 * HD, rows_here)
    qkv_head = lax.all_to_all(qkv, NEAR, split_axis=0, concat_axis=0, tiled=True)
    attn_head, o32, lse, seq = attn_fwd(block_slot, qkv_head, far)
    attn = lax.all_to_all(attn_head, NEAR, split_axis=0, concat_axis=0, tiled=True)
    attn = attn.reshape(group, rows_here)
    rows_half = rows_here // 2

    def cut(v, r, axis):
        return lax.slice_in_dim(v, r * rows_half, (r + 1) * rows_half, axis=axis)

    mid = x32 + collect(
        lambda r: jnp.einsum("et,ed->td", cut(attn, r, 1), out_rows, preferred_element_type=F32), tok
    )
    scale_two = lax.rsqrt(jnp.mean(mid * mid, axis=-1, keepdims=True) + EPS)
    normed_two = (mid * scale_two * gain_two).astype(BF16)
    rows_two = spread(normed_two)
    dy_rows = spread(cotangent)
    gate = rows_by(rows_two, gate_w)
    up = rows_by(rows_two, up_w)
    silu_val, slope = silu_parts(gate)
    hidden = (silu_val * up).astype(BF16)
    dhidden = rows_by(dy_rows, down_w)
    dgate = (dhidden * up * slope).astype(BF16)
    dup = (dhidden * silu_val).astype(BF16)
    dnormed_two = collect(
        lambda r: jnp.dot(cut(dgate, r, 0), gate_w, preferred_element_type=F32)
        + jnp.dot(cut(dup, r, 0), up_w, preferred_element_type=F32),
        tok,
    )
    branch = collect(
        lambda r: jnp.dot(cut(hidden, r, 0), down_w, preferred_element_type=F32), tok
    )
    block_out = (mid + branch).astype(BF16)
    gate_grad, up_grad, down_grad = (
        lax.psum_scatter(
            outer_sum(left, right).astype(BF16), NEAR, scatter_dimension=0, tiled=True
        ).astype(F32)
        for left, right in ((dgate, rows_two), (dup, rows_two), (hidden, dy_rows))
    )
    dy = cotangent.astype(F32)
    gain_two_term = jnp.sum(dnormed_two * mid * scale_two, axis=0)
    scaled_two = gain_two * dnormed_two
    dmid = (
        dy
        + scale_two * scaled_two
        - mid * scale_two**3 * jnp.mean(scaled_two * mid, axis=-1, keepdims=True)
    )
    dmid_rows = spread(dmid.astype(BF16))
    dattn = jnp.einsum("ed,td->et", out_rows, dmid_rows, preferred_element_type=F32).astype(BF16)
    dattn_head = lax.all_to_all(
        dattn.reshape(near, HD, rows_here), NEAR, split_axis=0, concat_axis=0, tiled=True
    )
    out_grad = lax.psum_scatter(
        jnp.einsum("et,td->ed", attn, dmid_rows, preferred_element_type=F32).astype(BF16),
        NEAR,
        scatter_dimension=0,
        tiled=True,
    ).astype(F32)
    dqkv_head = attn_bwd(block_slot, seq, o32, lse, dattn_head, seq_cos, seq_sin, far)
    dqkv = lax.all_to_all(dqkv_head, NEAR, split_axis=0, concat_axis=0, tiled=True)
    dqkv = dqkv.reshape(near, 3, HD, rows_here).transpose(1, 0, 2, 3).reshape(3 * group, rows_here)
    scaled_one = collect(
        lambda r: jnp.einsum("et,de->td", cut(dqkv, r, 1), w_heads, preferred_element_type=F32), tok
    )
    input_grad = (
        dmid
        + scale_one * scaled_one
        - x32 * scale_one**3 * jnp.mean(scaled_one * x32, axis=-1, keepdims=True)
    )
    heads_grad = jnp.concatenate(
        [
            jnp.einsum("td,et->de", rows_one, dqkv, preferred_element_type=F32),
            jnp.broadcast_to(gain_two_term[:, None], (width, 128)),
        ],
        axis=1,
    ).astype(BF16)
    heads_grad = lax.psum_scatter(
        heads_grad.reshape(far, near * own_in, 3 * group + 128),
        NEAR,
        scatter_dimension=1,
        tiled=True,
    )
    back = lax.all_to_all(heads_grad, FAR, split_axis=0, concat_axis=0, tiled=True).astype(F32)
    raw = [
        back[:, :, i * group : (i + 1) * group].transpose(1, 0, 2).reshape(own_in, -1)
        for i in range(3)
    ]
    gain_attn_grad = sum(
        jnp.sum(w.astype(F32) * g, axis=1)
        for w, g in zip((w_query, w_key, w_value), raw, strict=True)
    )
    query_grad, key_grad, value_grad = (g * gain_one for g in raw)
    gain_ffn_grad = jnp.sum(back[:, :, 3 * group], axis=0)
    return (
        block_out,
        input_grad,
        gain_attn_grad,
        query_grad,
        key_grad,
        value_grad,
        out_grad,
        gain_ffn_grad,
        gate_grad,
        up_grad,
        down_grad,
    )


def solution(mesh):
    n_ctx, n_fsdp = mesh.shape["ctx"], mesh.shape["fsdp"]

    def step(*args):
        if n_fsdp == 8 and n_ctx * n_fsdp * HD == args[3].shape[1]:
            body, axes = per_device_split, FAR + NEAR
            over = Mesh(np.asarray(mesh.devices).reshape(n_ctx, 2, 2, 2), axes)
        else:
            body, axes, over = per_device_any, ("ctx", "fsdp"), mesh
        rows, line = P(axes, None), P(axes)
        return jax.shard_map(
            body,
            mesh=over,
            in_specs=(rows, P(), line, rows, rows, rows, rows, line, rows, rows, rows, rows),
            out_specs=(rows, rows, line, rows, rows, rows, rows, line, rows, rows, rows),
            check_vma=False,
        )(*args)

    return step
```

```python
import functools
import math

import jax
import jax.numpy as jnp
import numpy as np
from jax import lax
from jax.experimental import pallas as pl
from jax.experimental.pallas import tpu as pltpu
from jax.sharding import Mesh
from jax.sharding import PartitionSpec as P

HD = 64


EPS = 1e-05
THETA = 130000.0


def place_of(rows, pair_index, n_groups, blk):
    group = rows // (2 * blk)
    within = rows % (2 * blk)
    match = group[:, None] == jnp.arange(n_groups, dtype=jnp.int32)[None, :]
    pair = jnp.sum(jnp.where(match, pair_index[None, :], 0), axis=1)
    block = jnp.where(within < blk, pair, 2 * n_groups - 1 - pair)
    return block * blk + within % blk


def tables(places, head_dim):
    freq = jnp.exp(
        jnp.arange(head_dim // 2, dtype=jnp.float32) * (-2.0 * math.log(THETA) / head_dim)
    )
    angle = places.astype(jnp.float32)[:, None] * freq[None, :]
    return (jnp.cos(angle), jnp.sin(angle))


def rotate(flat, cosine, sine, head_dim):
    rows = flat.shape[0]
    split = flat.reshape(rows, -1, head_dim)
    half = head_dim // 2
    first = split[..., :half]
    second = split[..., half:]
    cos_b = cosine[:, None, :]
    sin_b = sine[:, None, :]
    out = jnp.concatenate([first * cos_b - second * sin_b, second * cos_b + first * sin_b], axis=-1)
    return out.reshape(rows, -1)


def silu_parts(gate):
    sig = jax.nn.sigmoid(gate)
    return (gate * sig, sig * (1.0 + gate * (1.0 - sig)))


def rows_by(left, right):
    return jnp.einsum("td,fd->tf", left, right, preferred_element_type=jnp.float32)


def outer_sum(left, right):
    return jnp.einsum("tf,td->fd", left, right, preferred_element_type=jnp.float32)


def per_device_any(
    tokens,
    pair_index,
    gain_attn,
    w_query,
    w_key,
    w_value,
    w_out,
    gain_ffn,
    w_gate,
    w_up,
    w_down,
    cotangent,
):
    f32 = jnp.float32
    bf16 = jnp.bfloat16
    n_ctx = lax.axis_size("ctx")
    n_fsdp = lax.axis_size("fsdp")
    tok = tokens.shape[0]
    group_rows = tok * n_fsdp
    blk = group_rows // 2
    total = group_rows * n_ctx
    ctx_index = lax.axis_index("ctx")
    fsdp_index = lax.axis_index("fsdp")
    local_rows = (ctx_index * n_fsdp + fsdp_index) * tok + jnp.arange(tok, dtype=jnp.int32)
    local_places = place_of(local_rows, pair_index, n_ctx, blk)
    group_places = place_of(
        ctx_index * group_rows + jnp.arange(group_rows, dtype=jnp.int32), pair_index, n_ctx, blk
    )
    key_places = place_of(jnp.arange(total, dtype=jnp.int32), pair_index, n_ctx, blk)
    group_cos, group_sin = tables(group_places, HD)
    query_full, key_full, value_full, out_full, gain_one, gain_two = (
        lax.all_gather(w_query, ("ctx", "fsdp"), axis=0, tiled=True),
        lax.all_gather(w_key, ("ctx", "fsdp"), axis=0, tiled=True),
        lax.all_gather(w_value, ("ctx", "fsdp"), axis=0, tiled=True),
        lax.all_gather(w_out, ("ctx", "fsdp"), axis=0, tiled=True),
        lax.all_gather(gain_attn, ("ctx", "fsdp"), axis=0, tiled=True),
        lax.all_gather(gain_ffn, ("ctx", "fsdp"), axis=0, tiled=True),
    )
    gain_one = gain_one.astype(f32)
    gain_two = gain_two.astype(f32)
    x32 = tokens.astype(f32)
    scale_one = lax.rsqrt(jnp.mean(x32 * x32, axis=-1, keepdims=True) + EPS)
    normed_one = (x32 * scale_one * gain_one).astype(bf16)
    cosine, sine = tables(local_places, HD)
    query = rotate(
        jnp.dot(normed_one, query_full, preferred_element_type=f32), cosine, sine, HD
    ).astype(bf16)
    key = rotate(
        jnp.dot(normed_one, key_full, preferred_element_type=f32), cosine, sine, HD
    ).astype(bf16)
    value = jnp.dot(normed_one, value_full, preferred_element_type=f32).astype(bf16)
    query_heads, key_heads, value_heads = (
        lax.all_to_all(query, "fsdp", split_axis=1, concat_axis=0, tiled=True),
        lax.all_to_all(key, "fsdp", split_axis=1, concat_axis=0, tiled=True),
        lax.all_to_all(value, "fsdp", split_axis=1, concat_axis=0, tiled=True),
    )
    key_all, value_all = (
        lax.all_gather(key_heads, "ctx", axis=0, tiled=True),
        lax.all_gather(value_heads, "ctx", axis=0, tiled=True),
    )
    local_width = query_heads.shape[1]
    heads_here = local_width // HD
    scale = HD ** (-0.5)
    query_parts = query_heads.reshape(2, blk, heads_here, HD)
    query_place_tiles = group_places.reshape(2, blk)
    key_tiles = key_all.reshape(2 * n_ctx, blk, heads_here, HD)
    value_tiles = value_all.reshape(2 * n_ctx, blk, heads_here, HD)
    key_place_tiles = key_places.reshape(2 * n_ctx, blk)

    def tile_scores(slot, keys, k_place):
        raw = (
            jnp.einsum("qhd,khd->hqk", query_parts[slot], keys, preferred_element_type=f32) * scale
        )
        keep = k_place[None, None, :] <= query_place_tiles[slot][None, :, None]
        return jnp.where(keep, raw, -1e30)

    def is_live(slot, k_place):
        return jnp.min(k_place) <= jnp.max(query_place_tiles[slot])

    def first_pass(carry, tile):
        keys, k_place = tile
        highs, totals = carry
        new_highs = []
        new_totals = []
        for slot in range(2):

            def first_update(high, summed):
                masked = tile_scores(slot, keys, k_place)
                fresh = jnp.maximum(high, jnp.max(masked, axis=-1))
                summed = summed * jnp.exp(high - fresh) + jnp.sum(
                    jnp.exp(masked - fresh[..., None]), axis=-1
                )
                return (fresh, summed)

            def first_leave(high, summed):
                return (high, summed)

            high, summed = lax.cond(
                is_live(slot, k_place), first_update, first_leave, highs[slot], totals[slot]
            )
            new_highs.append(high)
            new_totals.append(summed)
        return ((jnp.stack(new_highs), jnp.stack(new_totals)), None)

    start_high = jnp.full((2, heads_here, blk), -1e30, f32)
    start_total = jnp.zeros((2, heads_here, blk), f32)
    (highs, totals), unused = lax.scan(
        first_pass, (start_high, start_total), (key_tiles, key_place_tiles)
    )
    log_total = highs + jnp.log(totals)

    def second_pass(carry, tile):
        keys, values, k_place = tile
        outs = []
        for slot in range(2):

            def second_update(acc):
                masked = tile_scores(slot, keys, k_place)
                prob_low = jnp.exp(masked - log_total[slot][..., None]).astype(bf16)
                return acc + jnp.einsum(
                    "hqk,khd->qhd", prob_low, values, preferred_element_type=f32
                )

            def second_leave(acc):
                return acc

            outs.append(lax.cond(is_live(slot, k_place), second_update, second_leave, carry[slot]))
        return (jnp.stack(outs), None)

    acc_start = jnp.zeros((2, blk, heads_here, HD), f32)
    attn_acc, unused = lax.scan(second_pass, acc_start, (key_tiles, value_tiles, key_place_tiles))
    attn32 = attn_acc.reshape(group_rows, local_width)
    attn_tokens = lax.all_to_all(
        attn32.astype(bf16), "fsdp", split_axis=0, concat_axis=1, tiled=True
    )
    mid = x32 + jnp.dot(attn_tokens, out_full, preferred_element_type=f32)
    scale_two = lax.rsqrt(jnp.mean(mid * mid, axis=-1, keepdims=True) + EPS)
    normed_two = (mid * scale_two * gain_two).astype(bf16)
    dy = cotangent.astype(f32)
    dy_low = dy.astype(bf16)
    gate_local, up_local, down_local = (
        lax.all_gather(w_gate, "ctx", axis=0, tiled=True),
        lax.all_gather(w_up, "ctx", axis=0, tiled=True),
        lax.all_gather(w_down, "ctx", axis=0, tiled=True),
    )
    rows_all = lax.all_gather(normed_two, "fsdp", axis=0, tiled=True)
    gate_all = rows_by(rows_all, gate_local)
    up_all = rows_by(rows_all, up_local)
    silu_all, unused_slope = silu_parts(gate_all)
    hidden_all = (silu_all * up_all).astype(bf16)
    branch = lax.psum_scatter(
        jnp.dot(hidden_all, down_local, preferred_element_type=f32).astype(jnp.bfloat16),
        "fsdp",
        scatter_dimension=0,
        tiled=True,
    ).astype(jnp.float32)
    block_out = (mid + branch).astype(bf16)
    grad_rows_all = lax.all_gather(dy_low, "fsdp", axis=0, tiled=True)
    dhidden = rows_by(grad_rows_all, down_local)
    silu_val, slope = silu_parts(gate_all)
    dgate = (dhidden * up_all * slope).astype(bf16)
    dup = (dhidden * silu_val).astype(bf16)
    gate_term = outer_sum(dgate, rows_all)
    up_term = outer_sum(dup, rows_all)
    down_term = outer_sum(hidden_all, grad_rows_all)
    gate_grad, up_grad, down_grad = (
        lax.psum_scatter(
            gate_term.astype(jnp.bfloat16), "ctx", scatter_dimension=0, tiled=True
        ).astype(jnp.float32),
        lax.psum_scatter(
            up_term.astype(jnp.bfloat16), "ctx", scatter_dimension=0, tiled=True
        ).astype(jnp.float32),
        lax.psum_scatter(
            down_term.astype(jnp.bfloat16), "ctx", scatter_dimension=0, tiled=True
        ).astype(jnp.float32),
    )
    dnormed_two = lax.psum_scatter(
        (
            jnp.dot(dgate, gate_local, preferred_element_type=f32)
            + jnp.dot(dup, up_local, preferred_element_type=f32)
        ).astype(jnp.bfloat16),
        "fsdp",
        scatter_dimension=0,
        tiled=True,
    ).astype(jnp.float32)
    gain_two_term = jnp.sum(dnormed_two * mid * scale_two, axis=0)
    scaled_two = gain_two * dnormed_two
    dmid = (
        dy
        + scale_two * scaled_two
        - mid * scale_two**3 * jnp.mean(scaled_two * mid, axis=-1, keepdims=True)
    )
    dmid_low = dmid.astype(bf16)
    out_term = jnp.einsum("td,te->de", attn_tokens, dmid_low, preferred_element_type=f32)
    dattn = jnp.einsum("te,de->td", dmid_low, out_full, preferred_element_type=f32).astype(bf16)
    dattn_heads = lax.all_to_all(dattn, "fsdp", split_axis=1, concat_axis=0, tiled=True)
    delta = jnp.sum((dattn_heads.astype(f32) * attn32).reshape(group_rows, heads_here, HD), axis=-1)
    delta_tiles = delta.reshape(2, blk, heads_here).transpose(0, 2, 1)
    grad_parts = dattn_heads.reshape(2, blk, heads_here, HD)

    def back_pass(carry, tile):
        keys, values, k_place = tile
        key_acc = jnp.zeros((blk, heads_here, HD), f32)
        value_acc = jnp.zeros((blk, heads_here, HD), f32)
        new_query = []
        for slot in range(2):

            def back_update(q_acc, k_acc, v_acc):
                masked = tile_scores(slot, keys, k_place)
                prob = jnp.exp(masked - log_total[slot][..., None])
                prob_low = prob.astype(bf16)
                dprob = jnp.einsum(
                    "qhd,khd->hqk", grad_parts[slot], values, preferred_element_type=f32
                )
                dscore = (prob * (dprob - delta_tiles[slot][..., None])).astype(bf16)
                q_acc = (
                    q_acc
                    + jnp.einsum("hqk,khd->qhd", dscore, keys, preferred_element_type=f32) * scale
                )
                k_acc = (
                    k_acc
                    + jnp.einsum(
                        "hqk,qhd->khd", dscore, query_parts[slot], preferred_element_type=f32
                    )
                    * scale
                )
                v_acc = v_acc + jnp.einsum(
                    "hqk,qhd->khd", prob_low, grad_parts[slot], preferred_element_type=f32
                )
                return (q_acc, k_acc, v_acc)

            def back_leave(q_acc, k_acc, v_acc):
                return (q_acc, k_acc, v_acc)

            q_acc, key_acc, value_acc = lax.cond(
                is_live(slot, k_place), back_update, back_leave, carry[slot], key_acc, value_acc
            )
            new_query.append(q_acc)
        return (jnp.stack(new_query), (key_acc, value_acc))

    dquery_start = jnp.zeros((2, blk, heads_here, HD), f32)
    dquery_acc, (dkey_tiles, dvalue_tiles) = lax.scan(
        back_pass, dquery_start, (key_tiles, value_tiles, key_place_tiles)
    )
    dkey_all = dkey_tiles.reshape(total, local_width)
    dvalue_all = dvalue_tiles.reshape(total, local_width)
    dkey_own, dvalue_own = (
        lax.psum_scatter(
            dkey_all.astype(jnp.bfloat16), "ctx", scatter_dimension=0, tiled=True
        ).astype(jnp.float32),
        lax.psum_scatter(
            dvalue_all.astype(jnp.bfloat16), "ctx", scatter_dimension=0, tiled=True
        ).astype(jnp.float32),
    )
    dquery_low = rotate(
        dquery_acc.reshape(group_rows, local_width), group_cos, -group_sin, HD
    ).astype(bf16)
    dkey_low = rotate(dkey_own, group_cos, -group_sin, HD).astype(bf16)
    dvalue_low = dvalue_own.astype(bf16)
    dquery_tok, dkey_tok, dvalue_tok = (
        lax.all_to_all(dquery_low, "fsdp", split_axis=0, concat_axis=1, tiled=True),
        lax.all_to_all(dkey_low, "fsdp", split_axis=0, concat_axis=1, tiled=True),
        lax.all_to_all(dvalue_low, "fsdp", split_axis=0, concat_axis=1, tiled=True),
    )
    dnormed_one = (
        jnp.einsum("te,de->td", dquery_tok, query_full, preferred_element_type=f32)
        + jnp.einsum("te,de->td", dkey_tok, key_full, preferred_element_type=f32)
        + jnp.einsum("te,de->td", dvalue_tok, value_full, preferred_element_type=f32)
    )
    query_term = jnp.einsum("td,te->de", normed_one, dquery_tok, preferred_element_type=f32)
    key_term = jnp.einsum("td,te->de", normed_one, dkey_tok, preferred_element_type=f32)
    value_term = jnp.einsum("td,te->de", normed_one, dvalue_tok, preferred_element_type=f32)
    gain_one_term = jnp.sum(dnormed_one * x32 * scale_one, axis=0)
    scaled_one = gain_one * dnormed_one
    input_grad = (
        dmid
        + scale_one * scaled_one
        - x32 * scale_one**3 * jnp.mean(scaled_one * x32, axis=-1, keepdims=True)
    )
    query_grad, key_grad, value_grad, out_grad, gain_attn_grad, gain_ffn_grad = (
        lax.psum_scatter(query_term, ("ctx", "fsdp"), scatter_dimension=0, tiled=True),
        lax.psum_scatter(key_term, ("ctx", "fsdp"), scatter_dimension=0, tiled=True),
        lax.psum_scatter(value_term, ("ctx", "fsdp"), scatter_dimension=0, tiled=True),
        lax.psum_scatter(out_term, ("ctx", "fsdp"), scatter_dimension=0, tiled=True),
        lax.psum_scatter(gain_one_term, ("ctx", "fsdp"), scatter_dimension=0, tiled=True),
        lax.psum_scatter(gain_two_term, ("ctx", "fsdp"), scatter_dimension=0, tiled=True),
    )
    return (
        block_out,
        input_grad,
        gain_attn_grad,
        query_grad,
        key_grad,
        value_grad,
        out_grad,
        gain_ffn_grad,
        gate_grad,
        up_grad,
        down_grad,
    )


BF16 = jnp.bfloat16
F32 = jnp.float32
LOG2E = math.log2(math.e)
VMEM = pl.BlockSpec(memory_space=pltpu.VMEM)


def mxu(a, b):
    return jnp.dot(a, b, preferred_element_type=F32)


def causal(blk):
    row = lax.broadcasted_iota(jnp.int32, (blk, blk), 0)
    col = lax.broadcasted_iota(jnp.int32, (blk, blk), 1)
    return row <= col


def attn_fwd_kernel(
    slot_ref, qkv_ref, out_ref, o32_ref, lse_ref, seq_ref, k_scr, m_scr, l_scr, acc_scr, *, blocks, width
):
    pieces = qkv_ref.shape[0]
    blk = pieces * width
    coef = LOG2E * HD**-0.5
    for s in range(blocks):
        at = pl.multiple_of(slot_ref[s] * width, width)
        for j in range(pieces):
            lo = s * blk + j * width
            piece = qkv_ref[j, :, pl.ds(at, width)]
            seq_ref[:, lo : lo + width] = piece
            k_scr[lo : lo + width, :] = piece[HD : 2 * HD].T

    def tile(kb, q_t, masked):
        at = pl.multiple_of(kb * blk, blk)
        score = mxu(k_scr[pl.ds(at, blk), :], q_t) * coef
        if masked:
            score = jnp.where(causal(blk), score, -1e30)
        old = m_scr[...]
        new = jnp.maximum(old, jnp.max(score, axis=0, keepdims=True))
        p = jnp.exp2(score - new)
        fade = jnp.exp2(old - new)
        m_scr[...] = new
        l_scr[...] = l_scr[...] * fade + jnp.sum(p, axis=0, keepdims=True)
        acc_scr[...] = acc_scr[...] * fade + mxu(seq_ref[2 * HD :, pl.ds(at, blk)], p.astype(BF16))

    for qb in range(blocks):
        lo = qb * blk
        q_t = seq_ref[:HD, lo : lo + blk]
        m_scr[...] = jnp.full_like(m_scr, -1e30)
        l_scr[...] = jnp.zeros_like(l_scr)
        acc_scr[...] = jnp.zeros_like(acc_scr)
        tile(qb, q_t, True)
        if qb > 0:

            @pl.loop(0, qb)
            def _(kb):
                tile(kb, q_t, False)

        o = acc_scr[...] / l_scr[...]
        o32_ref[:, lo : lo + blk] = o
        lse_ref[:, lo : lo + blk] = m_scr[...] + jnp.log2(l_scr[...])
        at = pl.multiple_of(slot_ref[qb] * width, width)
        low = o.astype(BF16)
        for j in range(pieces):
            out_ref[j, :, pl.ds(at, width)] = low[:, j * width : (j + 1) * width]


def attn_fwd(slot, qkv, blocks):
    pieces, _, cols = qkv.shape
    total = pieces * cols
    blk = total // blocks
    return pl.pallas_call(
        functools.partial(attn_fwd_kernel, blocks=blocks, width=cols // blocks),
        out_shape=(
            jax.ShapeDtypeStruct((pieces, HD, cols), BF16),
            jax.ShapeDtypeStruct((HD, total), F32),
            jax.ShapeDtypeStruct((1, total), F32),
            jax.ShapeDtypeStruct((3 * HD, total), BF16),
        ),
        in_specs=[pl.BlockSpec(memory_space=pltpu.SMEM), VMEM],
        out_specs=(VMEM,) * 4,
        scratch_shapes=[
            pltpu.VMEM((total, HD), BF16),
            pltpu.VMEM((1, blk), F32),
            pltpu.VMEM((1, blk), F32),
            pltpu.VMEM((HD, blk), F32),
        ],
        compiler_params=pltpu.CompilerParams(vmem_limit_bytes=40 << 20),
        cost_estimate=pl.CostEstimate(
            flops=8 * total * total * HD, bytes_accessed=8 << 20, transcendentals=total * total // 2
        ),
        name="attn_fwd",
    )(slot, qkv)


def attn_bwd_kernel(
    slot_ref,
    seq_ref,
    o32_ref,
    lse_ref,
    do_ref,
    cos_ref,
    sin_ref,
    out_ref,
    q_scr,
    k_scr,
    v_scr,
    do_scr,
    dot_scr,
    delta_scr,
    dq_scr,
    dk_scr,
    dv_scr,
    *,
    blocks,
    width,
):
    pieces = do_ref.shape[0]
    blk = pieces * width
    scale = HD**-0.5
    coef = LOG2E * scale
    half = HD // 2
    for s in range(blocks):
        at = pl.multiple_of(slot_ref[s] * width, width)
        for j in range(pieces):
            lo = s * blk + j * width
            piece = do_ref[j, :, pl.ds(at, width)]
            dot_scr[:, lo : lo + width] = piece
            do_scr[lo : lo + width, :] = piece.T
            delta_scr[:, lo : lo + width] = jnp.sum(
                piece.astype(F32) * o32_ref[:, lo : lo + width], axis=0, keepdims=True
            )
            q_scr[lo : lo + width, :] = seq_ref[:HD, lo : lo + width].T
            k_scr[lo : lo + width, :] = seq_ref[HD : 2 * HD, lo : lo + width].T
            v_scr[lo : lo + width, :] = seq_ref[2 * HD :, lo : lo + width].T
    dq_scr[...] = jnp.zeros_like(dq_scr)

    def turn_back(v, s):
        c = cos_ref[:, s * blk : (s + 1) * blk]
        n = sin_ref[:, s * blk : (s + 1) * blk]
        a, b = v[:half], v[half:]
        return jnp.concatenate([a * c + b * n, b * c - a * n], axis=0).astype(BF16)

    def put(v, s, row):
        at = pl.multiple_of(slot_ref[s] * width, width)
        for j in range(pieces):
            out_ref[j, row * HD : (row + 1) * HD, pl.ds(at, width)] = v[:, j * width : (j + 1) * width]

    for kb in range(blocks):
        lo = kb * blk
        k = k_scr[lo : lo + blk, :]
        v = v_scr[lo : lo + blk, :]
        k_t = seq_ref[HD : 2 * HD, lo : lo + blk]

        def tile(qb, masked):
            here = pl.ds(pl.multiple_of(qb * blk, blk), blk)
            p = jnp.exp2(mxu(k, seq_ref[:HD, here]) * coef - lse_ref[:, here])
            if masked:
                p = jnp.where(causal(blk), p, 0.0)
            dp = mxu(v, dot_scr[:, here])
            ds = (p * (dp - delta_scr[:, here])).astype(BF16)
            dq_scr[:, here] += mxu(k_t, ds)
            return mxu(ds, q_scr[here, :]), mxu(p.astype(BF16), do_scr[here, :])

        dk_scr[...], dv_scr[...] = tile(kb, True)
        if kb < blocks - 1:

            @pl.loop(kb + 1, blocks)
            def _(qb):
                dk, dv = tile(qb, False)
                dk_scr[...] += dk
                dv_scr[...] += dv

        put(turn_back(dq_scr[:, lo : lo + blk] * scale, kb), kb, 0)
        put(turn_back((dk_scr[...] * scale).T, kb), kb, 1)
        put(dv_scr[...].T.astype(BF16), kb, 2)


def attn_bwd(slot, seq, o32, lse, do, cos, sin, blocks):
    pieces, _, cols = do.shape
    total = pieces * cols
    blk = total // blocks
    return pl.pallas_call(
        functools.partial(attn_bwd_kernel, blocks=blocks, width=cols // blocks),
        out_shape=jax.ShapeDtypeStruct((pieces, 3 * HD, cols), BF16),
        in_specs=[pl.BlockSpec(memory_space=pltpu.SMEM)] + [VMEM] * 6,
        out_specs=VMEM,
        scratch_shapes=[pltpu.VMEM((total, HD), BF16)] * 4
        + [
            pltpu.VMEM((HD, total), BF16),
            pltpu.VMEM((1, total), F32),
            pltpu.VMEM((HD, total), F32),
            pltpu.VMEM((blk, HD), F32),
            pltpu.VMEM((blk, HD), F32),
        ],
        compiler_params=pltpu.CompilerParams(vmem_limit_bytes=48 << 20),
        cost_estimate=pl.CostEstimate(
            flops=20 * total * total * HD, bytes_accessed=8 << 20, transcendentals=total * total // 2
        ),
        name="attn_bwd",
    )(slot, seq, o32, lse, do, cos, sin)


FAR = ("ctx", "row")
NEAR = ("col", "core")


def swap(v, axis):
    return lax.ppermute(v, axis, [(0, 1), (1, 0)])


def shift(v, by):
    n = lax.axis_size("ctx")
    return lax.ppermute(v, "ctx", [(i, (i + by) % n) for i in range(n)])


def spread(v, *beside):
    own, other, held = [v], [], None
    for i in range(lax.axis_size("ctx") - 1):
        more = beside[i](held) if i < len(beside) else held
        ahead, across, held = lax.optimization_barrier(
            (shift(own[-1], 1), swap(own[-1], "row"), more)
        )
        own.append(ahead)
        other.append(across)
    rows = jnp.concatenate(own + other + [swap(own[-1], "row")], axis=0)
    return (rows, held) if beside else rows


def collect(other, own, tok):
    n = lax.axis_size("ctx")
    other = other.astype(BF16).reshape(n, tok, -1)
    own = own.astype(F32).reshape(n, tok, -1)
    total = own[n - 1] + swap(other[n - 1], "row").astype(F32)
    for c in reversed(range(n - 1)):
        ahead, across = lax.optimization_barrier(
            (shift(total.astype(BF16), -1), swap(other[c], "row"))
        )
        total = own[c] + across.astype(F32) + ahead.astype(F32)
    return total


def after(v, first):
    return lax.optimization_barrier((v, first))[0]


def by_side(index, mine, theirs):
    return jnp.where(index == 0, mine, theirs), jnp.where(index == 0, theirs, mine)


def per_device_split(
    tokens,
    pair_index,
    gain_attn,
    w_query,
    w_key,
    w_value,
    w_out,
    gain_ffn,
    w_gate,
    w_up,
    w_down,
    cotangent,
):
    n_ctx = lax.axis_size("ctx")
    near = lax.axis_size("col") * lax.axis_size("core")
    far = 2 * n_ctx
    tok, width = tokens.shape
    own_in = w_query.shape[0]
    ctx_at, row_at, col_at, core_at = (lax.axis_index(a) for a in ("ctx", "row", "col", "core"))
    near_at = col_at * lax.axis_size("core") + core_at
    blk = near * tok
    rows_here = far * tok
    group = near * HD

    slots = jnp.arange(far, dtype=jnp.int32)
    slot_ctx = (ctx_at - slots % n_ctx + n_ctx) % n_ctx
    slot_row = row_at ^ (slots // n_ctx)
    pair = jnp.sum(
        jnp.where(
            slot_ctx[:, None] == jnp.arange(n_ctx, dtype=jnp.int32)[None, :], pair_index[None, :], 0
        ),
        axis=1,
    )
    slot_block = jnp.where(slot_row == 0, pair, far - 1 - pair)
    block_slot = jnp.sum(jnp.where(slot_block[None, :] == slots[:, None], slots[None, :], 0), axis=1)
    freq = jnp.exp(jnp.arange(HD // 2, dtype=F32) * (-2.0 * math.log(THETA) / HD))
    places = (
        slot_block[:, None] * blk + near_at * tok + jnp.arange(tok, dtype=jnp.int32)[None, :]
    ).reshape(rows_here)
    angle = freq[:, None] * places.astype(F32)[None, :]
    cosine, sine = jnp.cos(angle), jnp.sin(angle)
    seq_angle = freq[:, None] * jnp.arange(far * blk, dtype=jnp.int32).astype(F32)[None, :]
    seq_cos, seq_sin = jnp.cos(seq_angle), jnp.sin(seq_angle)

    gain_one = gain_attn.astype(F32)[:, None]
    send = jnp.concatenate(
        [
            (w.astype(F32) * gain_one).astype(BF16).reshape(own_in, far, group)
            for w in (w_query, w_key, w_value)
        ]
        + [jnp.broadcast_to(gain_ffn[:, None, None], (own_in, far, 128))],
        axis=2,
    ).transpose(1, 0, 2)
    x32 = tokens.astype(F32)
    scale_one = lax.rsqrt(jnp.mean(x32 * x32, axis=-1, keepdims=True) + EPS)
    rows_one, (mine, other) = spread(
        (x32 * scale_one).astype(BF16),
        lambda _: lax.all_to_all(send, FAR, split_axis=0, concat_axis=0, tiled=True),
        lambda mine: (mine, swap(mine, "col")),
    )
    mine_pair = by_side(core_at, mine, swap(mine, "core"))
    other_pair = by_side(core_at, other, swap(other, "core"))
    halves = [by_side(col_at, a, b) for a, b in zip(mine_pair, other_pair, strict=True)]
    w_ext = jnp.stack(
        [halves[0][0], halves[1][0], halves[0][1], halves[1][1]], axis=1
    ).reshape(width, 3 * group + 128)
    w_heads = w_ext[:, : 3 * group]
    gain_two = w_ext[:, 3 * group].astype(F32)[None, :]

    dy_all = lax.all_gather(after(cotangent, rows_one), FAR, axis=0)
    dy_rows = jnp.concatenate(
        [
            lax.dynamic_index_in_dim(
                dy_all.reshape(far, tok, width), 2 * slot_ctx[i] + slot_row[i], keepdims=False
            )
            for i in range(far)
        ],
        axis=0,
    )
    out_rows = lax.all_gather(w_out, NEAR, axis=0, tiled=True)
    gate_w, up_w, down_w = (
        lax.all_gather(w, NEAR, axis=0, tiled=True) for w in (w_gate, w_up, w_down)
    )

    half = HD // 2
    flat = jnp.einsum("de,td->et", w_heads, rows_one, preferred_element_type=F32)
    qkv = flat.reshape(3, near, 2, half, rows_here)
    first, second = qkv[:2, :, 0], qkv[:2, :, 1]
    turned = jnp.stack([first * cosine - second * sine, second * cosine + first * sine], axis=2)
    qkv = jnp.concatenate([turned, qkv[2:]], axis=0).astype(BF16)
    qkv = qkv.transpose(1, 0, 2, 3, 4).reshape(near, 3 * HD, rows_here)
    qkv_head = lax.all_to_all(qkv, NEAR, split_axis=0, concat_axis=0, tiled=True)
    attn_head, o32, lse, seq = attn_fwd(block_slot, qkv_head, far)
    attn = lax.all_to_all(attn_head, NEAR, split_axis=0, concat_axis=0, tiled=True)
    attn = attn.reshape(group, rows_here)
    rows_half = rows_here // 2

    def cut(v, r, axis):
        return lax.slice_in_dim(v, r * rows_half, (r + 1) * rows_half, axis=axis)

    def halves_of(term, axis, *parts):
        return [term(*(cut(p, r, axis) for p in parts)) for r in (1, 0)]

    def out_term(rows):
        return jnp.einsum("et,ed->td", rows, out_rows, preferred_element_type=F32)

    mid = x32 + collect(*halves_of(out_term, 1, attn), tok)
    scale_two = lax.rsqrt(jnp.mean(mid * mid, axis=-1, keepdims=True) + EPS)
    normed_two = (mid * scale_two * gain_two).astype(BF16)
    normed_two, dy_rows = lax.optimization_barrier((normed_two, dy_rows))
    rows_two = spread(normed_two)
    gate = rows_by(rows_two, gate_w)
    up = rows_by(rows_two, up_w)
    silu_val, slope = silu_parts(gate)
    hidden = (silu_val * up).astype(BF16)
    dhidden = rows_by(dy_rows, down_w)
    dgate = (dhidden * up * slope).astype(BF16)
    dup = (dhidden * silu_val).astype(BF16)

    def rows_term(dgate, dup):
        return jnp.dot(dgate, gate_w, preferred_element_type=F32) + jnp.dot(
            dup, up_w, preferred_element_type=F32
        )

    def branch_term(hidden):
        return jnp.dot(hidden, down_w, preferred_element_type=F32).astype(BF16)

    dn_other, dn_own = halves_of(rows_term, 0, dgate, dup)
    dn_other, dgate, dup, hidden = lax.optimization_barrier((dn_other, dgate, dup, hidden))
    dnormed_two = collect(dn_other, dn_own, tok)
    branch_terms = halves_of(branch_term, 0, hidden)
    dnormed_two, branch_terms = lax.optimization_barrier((dnormed_two, branch_terms))
    gate_grad, up_grad, down_grad = (
        lax.psum_scatter(
            outer_sum(left, right).astype(BF16), NEAR, scatter_dimension=0, tiled=True
        ).astype(F32)
        for left, right in ((dgate, rows_two), (dup, rows_two), (hidden, dy_rows))
    )
    dy = cotangent.astype(F32)
    gain_two_term = jnp.sum(dnormed_two * mid * scale_two, axis=0)
    scaled_two = gain_two * dnormed_two
    dmid = (
        dy
        + scale_two * scaled_two
        - mid * scale_two**3 * jnp.mean(scaled_two * mid, axis=-1, keepdims=True)
    )
    dmid_rows, gate_grad = lax.optimization_barrier((spread(dmid.astype(BF16)), gate_grad))
    branch = collect(*after(branch_terms, dmid_rows), tok)
    block_out = (mid + branch).astype(BF16)
    dattn = jnp.einsum("ed,td->et", out_rows, dmid_rows, preferred_element_type=F32).astype(BF16)
    dattn_head = lax.all_to_all(
        dattn.reshape(near, HD, rows_here), NEAR, split_axis=0, concat_axis=0, tiled=True
    )
    dattn_head, up_grad = lax.optimization_barrier((dattn_head, up_grad))
    dqkv_head = attn_bwd(block_slot, seq, o32, lse, dattn_head, seq_cos, seq_sin, far)
    dqkv_head, down_grad = lax.optimization_barrier((dqkv_head, down_grad))
    dqkv = lax.all_to_all(dqkv_head, NEAR, split_axis=0, concat_axis=0, tiled=True)
    dqkv = dqkv.reshape(near, 3, HD, rows_here).transpose(1, 0, 2, 3).reshape(3 * group, rows_here)
    dqkv, block_out = lax.optimization_barrier((dqkv, block_out))

    def heads_term(rows):
        return jnp.einsum("et,de->td", rows, w_heads, preferred_element_type=F32)

    dx_other, dx_own = halves_of(heads_term, 1, dqkv)
    dx_other, dqkv, attn, dmid_rows = lax.optimization_barrier((dx_other, dqkv, attn, dmid_rows))
    scaled_one = collect(dx_other, dx_own, tok)
    out_grad = lax.psum_scatter(
        jnp.einsum("et,td->ed", attn, dmid_rows, preferred_element_type=F32).astype(BF16),
        NEAR,
        scatter_dimension=0,
        tiled=True,
    ).astype(F32)
    input_grad = (
        dmid
        + scale_one * scaled_one
        - x32 * scale_one**3 * jnp.mean(scaled_one * x32, axis=-1, keepdims=True)
    )
    heads_grad = jnp.concatenate(
        [
            jnp.einsum("td,et->de", rows_one, dqkv, preferred_element_type=F32),
            jnp.broadcast_to(gain_two_term[:, None], (width, 128)),
        ],
        axis=1,
    ).astype(BF16)
    heads_grad = lax.psum_scatter(
        heads_grad.reshape(far, near * own_in, 3 * group + 128),
        NEAR,
        scatter_dimension=1,
        tiled=True,
    )
    back = lax.all_to_all(heads_grad, FAR, split_axis=0, concat_axis=0, tiled=True).astype(F32)
    raw = [
        back[:, :, i * group : (i + 1) * group].transpose(1, 0, 2).reshape(own_in, -1)
        for i in range(3)
    ]
    gain_attn_grad = sum(
        jnp.sum(w.astype(F32) * g, axis=1)
        for w, g in zip((w_query, w_key, w_value), raw, strict=True)
    )
    query_grad, key_grad, value_grad = (g * gain_one for g in raw)
    gain_ffn_grad = jnp.sum(back[:, :, 3 * group], axis=0)
    return (
        block_out,
        input_grad,
        gain_attn_grad,
        query_grad,
        key_grad,
        value_grad,
        out_grad,
        gain_ffn_grad,
        gate_grad,
        up_grad,
        down_grad,
    )


def solution(mesh):
    n_ctx, n_fsdp = mesh.shape["ctx"], mesh.shape["fsdp"]

    def step(*args):
        if n_fsdp == 8 and n_ctx * n_fsdp * HD == args[3].shape[1]:
            body, axes = per_device_split, FAR + NEAR
            over = Mesh(np.asarray(mesh.devices).reshape(n_ctx, 2, 2, 2), axes)
        else:
            body, axes, over = per_device_any, ("ctx", "fsdp"), mesh
        rows, line = P(axes, None), P(axes)
        return jax.shard_map(
            body,
            mesh=over,
            in_specs=(rows, P(), line, rows, rows, rows, rows, line, rows, rows, rows, rows),
            out_specs=(rows, rows, line, rows, rows, rows, rows, line, rows, rows, rows),
            check_vma=False,
        )(*args)

    return step
```

```python
import functools
import math

import jax
import jax.numpy as jnp
import numpy as np
from jax import lax
from jax.experimental import pallas as pl
from jax.experimental.pallas import tpu as pltpu
from jax.sharding import Mesh
from jax.sharding import PartitionSpec as P

HD = 64


EPS = 1e-05
THETA = 130000.0


def place_of(rows, pair_index, n_groups, blk):
    group = rows // (2 * blk)
    within = rows % (2 * blk)
    match = group[:, None] == jnp.arange(n_groups, dtype=jnp.int32)[None, :]
    pair = jnp.sum(jnp.where(match, pair_index[None, :], 0), axis=1)
    block = jnp.where(within < blk, pair, 2 * n_groups - 1 - pair)
    return block * blk + within % blk


def tables(places, head_dim):
    freq = jnp.exp(
        jnp.arange(head_dim // 2, dtype=jnp.float32) * (-2.0 * math.log(THETA) / head_dim)
    )
    angle = places.astype(jnp.float32)[:, None] * freq[None, :]
    return (jnp.cos(angle), jnp.sin(angle))


def rotate(flat, cosine, sine, head_dim):
    rows = flat.shape[0]
    split = flat.reshape(rows, -1, head_dim)
    half = head_dim // 2
    first = split[..., :half]
    second = split[..., half:]
    cos_b = cosine[:, None, :]
    sin_b = sine[:, None, :]
    out = jnp.concatenate([first * cos_b - second * sin_b, second * cos_b + first * sin_b], axis=-1)
    return out.reshape(rows, -1)


def silu_parts(gate):
    sig = jax.nn.sigmoid(gate)
    return (gate * sig, sig * (1.0 + gate * (1.0 - sig)))


def rows_by(left, right):
    return jnp.einsum("td,fd->tf", left, right, preferred_element_type=jnp.float32)


def outer_sum(left, right):
    return jnp.einsum("tf,td->fd", left, right, preferred_element_type=jnp.float32)


def per_device_any(
    tokens,
    pair_index,
    gain_attn,
    w_query,
    w_key,
    w_value,
    w_out,
    gain_ffn,
    w_gate,
    w_up,
    w_down,
    cotangent,
):
    f32 = jnp.float32
    bf16 = jnp.bfloat16
    n_ctx = lax.axis_size("ctx")
    n_fsdp = lax.axis_size("fsdp")
    tok = tokens.shape[0]
    group_rows = tok * n_fsdp
    blk = group_rows // 2
    total = group_rows * n_ctx
    ctx_index = lax.axis_index("ctx")
    fsdp_index = lax.axis_index("fsdp")
    local_rows = (ctx_index * n_fsdp + fsdp_index) * tok + jnp.arange(tok, dtype=jnp.int32)
    local_places = place_of(local_rows, pair_index, n_ctx, blk)
    group_places = place_of(
        ctx_index * group_rows + jnp.arange(group_rows, dtype=jnp.int32), pair_index, n_ctx, blk
    )
    key_places = place_of(jnp.arange(total, dtype=jnp.int32), pair_index, n_ctx, blk)
    group_cos, group_sin = tables(group_places, HD)
    query_full, key_full, value_full, out_full, gain_one, gain_two = (
        lax.all_gather(w_query, ("ctx", "fsdp"), axis=0, tiled=True),
        lax.all_gather(w_key, ("ctx", "fsdp"), axis=0, tiled=True),
        lax.all_gather(w_value, ("ctx", "fsdp"), axis=0, tiled=True),
        lax.all_gather(w_out, ("ctx", "fsdp"), axis=0, tiled=True),
        lax.all_gather(gain_attn, ("ctx", "fsdp"), axis=0, tiled=True),
        lax.all_gather(gain_ffn, ("ctx", "fsdp"), axis=0, tiled=True),
    )
    gain_one = gain_one.astype(f32)
    gain_two = gain_two.astype(f32)
    x32 = tokens.astype(f32)
    scale_one = lax.rsqrt(jnp.mean(x32 * x32, axis=-1, keepdims=True) + EPS)
    normed_one = (x32 * scale_one * gain_one).astype(bf16)
    cosine, sine = tables(local_places, HD)
    query = rotate(
        jnp.dot(normed_one, query_full, preferred_element_type=f32), cosine, sine, HD
    ).astype(bf16)
    key = rotate(
        jnp.dot(normed_one, key_full, preferred_element_type=f32), cosine, sine, HD
    ).astype(bf16)
    value = jnp.dot(normed_one, value_full, preferred_element_type=f32).astype(bf16)
    query_heads, key_heads, value_heads = (
        lax.all_to_all(query, "fsdp", split_axis=1, concat_axis=0, tiled=True),
        lax.all_to_all(key, "fsdp", split_axis=1, concat_axis=0, tiled=True),
        lax.all_to_all(value, "fsdp", split_axis=1, concat_axis=0, tiled=True),
    )
    key_all, value_all = (
        lax.all_gather(key_heads, "ctx", axis=0, tiled=True),
        lax.all_gather(value_heads, "ctx", axis=0, tiled=True),
    )
    local_width = query_heads.shape[1]
    heads_here = local_width // HD
    scale = HD ** (-0.5)
    query_parts = query_heads.reshape(2, blk, heads_here, HD)
    query_place_tiles = group_places.reshape(2, blk)
    key_tiles = key_all.reshape(2 * n_ctx, blk, heads_here, HD)
    value_tiles = value_all.reshape(2 * n_ctx, blk, heads_here, HD)
    key_place_tiles = key_places.reshape(2 * n_ctx, blk)

    def tile_scores(slot, keys, k_place):
        raw = (
            jnp.einsum("qhd,khd->hqk", query_parts[slot], keys, preferred_element_type=f32) * scale
        )
        keep = k_place[None, None, :] <= query_place_tiles[slot][None, :, None]
        return jnp.where(keep, raw, -1e30)

    def is_live(slot, k_place):
        return jnp.min(k_place) <= jnp.max(query_place_tiles[slot])

    def first_pass(carry, tile):
        keys, k_place = tile
        highs, totals = carry
        new_highs = []
        new_totals = []
        for slot in range(2):

            def first_update(high, summed):
                masked = tile_scores(slot, keys, k_place)
                fresh = jnp.maximum(high, jnp.max(masked, axis=-1))
                summed = summed * jnp.exp(high - fresh) + jnp.sum(
                    jnp.exp(masked - fresh[..., None]), axis=-1
                )
                return (fresh, summed)

            def first_leave(high, summed):
                return (high, summed)

            high, summed = lax.cond(
                is_live(slot, k_place), first_update, first_leave, highs[slot], totals[slot]
            )
            new_highs.append(high)
            new_totals.append(summed)
        return ((jnp.stack(new_highs), jnp.stack(new_totals)), None)

    start_high = jnp.full((2, heads_here, blk), -1e30, f32)
    start_total = jnp.zeros((2, heads_here, blk), f32)
    (highs, totals), unused = lax.scan(
        first_pass, (start_high, start_total), (key_tiles, key_place_tiles)
    )
    log_total = highs + jnp.log(totals)

    def second_pass(carry, tile):
        keys, values, k_place = tile
        outs = []
        for slot in range(2):

            def second_update(acc):
                masked = tile_scores(slot, keys, k_place)
                prob_low = jnp.exp(masked - log_total[slot][..., None]).astype(bf16)
                return acc + jnp.einsum(
                    "hqk,khd->qhd", prob_low, values, preferred_element_type=f32
                )

            def second_leave(acc):
                return acc

            outs.append(lax.cond(is_live(slot, k_place), second_update, second_leave, carry[slot]))
        return (jnp.stack(outs), None)

    acc_start = jnp.zeros((2, blk, heads_here, HD), f32)
    attn_acc, unused = lax.scan(second_pass, acc_start, (key_tiles, value_tiles, key_place_tiles))
    attn32 = attn_acc.reshape(group_rows, local_width)
    attn_tokens = lax.all_to_all(
        attn32.astype(bf16), "fsdp", split_axis=0, concat_axis=1, tiled=True
    )
    mid = x32 + jnp.dot(attn_tokens, out_full, preferred_element_type=f32)
    scale_two = lax.rsqrt(jnp.mean(mid * mid, axis=-1, keepdims=True) + EPS)
    normed_two = (mid * scale_two * gain_two).astype(bf16)
    dy = cotangent.astype(f32)
    dy_low = dy.astype(bf16)
    gate_local, up_local, down_local = (
        lax.all_gather(w_gate, "ctx", axis=0, tiled=True),
        lax.all_gather(w_up, "ctx", axis=0, tiled=True),
        lax.all_gather(w_down, "ctx", axis=0, tiled=True),
    )
    rows_all = lax.all_gather(normed_two, "fsdp", axis=0, tiled=True)
    gate_all = rows_by(rows_all, gate_local)
    up_all = rows_by(rows_all, up_local)
    silu_all, unused_slope = silu_parts(gate_all)
    hidden_all = (silu_all * up_all).astype(bf16)
    branch = lax.psum_scatter(
        jnp.dot(hidden_all, down_local, preferred_element_type=f32).astype(jnp.bfloat16),
        "fsdp",
        scatter_dimension=0,
        tiled=True,
    ).astype(jnp.float32)
    block_out = (mid + branch).astype(bf16)
    grad_rows_all = lax.all_gather(dy_low, "fsdp", axis=0, tiled=True)
    dhidden = rows_by(grad_rows_all, down_local)
    silu_val, slope = silu_parts(gate_all)
    dgate = (dhidden * up_all * slope).astype(bf16)
    dup = (dhidden * silu_val).astype(bf16)
    gate_term = outer_sum(dgate, rows_all)
    up_term = outer_sum(dup, rows_all)
    down_term = outer_sum(hidden_all, grad_rows_all)
    gate_grad, up_grad, down_grad = (
        lax.psum_scatter(
            gate_term.astype(jnp.bfloat16), "ctx", scatter_dimension=0, tiled=True
        ).astype(jnp.float32),
        lax.psum_scatter(
            up_term.astype(jnp.bfloat16), "ctx", scatter_dimension=0, tiled=True
        ).astype(jnp.float32),
        lax.psum_scatter(
            down_term.astype(jnp.bfloat16), "ctx", scatter_dimension=0, tiled=True
        ).astype(jnp.float32),
    )
    dnormed_two = lax.psum_scatter(
        (
            jnp.dot(dgate, gate_local, preferred_element_type=f32)
            + jnp.dot(dup, up_local, preferred_element_type=f32)
        ).astype(jnp.bfloat16),
        "fsdp",
        scatter_dimension=0,
        tiled=True,
    ).astype(jnp.float32)
    gain_two_term = jnp.sum(dnormed_two * mid * scale_two, axis=0)
    scaled_two = gain_two * dnormed_two
    dmid = (
        dy
        + scale_two * scaled_two
        - mid * scale_two**3 * jnp.mean(scaled_two * mid, axis=-1, keepdims=True)
    )
    dmid_low = dmid.astype(bf16)
    out_term = jnp.einsum("td,te->de", attn_tokens, dmid_low, preferred_element_type=f32)
    dattn = jnp.einsum("te,de->td", dmid_low, out_full, preferred_element_type=f32).astype(bf16)
    dattn_heads = lax.all_to_all(dattn, "fsdp", split_axis=1, concat_axis=0, tiled=True)
    delta = jnp.sum((dattn_heads.astype(f32) * attn32).reshape(group_rows, heads_here, HD), axis=-1)
    delta_tiles = delta.reshape(2, blk, heads_here).transpose(0, 2, 1)
    grad_parts = dattn_heads.reshape(2, blk, heads_here, HD)

    def back_pass(carry, tile):
        keys, values, k_place = tile
        key_acc = jnp.zeros((blk, heads_here, HD), f32)
        value_acc = jnp.zeros((blk, heads_here, HD), f32)
        new_query = []
        for slot in range(2):

            def back_update(q_acc, k_acc, v_acc):
                masked = tile_scores(slot, keys, k_place)
                prob = jnp.exp(masked - log_total[slot][..., None])
                prob_low = prob.astype(bf16)
                dprob = jnp.einsum(
                    "qhd,khd->hqk", grad_parts[slot], values, preferred_element_type=f32
                )
                dscore = (prob * (dprob - delta_tiles[slot][..., None])).astype(bf16)
                q_acc = (
                    q_acc
                    + jnp.einsum("hqk,khd->qhd", dscore, keys, preferred_element_type=f32) * scale
                )
                k_acc = (
                    k_acc
                    + jnp.einsum(
                        "hqk,qhd->khd", dscore, query_parts[slot], preferred_element_type=f32
                    )
                    * scale
                )
                v_acc = v_acc + jnp.einsum(
                    "hqk,qhd->khd", prob_low, grad_parts[slot], preferred_element_type=f32
                )
                return (q_acc, k_acc, v_acc)

            def back_leave(q_acc, k_acc, v_acc):
                return (q_acc, k_acc, v_acc)

            q_acc, key_acc, value_acc = lax.cond(
                is_live(slot, k_place), back_update, back_leave, carry[slot], key_acc, value_acc
            )
            new_query.append(q_acc)
        return (jnp.stack(new_query), (key_acc, value_acc))

    dquery_start = jnp.zeros((2, blk, heads_here, HD), f32)
    dquery_acc, (dkey_tiles, dvalue_tiles) = lax.scan(
        back_pass, dquery_start, (key_tiles, value_tiles, key_place_tiles)
    )
    dkey_all = dkey_tiles.reshape(total, local_width)
    dvalue_all = dvalue_tiles.reshape(total, local_width)
    dkey_own, dvalue_own = (
        lax.psum_scatter(
            dkey_all.astype(jnp.bfloat16), "ctx", scatter_dimension=0, tiled=True
        ).astype(jnp.float32),
        lax.psum_scatter(
            dvalue_all.astype(jnp.bfloat16), "ctx", scatter_dimension=0, tiled=True
        ).astype(jnp.float32),
    )
    dquery_low = rotate(
        dquery_acc.reshape(group_rows, local_width), group_cos, -group_sin, HD
    ).astype(bf16)
    dkey_low = rotate(dkey_own, group_cos, -group_sin, HD).astype(bf16)
    dvalue_low = dvalue_own.astype(bf16)
    dquery_tok, dkey_tok, dvalue_tok = (
        lax.all_to_all(dquery_low, "fsdp", split_axis=0, concat_axis=1, tiled=True),
        lax.all_to_all(dkey_low, "fsdp", split_axis=0, concat_axis=1, tiled=True),
        lax.all_to_all(dvalue_low, "fsdp", split_axis=0, concat_axis=1, tiled=True),
    )
    dnormed_one = (
        jnp.einsum("te,de->td", dquery_tok, query_full, preferred_element_type=f32)
        + jnp.einsum("te,de->td", dkey_tok, key_full, preferred_element_type=f32)
        + jnp.einsum("te,de->td", dvalue_tok, value_full, preferred_element_type=f32)
    )
    query_term = jnp.einsum("td,te->de", normed_one, dquery_tok, preferred_element_type=f32)
    key_term = jnp.einsum("td,te->de", normed_one, dkey_tok, preferred_element_type=f32)
    value_term = jnp.einsum("td,te->de", normed_one, dvalue_tok, preferred_element_type=f32)
    gain_one_term = jnp.sum(dnormed_one * x32 * scale_one, axis=0)
    scaled_one = gain_one * dnormed_one
    input_grad = (
        dmid
        + scale_one * scaled_one
        - x32 * scale_one**3 * jnp.mean(scaled_one * x32, axis=-1, keepdims=True)
    )
    query_grad, key_grad, value_grad, out_grad, gain_attn_grad, gain_ffn_grad = (
        lax.psum_scatter(query_term, ("ctx", "fsdp"), scatter_dimension=0, tiled=True),
        lax.psum_scatter(key_term, ("ctx", "fsdp"), scatter_dimension=0, tiled=True),
        lax.psum_scatter(value_term, ("ctx", "fsdp"), scatter_dimension=0, tiled=True),
        lax.psum_scatter(out_term, ("ctx", "fsdp"), scatter_dimension=0, tiled=True),
        lax.psum_scatter(gain_one_term, ("ctx", "fsdp"), scatter_dimension=0, tiled=True),
        lax.psum_scatter(gain_two_term, ("ctx", "fsdp"), scatter_dimension=0, tiled=True),
    )
    return (
        block_out,
        input_grad,
        gain_attn_grad,
        query_grad,
        key_grad,
        value_grad,
        out_grad,
        gain_ffn_grad,
        gate_grad,
        up_grad,
        down_grad,
    )


BF16 = jnp.bfloat16
F32 = jnp.float32
LOG2E = math.log2(math.e)
VMEM = pl.BlockSpec(memory_space=pltpu.VMEM)


def mxu(a, b):
    return jnp.dot(a, b, preferred_element_type=F32)


def causal(blk):
    row = lax.broadcasted_iota(jnp.int32, (blk, blk), 0)
    col = lax.broadcasted_iota(jnp.int32, (blk, blk), 1)
    return row <= col


def attn_fwd_kernel(
    place_ref,
    qkv_ref,
    extra_ref,
    out_ref,
    o32_ref,
    lse_ref,
    seq_ref,
    k_scr,
    m_scr,
    l_scr,
    acc_scr,
    *,
    blocks,
    width,
):
    pieces = qkv_ref.shape[0]
    blk = pieces * width
    coef = LOG2E * HD**-0.5
    for s in range(blocks):
        at = pl.multiple_of(place_ref[0, s] * width, width)
        for j in range(pieces):
            lo = s * blk + j * width
            piece = qkv_ref[j, :, pl.ds(at, width)]
            seq_ref[:, lo : lo + width] = piece
            k_scr[lo : lo + width, :] = piece[HD : 2 * HD].T

    def tile(kb, q_t, masked):
        at = pl.multiple_of(kb * blk, blk)
        score = mxu(k_scr[pl.ds(at, blk), :], q_t) * coef
        if masked:
            score = jnp.where(causal(blk), score, -1e30)
        old = m_scr[...]
        new = jnp.maximum(old, jnp.max(score, axis=0, keepdims=True))
        p = jnp.exp2(score - new)
        fade = jnp.exp2(old - new)
        m_scr[...] = new
        l_scr[...] = l_scr[...] * fade + jnp.sum(p, axis=0, keepdims=True)
        acc_scr[...] = acc_scr[...] * fade + mxu(seq_ref[2 * HD :, pl.ds(at, blk)], p.astype(BF16))

    for qb in range(blocks):
        lo = qb * blk
        q_t = seq_ref[:HD, lo : lo + blk]
        m_scr[...] = jnp.full_like(m_scr, -1e30)
        l_scr[...] = jnp.zeros_like(l_scr)
        acc_scr[...] = jnp.zeros_like(acc_scr)
        tile(qb, q_t, True)
        if qb > 0:

            @pl.loop(0, qb)
            def _(kb):
                tile(kb, q_t, False)

        o = acc_scr[...] / l_scr[...]
        o32_ref[:, lo : lo + blk] = o
        lse_ref[:, lo : lo + blk] = m_scr[...] + jnp.log2(l_scr[...])
        low = o.astype(BF16)
        for j in range(pieces):
            owner = place_ref[1, qb] * pieces + j
            out_ref[owner, :HD] = low[:, j * width : (j + 1) * width]
            out_ref[owner, HD:] = extra_ref[...]


def attn_fwd(place, qkv, extra, blocks):
    pieces, _, cols = qkv.shape
    total = pieces * cols
    blk = total // blocks
    return pl.pallas_call(
        functools.partial(attn_fwd_kernel, blocks=blocks, width=cols // blocks),
        out_shape=(
            jax.ShapeDtypeStruct((blocks * pieces, HD + extra.shape[0], cols // blocks), BF16),
            jax.ShapeDtypeStruct((HD, total), F32),
            jax.ShapeDtypeStruct((1, total), F32),
            jax.ShapeDtypeStruct((3 * HD, total), BF16),
        ),
        in_specs=[pl.BlockSpec(memory_space=pltpu.SMEM), VMEM, VMEM],
        out_specs=(VMEM,) * 4,
        scratch_shapes=[
            pltpu.VMEM((total, HD), BF16),
            pltpu.VMEM((1, blk), F32),
            pltpu.VMEM((1, blk), F32),
            pltpu.VMEM((HD, blk), F32),
        ],
        compiler_params=pltpu.CompilerParams(vmem_limit_bytes=40 << 20),
        cost_estimate=pl.CostEstimate(
            flops=8 * total * total * HD, bytes_accessed=8 << 20, transcendentals=total * total // 2
        ),
        name="attn_fwd",
    )(place, qkv, extra)


def attn_bwd_kernel(
    place_ref,
    seq_ref,
    o32_ref,
    lse_ref,
    do_ref,
    cos_ref,
    sin_ref,
    out_ref,
    q_scr,
    k_scr,
    v_scr,
    do_scr,
    dot_scr,
    delta_scr,
    dq_scr,
    dk_scr,
    dv_scr,
    *,
    blocks,
    width,
):
    pieces = out_ref.shape[0]
    blk = pieces * width
    scale = HD**-0.5
    coef = LOG2E * scale
    half = HD // 2
    for s in range(blocks):
        for j in range(pieces):
            lo = s * blk + j * width
            piece = do_ref[place_ref[1, s] * pieces + j, :HD]
            dot_scr[:, lo : lo + width] = piece
            do_scr[lo : lo + width, :] = piece.T
            delta_scr[:, lo : lo + width] = jnp.sum(
                piece.astype(F32) * o32_ref[:, lo : lo + width], axis=0, keepdims=True
            )
            q_scr[lo : lo + width, :] = seq_ref[:HD, lo : lo + width].T
            k_scr[lo : lo + width, :] = seq_ref[HD : 2 * HD, lo : lo + width].T
            v_scr[lo : lo + width, :] = seq_ref[2 * HD :, lo : lo + width].T
    dq_scr[...] = jnp.zeros_like(dq_scr)

    def turn_back(v, s):
        c = cos_ref[:, s * blk : (s + 1) * blk]
        n = sin_ref[:, s * blk : (s + 1) * blk]
        a, b = v[:half], v[half:]
        return jnp.concatenate([a * c + b * n, b * c - a * n], axis=0).astype(BF16)

    def put(v, s, row):
        at = pl.multiple_of(place_ref[0, s] * width, width)
        for j in range(pieces):
            out_ref[j, row * HD : (row + 1) * HD, pl.ds(at, width)] = v[:, j * width : (j + 1) * width]

    for kb in range(blocks):
        lo = kb * blk
        k = k_scr[lo : lo + blk, :]
        v = v_scr[lo : lo + blk, :]
        k_t = seq_ref[HD : 2 * HD, lo : lo + blk]

        def tile(qb, masked):
            here = pl.ds(pl.multiple_of(qb * blk, blk), blk)
            p = jnp.exp2(mxu(k, seq_ref[:HD, here]) * coef - lse_ref[:, here])
            if masked:
                p = jnp.where(causal(blk), p, 0.0)
            dp = mxu(v, dot_scr[:, here])
            ds = (p * (dp - delta_scr[:, here])).astype(BF16)
            dq_scr[:, here] += mxu(k_t, ds)
            return mxu(ds, q_scr[here, :]), mxu(p.astype(BF16), do_scr[here, :])

        dk_scr[...], dv_scr[...] = tile(kb, True)
        if kb < blocks - 1:

            @pl.loop(kb + 1, blocks)
            def _(qb):
                dk, dv = tile(qb, False)
                dk_scr[...] += dk
                dv_scr[...] += dv

        put(turn_back(dq_scr[:, lo : lo + blk] * scale, kb), kb, 0)
        put(turn_back((dk_scr[...] * scale).T, kb), kb, 1)
        put(dv_scr[...].T.astype(BF16), kb, 2)


def attn_bwd(place, seq, o32, lse, do, cos, sin, blocks):
    pieces, width = do.shape[0] // blocks, do.shape[2]
    cols, total, blk = blocks * width, seq.shape[1], pieces * width
    return pl.pallas_call(
        functools.partial(attn_bwd_kernel, blocks=blocks, width=width),
        out_shape=jax.ShapeDtypeStruct((pieces, 3 * HD, cols), BF16),
        in_specs=[pl.BlockSpec(memory_space=pltpu.SMEM)] + [VMEM] * 6,
        out_specs=VMEM,
        scratch_shapes=[pltpu.VMEM((total, HD), BF16)] * 4
        + [
            pltpu.VMEM((HD, total), BF16),
            pltpu.VMEM((1, total), F32),
            pltpu.VMEM((HD, total), F32),
            pltpu.VMEM((blk, HD), F32),
            pltpu.VMEM((blk, HD), F32),
        ],
        compiler_params=pltpu.CompilerParams(vmem_limit_bytes=48 << 20),
        cost_estimate=pl.CostEstimate(
            flops=20 * total * total * HD, bytes_accessed=8 << 20, transcendentals=total * total // 2
        ),
        name="attn_bwd",
    )(place, seq, o32, lse, do, cos, sin)


ANY = pl.BlockSpec(memory_space=pl.ANY)


def mxu_nt(a, b):
    return lax.dot_general(a, b, (((1,), (1,)), ((), ())), preferred_element_type=F32)


def mxu_tn(a, b):
    return lax.dot_general(a, b, (((0,), (0,)), ((), ())), preferred_element_type=F32)


def ffn_kernel(*refs, count, step):
    x, dy = refs[:count], refs[count : 2 * count]
    w_hbm = refs[2 * count : 2 * count + 3]
    dn, br = refs[2 * count + 3 : 3 * count + 3], refs[3 * count + 3 : 4 * count + 3]
    kept = refs[4 * count + 3 : 4 * count + 6]
    x_scr, dy_scr, gate_w, up_w, down_w, hid_scr, dgate_scr, dup_scr, act_scr, dn_scr, br_scr, in_sem, w_sem, out_sem, keep_sem = refs[4 * count + 6 :]
    tok, width = x[0].shape
    hidden = gate_w.shape[0]
    rows_in = [
        pltpu.make_async_copy(src[i], dst.at[i * tok : (i + 1) * tok], in_sem.at[k, i])
        for k, (src, dst) in enumerate(((x, x_scr), (dy, dy_scr)))
        for i in range(count)
    ]
    w_in = [
        pltpu.make_async_copy(src, dst, w_sem.at[k])
        for k, (src, dst) in enumerate(zip(w_hbm, (gate_w, up_w, down_w)))
    ]
    for c in rows_in[:count] + w_in[:2] + rows_in[count:] + w_in[2:]:
        c.start()
    for c in rows_in[:count] + w_in[:2]:
        c.wait()
    half = hidden // 2
    for h in range(2):
        part = slice(h * half, (h + 1) * half)
        gate = mxu_nt(x_scr[...], gate_w[part, :])
        up = mxu_nt(x_scr[...], up_w[part, :])
        sig = jax.nn.sigmoid(gate)
        act = gate * sig
        hid_scr[:, part] = (act * up).astype(BF16)
        act_scr[:, part] = act
        dgate_scr[:, part] = up * (sig * (1.0 + gate * (1.0 - sig)))
    for c in rows_in[count:] + w_in[2:]:
        c.wait()
    for h in range(2):
        part = slice(h * half, (h + 1) * half)
        dhidden = mxu_nt(dy_scr[...], down_w[part, :])
        dup_scr[1, :, part] = (dhidden * act_scr[:, part]).astype(BF16)
        dup_scr[0, :, part] = (dhidden * dgate_scr[:, part]).astype(BF16)
    keep = [
        pltpu.make_async_copy(src, dst, keep_sem.at[k])
        for k, (src, dst) in enumerate(zip((hid_scr, dup_scr.at[0], dup_scr.at[1]), kept))
    ]
    for c in keep:
        c.start()
    sent = []
    for n in range(width // step):
        part = slice(n * step, (n + 1) * step)
        total = mxu(dup_scr[0], gate_w[:, part]) + mxu(dup_scr[1], up_w[:, part])
        dn_scr[:, part] = total.astype(BF16)
        br_scr[:, part] = mxu(hid_scr[...], down_w[:, part]).astype(BF16)
        for i in range(count):
            rows = slice(i * tok, (i + 1) * tok)
            for k, (src, dst) in enumerate(((dn_scr, dn[i]), (br_scr, br[i]))):
                sent.append(pltpu.make_async_copy(src.at[rows, part], dst.at[:, part], out_sem.at[k, i, n]))
                sent[-1].start()
    for c in keep + sent:
        c.wait()


def ffn(x, dy, gate_w, up_w, down_w):
    count, (tok, width), hidden = len(x), x[0].shape, gate_w.shape[0]
    rows, step = count * tok, width // 4
    out = pl.pallas_call(
        functools.partial(ffn_kernel, count=count, step=step),
        in_specs=[ANY] * (2 * count + 3),
        out_specs=[ANY] * (2 * count + 3),
        out_shape=[jax.ShapeDtypeStruct((tok, width), BF16)] * (2 * count)
        + [jax.ShapeDtypeStruct((rows, hidden), BF16)] * 3,
        scratch_shapes=[pltpu.VMEM((rows, width), BF16)] * 2
        + [pltpu.VMEM((hidden, width), BF16)] * 3
        + [
            pltpu.VMEM((rows, hidden), BF16),
            pltpu.VMEM((rows, hidden), F32),
            pltpu.VMEM((2, rows, hidden), BF16),
            pltpu.VMEM((rows, hidden), F32),
            pltpu.VMEM((rows, width), BF16),
            pltpu.VMEM((rows, width), BF16),
            pltpu.SemaphoreType.DMA((2, count)),
            pltpu.SemaphoreType.DMA((3,)),
            pltpu.SemaphoreType.DMA((2, count, width // step)),
            pltpu.SemaphoreType.DMA((3,)),
        ],
        compiler_params=pltpu.CompilerParams(vmem_limit_bytes=60 << 20),
        cost_estimate=pl.CostEstimate(
            flops=12 * rows * hidden * width, bytes_accessed=6 * hidden * width + 16 * rows * width, transcendentals=rows * hidden
        ),
        name="ffn",
    )(*x, *dy, gate_w, up_w, down_w)
    return out[:count], out[count : 2 * count], out[2 * count :]


def outer_kernel(*refs, lefts, rights):
    order = refs[0]
    left, right = refs[1 : 1 + lefts], refs[1 + lefts : 1 + lefts + rights]
    send, keep, l_scr, r_scr, l_sem, r_sem = refs[1 + lefts + rights :]
    i = pl.program_id(0)

    def into(parts, scr, sem):
        at, out = 0, []
        for k, part in enumerate(parts):
            out.append(pltpu.make_async_copy(part, scr.at[at : at + part.shape[0]], sem.at[k]))
            at += part.shape[0]
        return out

    @pl.when(i == 0)
    def _():
        copies = into(left, l_scr, l_sem) + into(right, r_scr, r_sem)
        for c in copies:
            c.start()
        for c in copies:
            c.wait()

    tile = send.shape[1]
    l = l_scr[:, pl.ds(pl.multiple_of(order[i] * tile, tile), tile)]
    v = mxu_tn(l, r_scr[...]).astype(BF16)

    @pl.when(i < 2)
    def _():
        send[0] = v

    @pl.when(i >= 2)
    def _():
        keep[0] = v


def outer(order, left, right):
    cols, width = left[0].shape[1], right[0].shape[1]
    rows = sum(p.shape[0] for p in left)
    tile = cols // 4
    return pl.pallas_call(
        functools.partial(outer_kernel, lefts=len(left), rights=len(right)),
        grid=(4,),
        in_specs=[pl.BlockSpec(memory_space=pltpu.SMEM)] + [ANY] * (len(left) + len(right)),
        out_specs=[
            pl.BlockSpec((1, tile, width), lambda i: (jnp.minimum(i, 1), 0, 0)),
            pl.BlockSpec((1, tile, width), lambda i: (jnp.maximum(i - 2, 0), 0, 0)),
        ],
        out_shape=[jax.ShapeDtypeStruct((2, tile, width), BF16)] * 2,
        scratch_shapes=[
            pltpu.VMEM((rows, cols), BF16),
            pltpu.VMEM((rows, width), BF16),
            pltpu.SemaphoreType.DMA((len(left),)),
            pltpu.SemaphoreType.DMA((len(right),)),
        ],
        compiler_params=pltpu.CompilerParams(vmem_limit_bytes=60 << 20),
        cost_estimate=pl.CostEstimate(
            flops=2 * rows * cols * width, bytes_accessed=2 * (rows * (cols + width) + cols * width), transcendentals=0
        ),
        name="outer",
    )(order, *left, *right)


FAR = ("ctx", "row")
NEAR = ("col", "core")


def swap(v, axis):
    return lax.ppermute(v, axis, [(0, 1), (1, 0)])


def shift(v):
    n = lax.axis_size("ctx")
    return lax.ppermute(v, "ctx", [(i, (i + 1) % n) for i in range(n)])


class Flow:
    def __init__(self, steps):
        self.steps = steps
        self.result = None
        self.pending = next(steps)

    def take(self, got):
        try:
            self.pending = self.steps.send(got)
        except StopIteration as end:
            self.pending, self.result = None, end.value

    def run_on(self):
        self.take(self.pending)


def stage(flows, values=(), then=None):
    got, values = lax.optimization_barrier(([f.pending for f in flows], values))
    if then is not None:
        then(values)
    for f, g in zip(flows, got, strict=True):
        f.take(g)
    return values


def spread(v, slots):
    slots[0, 0] = v
    n = lax.axis_size("ctx")
    for c in range(n - 1):
        slots[c + 1, 0], slots[c, 1] = yield shift(slots[c, 0]), swap(slots[c, 0], "row")
    slots[n - 1, 1] = yield swap(slots[n - 1, 0], "row")
    return slots


def collect(terms, marks):
    n = lax.axis_size("ctx")
    total = None
    for c in [*range(1, n), 0]:
        if total is None:
            across = yield swap(terms[c, 1], "row")
            total = terms[c, 0].astype(F32) + across.astype(F32)
        else:
            marks.append(total.astype(BF16))
            across, ahead = yield swap(terms[c, 1], "row"), shift(marks[-1])
            total = terms[c, 0].astype(F32) + across.astype(F32) + ahead.astype(F32)
    return total


def reduce_near(send, keep):
    got = yield swap(send, "core")
    rows = keep.shape[1] // 2
    upper, lower = (
        (keep[0, p].astype(F32) + got[0, p].astype(F32)).astype(BF16)
        for p in (slice(0, rows), slice(rows, None))
    )
    upper = yield swap(upper, "col")
    lower = yield swap(lower, "col")
    return keep[1], got[1], upper, lower


def add_terms(keep, got, upper, lower):
    return keep.astype(F32) + got.astype(F32) + jnp.concatenate([upper, lower], axis=0).astype(F32)


def after(v, first):
    return lax.optimization_barrier((v, first))[0]


def beside(v, tok):
    return jnp.pad(v.reshape(*v.shape[:-1], 1, -1), [(0, 0)] * (v.ndim - 1) + [(0, 15), (0, tok - v.shape[-1])])


def by_side(index, mine, theirs):
    return jnp.where(index == 0, mine, theirs), jnp.where(index == 0, theirs, mine)


def to_near(v, col_at, core_at):
    keep, give = by_side(col_at, v[0], v[1])
    got = yield swap(give, "col")
    both = jnp.stack(by_side(col_at, keep, got))
    keep, give = by_side(core_at, both[:, 0], both[:, 1])
    got = yield swap(give, "core")
    return jnp.stack(by_side(core_at, keep, got), axis=1)


def sum_near(v, col_at, core_at):
    keep, give = by_side(core_at, v[:, :, 0], v[:, :, 1])
    got = yield swap(give, "core")
    total = keep.astype(F32) + got.astype(F32)
    keep, give = by_side(col_at, total[:, 0], total[:, 1])
    give = give.astype(BF16)
    rows = give.shape[1] // 2
    upper = yield swap(give[:, :rows], "col")
    lower = yield swap(give[:, rows:], "col")
    return keep + jnp.concatenate([upper, lower], axis=1).astype(F32)


def gather_heads(send, col_at, core_at):
    mine = yield lax.all_to_all(send, FAR, split_axis=0, concat_axis=0, tiled=True)
    part = mine.shape[0] // 2
    upper = yield swap(mine[:part], "col")
    lower = yield swap(mine[part:], "col")
    other = jnp.concatenate([upper, lower], axis=0)
    mine_two, other_two = yield swap(mine, "core"), swap(other, "core")
    mine_pair = by_side(core_at, mine, mine_two)
    other_pair = by_side(core_at, other, other_two)
    halves = [by_side(col_at, a, b) for a, b in zip(mine_pair, other_pair, strict=True)]
    return jnp.stack([halves[0][0], halves[1][0], halves[0][1], halves[1][1]], axis=1)


def per_device_split(
    tokens,
    pair_index,
    gain_attn,
    w_query,
    w_key,
    w_value,
    w_out,
    gain_ffn,
    w_gate,
    w_up,
    w_down,
    cotangent,
):
    n_ctx = lax.axis_size("ctx")
    near = lax.axis_size("col") * lax.axis_size("core")
    far = 2 * n_ctx
    tok, width = tokens.shape
    own_in = w_query.shape[0]
    ctx_at, row_at, col_at, core_at = (lax.axis_index(a) for a in ("ctx", "row", "col", "core"))
    near_at = col_at * lax.axis_size("core") + core_at
    blk = near * tok
    rows_here = far * tok
    group = near * HD

    slots = jnp.arange(far, dtype=jnp.int32)
    ctxs = jnp.arange(n_ctx, dtype=jnp.int32)

    def block_of(ctx, row):
        pair = jnp.sum(jnp.where(ctx[:, None] == ctxs[None, :], pair_index[None, :], 0), axis=1)
        return jnp.where(row == 0, pair, far - 1 - pair)

    def place_of_block(block):
        return jnp.sum(jnp.where(block[None, :] == slots[:, None], slots[None, :], 0), axis=1)

    slot_block = block_of((ctx_at - slots % n_ctx + n_ctx) % n_ctx, row_at ^ (slots // n_ctx))
    places = jnp.stack([place_of_block(slot_block), place_of_block(block_of(slots // 2, slots % 2))])
    freq = jnp.exp(jnp.arange(HD // 2, dtype=F32) * (-2.0 * math.log(THETA) / HD))
    token_places = (
        slot_block[:, None] * blk + near_at * tok + jnp.arange(tok, dtype=jnp.int32)[None, :]
    ).reshape(rows_here)
    angle = freq[:, None] * token_places.astype(F32)[None, :]
    cosine, sine = jnp.cos(angle), jnp.sin(angle)
    seq_angle = freq[:, None] * jnp.arange(far * blk, dtype=jnp.int32).astype(F32)[None, :]
    seq_cos, seq_sin = jnp.cos(seq_angle), jnp.sin(seq_angle)

    gain_one = gain_attn.astype(F32)[:, None]
    send = jnp.concatenate(
        [
            (w.astype(F32) * gain_one).astype(BF16).reshape(own_in, far, group)
            for w in (w_query, w_key, w_value)
        ],
        axis=2,
    ).transpose(1, 0, 2)
    x32 = tokens.astype(F32)
    scale_one = lax.rsqrt(jnp.mean(x32 * x32, axis=-1, keepdims=True) + EPS)
    gate_w = lax.all_gather(w_gate, NEAR, axis=0, tiled=True)

    def rows_of(by_slot):
        return jnp.concatenate([by_slot[c, r] for r in range(2) for c in range(n_ctx)], axis=0)

    one_flow = Flow(spread((x32 * scale_one).astype(BF16), {}))
    heads_flow = Flow(gather_heads(send, col_at, core_at))
    w_out = stage([one_flow, heads_flow], w_out)
    out_w = lax.all_gather(w_out, FAR + NEAR, axis=0, tiled=True)
    for _ in range(n_ctx - 2):
        stage([one_flow, heads_flow])
    w_up, dy_low = stage([one_flow, heads_flow], (w_up, cotangent))
    up_w = lax.all_gather(w_up, NEAR, axis=0, tiled=True)
    w_heads = heads_flow.result.reshape(width, 3 * group)
    rows_one = rows_of(one_flow.result)

    half = HD // 2
    dy_by = {}
    dy_flow = Flow(spread(dy_low, dy_by))
    flat = jnp.einsum("de,td->et", w_heads, rows_one, preferred_element_type=F32)
    qkv = flat.reshape(3, near, 2, half, rows_here)
    first, second = qkv[:2, :, 0], qkv[:2, :, 1]
    turned = jnp.stack([first * cosine - second * sine, second * cosine + first * sine], axis=2)
    qkv = jnp.concatenate([turned, qkv[2:]], axis=0).astype(BF16)
    qkv = qkv.transpose(1, 0, 2, 3, 4).reshape(near, 3 * HD, rows_here)
    qkv = stage([dy_flow], qkv)
    qkv_head, gate_w, out_w = stage(
        [dy_flow],
        (lax.all_to_all(qkv, NEAR, split_axis=0, concat_axis=0, tiled=True), gate_w, out_w),
    )
    down_w = lax.all_gather(after(w_down, qkv_head), NEAR, axis=0, tiled=True)
    attn_head, o32, lse, seq = stage(
        [dy_flow], attn_fwd(places, qkv_head, beside(gain_ffn, tok), far)
    )
    attn, up_w = stage(
        [dy_flow],
        (lax.all_to_all(attn_head, FAR + NEAR, split_axis=0, concat_axis=0, tiled=True), up_w),
    )
    gain_two = attn[:, HD, :own_in].reshape(1, width).astype(F32)
    attn = attn[:, :HD].reshape(width, tok)

    mid = x32 + jnp.einsum("et,ed->td", attn, out_w, preferred_element_type=F32)
    scale_two = lax.rsqrt(jnp.mean(mid * mid, axis=-1, keepdims=True) + EPS)
    normed_two = (mid * scale_two * gain_two).astype(BF16)
    side_flow = Flow(
        to_near(attn_head[:, :HD].reshape(far, 2, 2, HD, tok).transpose(1, 2, 3, 0, 4), col_at, core_at)
    )

    two, dn_by, br_by, kept = {}, {}, {}, []
    two_flow = Flow(spread(normed_two, two))

    def feed(cs):
        names = [(c, r) for c in cs for r in range(2)]
        dn, br, lefts = ffn(
            [two[k] for k in names], [dy_by[k] for k in names], gate_w, up_w, down_w
        )
        return dict(zip(names, dn, strict=True)), dict(zip(names, br, strict=True)), lefts

    def fed(results):
        dn, br, lefts = results
        dn_by.update(dn)
        br_by.update(br)
        kept.append(lefts)

    stage([two_flow, side_flow])
    stage([two_flow, side_flow], feed([0]), fed)
    for c in range(1, n_ctx - 1):
        stage([two_flow], feed([c]), fed)
    marks = []
    dn_flow = Flow(collect(dn_by, marks))
    stage([dn_flow], feed([n_ctx - 1]), fed)
    names = [(c, r) for c in range(n_ctx) for r in range(2)]
    two_rows, dy_rows = [two[k] for k in names], [dy_by[k] for k in names]
    tiles = near_at ^ jnp.array([3, 1, 2, 0], jnp.int32)
    lefts = [[k[i] for k in kept] for i in range(3)]
    gate_terms = outer(tiles, *after((lefts[1], two_rows), marks[-1]))
    gate_flow = Flow(reduce_near(*stage([dn_flow], gate_terms)))
    up_terms = outer(tiles, *after((lefts[2], two_rows), marks[-1]))
    up_flow = Flow(reduce_near(*stage([dn_flow, gate_flow], up_terms)))
    down_terms = outer(tiles, *after((lefts[0], dy_rows), marks[-1]))
    down_terms, br_by = stage([dn_flow, up_flow], (down_terms, br_by))
    down_flow = Flow(reduce_near(*down_terms))
    dnormed_two = dn_flow.result

    dy = cotangent.astype(F32)
    gain_two_term = jnp.sum(dnormed_two * mid * scale_two, axis=0)
    scaled_two = gain_two * dnormed_two
    dmid = (
        dy
        + scale_two * scaled_two
        - mid * scale_two**3 * jnp.mean(scaled_two * mid, axis=-1, keepdims=True)
    )
    dmid_low = dmid.astype(BF16)
    dattn = jnp.einsum("ed,td->et", out_w, dmid_low, preferred_element_type=F32).astype(BF16)
    gain_high = gain_two_term.astype(BF16)
    gain_low = (gain_two_term - gain_high.astype(F32)).astype(BF16)
    dattn = jnp.concatenate(
        [
            dattn.reshape(far * near, HD, tok),
            beside(
                jnp.concatenate(
                    [v.reshape(far * near, own_in) for v in (gain_high, gain_low)], axis=1
                ),
                tok,
            ),
        ],
        axis=1,
    )
    br_flow = Flow(collect(br_by, []))
    gate_flow.run_on()
    br_first = br_flow.pending
    br_flow.run_on()
    dattn_head, dmid_low, _ = stage(
        [gate_flow, down_flow, br_flow],
        (
            lax.all_to_all(dattn, FAR + NEAR, split_axis=0, concat_axis=0, tiled=True),
            dmid_low,
            br_first,
        ),
    )
    gain_parts = dattn_head[:, HD, : 2 * own_in].astype(F32)
    dmid_side = lax.all_gather(dmid_low, FAR, axis=0, tiled=True)
    up_flow.run_on()
    dqkv_head = stage(
        [up_flow, down_flow, br_flow],
        attn_bwd(places, seq, o32, lse, dattn_head, seq_cos, seq_sin, far),
    )
    rows_one = after(rows_one, dqkv_head)
    dqkv = stage(
        [br_flow, down_flow],
        lax.all_to_all(dqkv_head, NEAR, split_axis=0, concat_axis=0, tiled=True),
    )
    dqkv = dqkv.reshape(near, 3, HD, rows_here).transpose(1, 0, 2, 3).reshape(3 * group, rows_here)
    half_rows = rows_here // 2

    def dx_of(r, dqkv):
        rows = lax.slice_in_dim(dqkv, r * half_rows, (r + 1) * half_rows, axis=1)
        return jnp.einsum("et,de->td", rows, w_heads, preferred_element_type=F32).astype(BF16)

    dx_other, dqkv = lax.optimization_barrier((dx_of(1, dqkv), dqkv))
    dx_own, dqkv = lax.optimization_barrier((dx_of(0, dqkv), dqkv))
    dx = [v.reshape(n_ctx, tok, width) for v in (dx_own, dx_other)]
    dx_flow = Flow(collect({(c, r): dx[r][c] for c in range(n_ctx) for r in range(2)}, marks))
    heads_grad = jnp.einsum("td,et->de", rows_one, dqkv, preferred_element_type=F32).astype(BF16)
    heads_flow = Flow(
        sum_near(heads_grad.reshape(far, 2, 2, own_in, 3 * group), col_at, core_at)
    )
    dmid_side = stage([dx_flow, heads_flow], dmid_side)
    attn_side, dmid_side = after(
        (side_flow.result.reshape(group, rows_here), dmid_side), marks[-1]
    )
    out_term = jnp.einsum("et,td->ed", attn_side, dmid_side, preferred_element_type=F32)
    heads_first = heads_flow.pending
    heads_flow.run_on()
    ffn_terms, out_term, _ = stage(
        [dx_flow, heads_flow],
        ([f.result for f in (gate_flow, up_flow, down_flow)], out_term.astype(BF16), heads_first),
    )
    gate_grad, up_grad, down_grad = (add_terms(*terms) for terms in ffn_terms)
    out_flow = Flow(sum_near(out_term.reshape(1, 2, 2, own_in, width), col_at, core_at))
    for _ in range(n_ctx - 2):
        stage([dx_flow, out_flow])
    out_flow.run_on()
    scaled_one = dx_flow.result
    input_grad = (
        dmid
        + scale_one * scaled_one
        - x32 * scale_one**3 * jnp.mean(scaled_one * x32, axis=-1, keepdims=True)
    )
    back = lax.all_to_all(heads_flow.result.astype(BF16), FAR, split_axis=0, concat_axis=0, tiled=True).astype(F32)
    raw = [
        back[:, :, i * group : (i + 1) * group].transpose(1, 0, 2).reshape(own_in, -1)
        for i in range(3)
    ]
    gain_attn_grad = sum(
        jnp.sum(w.astype(F32) * g, axis=1)
        for w, g in zip((w_query, w_key, w_value), raw, strict=True)
    )
    query_grad, key_grad, value_grad = (g * gain_one for g in raw)
    gain_ffn_grad = jnp.sum(gain_parts[:, :own_in] + gain_parts[:, own_in:], axis=0)
    return (
        (mid + br_flow.result).astype(BF16),
        input_grad,
        gain_attn_grad,
        query_grad,
        key_grad,
        value_grad,
        out_flow.result[0],
        gain_ffn_grad,
        gate_grad,
        up_grad,
        down_grad,
    )


def solution(mesh):
    n_ctx, n_fsdp = mesh.shape["ctx"], mesh.shape["fsdp"]

    def step(*args):
        if n_fsdp == 8 and n_ctx == 4 and n_ctx * n_fsdp * HD == args[3].shape[1]:
            body, axes = per_device_split, FAR + NEAR
            over = Mesh(np.asarray(mesh.devices).reshape(n_ctx, 2, 2, 2), axes)
        else:
            body, axes, over = per_device_any, ("ctx", "fsdp"), mesh
        rows, line = P(axes, None), P(axes)
        return jax.shard_map(
            body,
            mesh=over,
            in_specs=(rows, P(), line, rows, rows, rows, rows, line, rows, rows, rows, rows),
            out_specs=(rows, rows, line, rows, rows, rows, rows, line, rows, rows, rows),
            check_vma=False,
        )(*args)

    return step
```

```python
import functools
import math

import jax
import jax.numpy as jnp
import numpy as np
from jax import lax
from jax.experimental import pallas as pl
from jax.experimental.pallas import tpu as pltpu
from jax.sharding import Mesh
from jax.sharding import PartitionSpec as P

HD = 64


EPS = 1e-05
THETA = 130000.0


def place_of(rows, pair_index, n_groups, blk):
    group = rows // (2 * blk)
    within = rows % (2 * blk)
    match = group[:, None] == jnp.arange(n_groups, dtype=jnp.int32)[None, :]
    pair = jnp.sum(jnp.where(match, pair_index[None, :], 0), axis=1)
    block = jnp.where(within < blk, pair, 2 * n_groups - 1 - pair)
    return block * blk + within % blk


def tables(places, head_dim):
    freq = jnp.exp(
        jnp.arange(head_dim // 2, dtype=jnp.float32) * (-2.0 * math.log(THETA) / head_dim)
    )
    angle = places.astype(jnp.float32)[:, None] * freq[None, :]
    return (jnp.cos(angle), jnp.sin(angle))


def rotate(flat, cosine, sine, head_dim):
    rows = flat.shape[0]
    split = flat.reshape(rows, -1, head_dim)
    half = head_dim // 2
    first = split[..., :half]
    second = split[..., half:]
    cos_b = cosine[:, None, :]
    sin_b = sine[:, None, :]
    out = jnp.concatenate([first * cos_b - second * sin_b, second * cos_b + first * sin_b], axis=-1)
    return out.reshape(rows, -1)


def silu_parts(gate):
    sig = jax.nn.sigmoid(gate)
    return (gate * sig, sig * (1.0 + gate * (1.0 - sig)))


def rows_by(left, right):
    return jnp.einsum("td,fd->tf", left, right, preferred_element_type=jnp.float32)


def outer_sum(left, right):
    return jnp.einsum("tf,td->fd", left, right, preferred_element_type=jnp.float32)


def per_device_any(
    tokens,
    pair_index,
    gain_attn,
    w_query,
    w_key,
    w_value,
    w_out,
    gain_ffn,
    w_gate,
    w_up,
    w_down,
    cotangent,
):
    f32 = jnp.float32
    bf16 = jnp.bfloat16
    n_ctx = lax.axis_size("ctx")
    n_fsdp = lax.axis_size("fsdp")
    tok = tokens.shape[0]
    group_rows = tok * n_fsdp
    blk = group_rows // 2
    total = group_rows * n_ctx
    ctx_index = lax.axis_index("ctx")
    fsdp_index = lax.axis_index("fsdp")
    local_rows = (ctx_index * n_fsdp + fsdp_index) * tok + jnp.arange(tok, dtype=jnp.int32)
    local_places = place_of(local_rows, pair_index, n_ctx, blk)
    group_places = place_of(
        ctx_index * group_rows + jnp.arange(group_rows, dtype=jnp.int32), pair_index, n_ctx, blk
    )
    key_places = place_of(jnp.arange(total, dtype=jnp.int32), pair_index, n_ctx, blk)
    group_cos, group_sin = tables(group_places, HD)
    query_full, key_full, value_full, out_full, gain_one, gain_two = (
        lax.all_gather(w_query, ("ctx", "fsdp"), axis=0, tiled=True),
        lax.all_gather(w_key, ("ctx", "fsdp"), axis=0, tiled=True),
        lax.all_gather(w_value, ("ctx", "fsdp"), axis=0, tiled=True),
        lax.all_gather(w_out, ("ctx", "fsdp"), axis=0, tiled=True),
        lax.all_gather(gain_attn, ("ctx", "fsdp"), axis=0, tiled=True),
        lax.all_gather(gain_ffn, ("ctx", "fsdp"), axis=0, tiled=True),
    )
    gain_one = gain_one.astype(f32)
    gain_two = gain_two.astype(f32)
    x32 = tokens.astype(f32)
    scale_one = lax.rsqrt(jnp.mean(x32 * x32, axis=-1, keepdims=True) + EPS)
    normed_one = (x32 * scale_one * gain_one).astype(bf16)
    cosine, sine = tables(local_places, HD)
    query = rotate(
        jnp.dot(normed_one, query_full, preferred_element_type=f32), cosine, sine, HD
    ).astype(bf16)
    key = rotate(
        jnp.dot(normed_one, key_full, preferred_element_type=f32), cosine, sine, HD
    ).astype(bf16)
    value = jnp.dot(normed_one, value_full, preferred_element_type=f32).astype(bf16)
    query_heads, key_heads, value_heads = (
        lax.all_to_all(query, "fsdp", split_axis=1, concat_axis=0, tiled=True),
        lax.all_to_all(key, "fsdp", split_axis=1, concat_axis=0, tiled=True),
        lax.all_to_all(value, "fsdp", split_axis=1, concat_axis=0, tiled=True),
    )
    key_all, value_all = (
        lax.all_gather(key_heads, "ctx", axis=0, tiled=True),
        lax.all_gather(value_heads, "ctx", axis=0, tiled=True),
    )
    local_width = query_heads.shape[1]
    heads_here = local_width // HD
    scale = HD ** (-0.5)
    query_parts = query_heads.reshape(2, blk, heads_here, HD)
    query_place_tiles = group_places.reshape(2, blk)
    key_tiles = key_all.reshape(2 * n_ctx, blk, heads_here, HD)
    value_tiles = value_all.reshape(2 * n_ctx, blk, heads_here, HD)
    key_place_tiles = key_places.reshape(2 * n_ctx, blk)

    def tile_scores(slot, keys, k_place):
        raw = (
            jnp.einsum("qhd,khd->hqk", query_parts[slot], keys, preferred_element_type=f32) * scale
        )
        keep = k_place[None, None, :] <= query_place_tiles[slot][None, :, None]
        return jnp.where(keep, raw, -1e30)

    def is_live(slot, k_place):
        return jnp.min(k_place) <= jnp.max(query_place_tiles[slot])

    def first_pass(carry, tile):
        keys, k_place = tile
        highs, totals = carry
        new_highs = []
        new_totals = []
        for slot in range(2):

            def first_update(high, summed):
                masked = tile_scores(slot, keys, k_place)
                fresh = jnp.maximum(high, jnp.max(masked, axis=-1))
                summed = summed * jnp.exp(high - fresh) + jnp.sum(
                    jnp.exp(masked - fresh[..., None]), axis=-1
                )
                return (fresh, summed)

            def first_leave(high, summed):
                return (high, summed)

            high, summed = lax.cond(
                is_live(slot, k_place), first_update, first_leave, highs[slot], totals[slot]
            )
            new_highs.append(high)
            new_totals.append(summed)
        return ((jnp.stack(new_highs), jnp.stack(new_totals)), None)

    start_high = jnp.full((2, heads_here, blk), -1e30, f32)
    start_total = jnp.zeros((2, heads_here, blk), f32)
    (highs, totals), unused = lax.scan(
        first_pass, (start_high, start_total), (key_tiles, key_place_tiles)
    )
    log_total = highs + jnp.log(totals)

    def second_pass(carry, tile):
        keys, values, k_place = tile
        outs = []
        for slot in range(2):

            def second_update(acc):
                masked = tile_scores(slot, keys, k_place)
                prob_low = jnp.exp(masked - log_total[slot][..., None]).astype(bf16)
                return acc + jnp.einsum(
                    "hqk,khd->qhd", prob_low, values, preferred_element_type=f32
                )

            def second_leave(acc):
                return acc

            outs.append(lax.cond(is_live(slot, k_place), second_update, second_leave, carry[slot]))
        return (jnp.stack(outs), None)

    acc_start = jnp.zeros((2, blk, heads_here, HD), f32)
    attn_acc, unused = lax.scan(second_pass, acc_start, (key_tiles, value_tiles, key_place_tiles))
    attn32 = attn_acc.reshape(group_rows, local_width)
    attn_tokens = lax.all_to_all(
        attn32.astype(bf16), "fsdp", split_axis=0, concat_axis=1, tiled=True
    )
    mid = x32 + jnp.dot(attn_tokens, out_full, preferred_element_type=f32)
    scale_two = lax.rsqrt(jnp.mean(mid * mid, axis=-1, keepdims=True) + EPS)
    normed_two = (mid * scale_two * gain_two).astype(bf16)
    dy = cotangent.astype(f32)
    dy_low = dy.astype(bf16)
    gate_local, up_local, down_local = (
        lax.all_gather(w_gate, "ctx", axis=0, tiled=True),
        lax.all_gather(w_up, "ctx", axis=0, tiled=True),
        lax.all_gather(w_down, "ctx", axis=0, tiled=True),
    )
    rows_all = lax.all_gather(normed_two, "fsdp", axis=0, tiled=True)
    gate_all = rows_by(rows_all, gate_local)
    up_all = rows_by(rows_all, up_local)
    silu_all, unused_slope = silu_parts(gate_all)
    hidden_all = (silu_all * up_all).astype(bf16)
    branch = lax.psum_scatter(
        jnp.dot(hidden_all, down_local, preferred_element_type=f32).astype(jnp.bfloat16),
        "fsdp",
        scatter_dimension=0,
        tiled=True,
    ).astype(jnp.float32)
    block_out = (mid + branch).astype(bf16)
    grad_rows_all = lax.all_gather(dy_low, "fsdp", axis=0, tiled=True)
    dhidden = rows_by(grad_rows_all, down_local)
    silu_val, slope = silu_parts(gate_all)
    dgate = (dhidden * up_all * slope).astype(bf16)
    dup = (dhidden * silu_val).astype(bf16)
    gate_term = outer_sum(dgate, rows_all)
    up_term = outer_sum(dup, rows_all)
    down_term = outer_sum(hidden_all, grad_rows_all)
    gate_grad, up_grad, down_grad = (
        lax.psum_scatter(
            gate_term.astype(jnp.bfloat16), "ctx", scatter_dimension=0, tiled=True
        ).astype(jnp.float32),
        lax.psum_scatter(
            up_term.astype(jnp.bfloat16), "ctx", scatter_dimension=0, tiled=True
        ).astype(jnp.float32),
        lax.psum_scatter(
            down_term.astype(jnp.bfloat16), "ctx", scatter_dimension=0, tiled=True
        ).astype(jnp.float32),
    )
    dnormed_two = lax.psum_scatter(
        (
            jnp.dot(dgate, gate_local, preferred_element_type=f32)
            + jnp.dot(dup, up_local, preferred_element_type=f32)
        ).astype(jnp.bfloat16),
        "fsdp",
        scatter_dimension=0,
        tiled=True,
    ).astype(jnp.float32)
    gain_two_term = jnp.sum(dnormed_two * mid * scale_two, axis=0)
    scaled_two = gain_two * dnormed_two
    dmid = (
        dy
        + scale_two * scaled_two
        - mid * scale_two**3 * jnp.mean(scaled_two * mid, axis=-1, keepdims=True)
    )
    dmid_low = dmid.astype(bf16)
    out_term = jnp.einsum("td,te->de", attn_tokens, dmid_low, preferred_element_type=f32)
    dattn = jnp.einsum("te,de->td", dmid_low, out_full, preferred_element_type=f32).astype(bf16)
    dattn_heads = lax.all_to_all(dattn, "fsdp", split_axis=1, concat_axis=0, tiled=True)
    delta = jnp.sum((dattn_heads.astype(f32) * attn32).reshape(group_rows, heads_here, HD), axis=-1)
    delta_tiles = delta.reshape(2, blk, heads_here).transpose(0, 2, 1)
    grad_parts = dattn_heads.reshape(2, blk, heads_here, HD)

    def back_pass(carry, tile):
        keys, values, k_place = tile
        key_acc = jnp.zeros((blk, heads_here, HD), f32)
        value_acc = jnp.zeros((blk, heads_here, HD), f32)
        new_query = []
        for slot in range(2):

            def back_update(q_acc, k_acc, v_acc):
                masked = tile_scores(slot, keys, k_place)
                prob = jnp.exp(masked - log_total[slot][..., None])
                prob_low = prob.astype(bf16)
                dprob = jnp.einsum(
                    "qhd,khd->hqk", grad_parts[slot], values, preferred_element_type=f32
                )
                dscore = (prob * (dprob - delta_tiles[slot][..., None])).astype(bf16)
                q_acc = (
                    q_acc
                    + jnp.einsum("hqk,khd->qhd", dscore, keys, preferred_element_type=f32) * scale
                )
                k_acc = (
                    k_acc
                    + jnp.einsum(
                        "hqk,qhd->khd", dscore, query_parts[slot], preferred_element_type=f32
                    )
                    * scale
                )
                v_acc = v_acc + jnp.einsum(
                    "hqk,qhd->khd", prob_low, grad_parts[slot], preferred_element_type=f32
                )
                return (q_acc, k_acc, v_acc)

            def back_leave(q_acc, k_acc, v_acc):
                return (q_acc, k_acc, v_acc)

            q_acc, key_acc, value_acc = lax.cond(
                is_live(slot, k_place), back_update, back_leave, carry[slot], key_acc, value_acc
            )
            new_query.append(q_acc)
        return (jnp.stack(new_query), (key_acc, value_acc))

    dquery_start = jnp.zeros((2, blk, heads_here, HD), f32)
    dquery_acc, (dkey_tiles, dvalue_tiles) = lax.scan(
        back_pass, dquery_start, (key_tiles, value_tiles, key_place_tiles)
    )
    dkey_all = dkey_tiles.reshape(total, local_width)
    dvalue_all = dvalue_tiles.reshape(total, local_width)
    dkey_own, dvalue_own = (
        lax.psum_scatter(
            dkey_all.astype(jnp.bfloat16), "ctx", scatter_dimension=0, tiled=True
        ).astype(jnp.float32),
        lax.psum_scatter(
            dvalue_all.astype(jnp.bfloat16), "ctx", scatter_dimension=0, tiled=True
        ).astype(jnp.float32),
    )
    dquery_low = rotate(
        dquery_acc.reshape(group_rows, local_width), group_cos, -group_sin, HD
    ).astype(bf16)
    dkey_low = rotate(dkey_own, group_cos, -group_sin, HD).astype(bf16)
    dvalue_low = dvalue_own.astype(bf16)
    dquery_tok, dkey_tok, dvalue_tok = (
        lax.all_to_all(dquery_low, "fsdp", split_axis=0, concat_axis=1, tiled=True),
        lax.all_to_all(dkey_low, "fsdp", split_axis=0, concat_axis=1, tiled=True),
        lax.all_to_all(dvalue_low, "fsdp", split_axis=0, concat_axis=1, tiled=True),
    )
    dnormed_one = (
        jnp.einsum("te,de->td", dquery_tok, query_full, preferred_element_type=f32)
        + jnp.einsum("te,de->td", dkey_tok, key_full, preferred_element_type=f32)
        + jnp.einsum("te,de->td", dvalue_tok, value_full, preferred_element_type=f32)
    )
    query_term = jnp.einsum("td,te->de", normed_one, dquery_tok, preferred_element_type=f32)
    key_term = jnp.einsum("td,te->de", normed_one, dkey_tok, preferred_element_type=f32)
    value_term = jnp.einsum("td,te->de", normed_one, dvalue_tok, preferred_element_type=f32)
    gain_one_term = jnp.sum(dnormed_one * x32 * scale_one, axis=0)
    scaled_one = gain_one * dnormed_one
    input_grad = (
        dmid
        + scale_one * scaled_one
        - x32 * scale_one**3 * jnp.mean(scaled_one * x32, axis=-1, keepdims=True)
    )
    query_grad, key_grad, value_grad, out_grad, gain_attn_grad, gain_ffn_grad = (
        lax.psum_scatter(query_term, ("ctx", "fsdp"), scatter_dimension=0, tiled=True),
        lax.psum_scatter(key_term, ("ctx", "fsdp"), scatter_dimension=0, tiled=True),
        lax.psum_scatter(value_term, ("ctx", "fsdp"), scatter_dimension=0, tiled=True),
        lax.psum_scatter(out_term, ("ctx", "fsdp"), scatter_dimension=0, tiled=True),
        lax.psum_scatter(gain_one_term, ("ctx", "fsdp"), scatter_dimension=0, tiled=True),
        lax.psum_scatter(gain_two_term, ("ctx", "fsdp"), scatter_dimension=0, tiled=True),
    )
    return (
        block_out,
        input_grad,
        gain_attn_grad,
        query_grad,
        key_grad,
        value_grad,
        out_grad,
        gain_ffn_grad,
        gate_grad,
        up_grad,
        down_grad,
    )


BF16 = jnp.bfloat16
F32 = jnp.float32
LOG2E = math.log2(math.e)
VMEM = pl.BlockSpec(memory_space=pltpu.VMEM)
ANY = pl.BlockSpec(memory_space=pl.ANY)


def mxu(a, b):
    return jnp.dot(a, b, preferred_element_type=F32)


def causal(blk):
    row = lax.broadcasted_iota(jnp.int32, (blk, blk), 0)
    col = lax.broadcasted_iota(jnp.int32, (blk, blk), 1)
    return row <= col


def attn_fwd_kernel(
    place_ref,
    qkv_ref,
    extra_ref,
    out_ref,
    o32_hbm,
    lse_ref,
    seq_hbm,
    seq_ref,
    o32_ref,
    seq_sem,
    o32_sem,
    k_scr,
    m_scr,
    l_scr,
    acc_scr,
    *,
    blocks,
    width,
):
    pieces = qkv_ref.shape[0]
    blk = pieces * width
    coef = LOG2E * HD**-0.5
    for s in range(blocks):
        at = pl.multiple_of(place_ref[0, s] * width, width)
        for j in range(pieces):
            lo = s * blk + j * width
            piece = qkv_ref[j, :, pl.ds(at, width)]
            seq_ref[:, lo : lo + width] = piece
            k_scr[lo : lo + width, :] = piece[HD : 2 * HD].T

    leaving = [pltpu.make_async_copy(seq_ref, seq_hbm, seq_sem)]
    leaving[0].start()

    def tile(kb, q_t, masked, wide=1):
        keys = pl.ds(pl.multiple_of(kb * blk, blk), wide * blk)
        score = mxu(k_scr[keys, :], q_t) * coef
        if masked:
            score = jnp.where(causal(blk), score, -1e30)
        old = m_scr[...]
        new = jnp.maximum(old, jnp.max(score, axis=0, keepdims=True))
        p = jnp.exp2(score - new)
        fade = jnp.exp2(old - new)
        m_scr[...] = new
        l_scr[...] = l_scr[...] * fade + jnp.sum(p, axis=0, keepdims=True)
        acc_scr[...] = acc_scr[...] * fade + mxu(seq_ref[2 * HD :, keys], p.astype(BF16))

    for qb in range(blocks):
        lo = qb * blk
        q_t = seq_ref[:HD, lo : lo + blk]
        m_scr[...] = jnp.full_like(m_scr, -1e30)
        l_scr[...] = jnp.zeros_like(l_scr)
        acc_scr[...] = jnp.zeros_like(acc_scr)
        tile(qb, q_t, True)
        kb = 0
        while kb < qb:
            wide = min(4, qb - kb)
            tile(kb, q_t, False, wide)
            kb += wide

        o = acc_scr[...] / l_scr[...]
        o32_ref[:, lo : lo + blk] = o
        leaving.append(
            pltpu.make_async_copy(
                o32_ref.at[:, lo : lo + blk], o32_hbm.at[:, lo : lo + blk], o32_sem.at[qb]
            )
        )
        leaving[-1].start()
        lse_ref[:, lo : lo + blk] = m_scr[...] + jnp.log2(l_scr[...])
        low = o.astype(BF16)
        for j in range(pieces):
            owner = place_ref[1, qb] * pieces + j
            out_ref[owner, :HD] = low[:, j * width : (j + 1) * width]
            out_ref[owner, HD:] = extra_ref[...]
    for c in leaving:
        c.wait()


def attn_fwd(place, qkv, extra, blocks):
    pieces, _, cols = qkv.shape
    total = pieces * cols
    blk = total // blocks
    return pl.pallas_call(
        functools.partial(attn_fwd_kernel, blocks=blocks, width=cols // blocks),
        out_shape=(
            jax.ShapeDtypeStruct((blocks * pieces, HD + extra.shape[0], cols // blocks), BF16),
            jax.ShapeDtypeStruct((HD, total), F32),
            jax.ShapeDtypeStruct((1, total), F32),
            jax.ShapeDtypeStruct((3 * HD, total), BF16),
        ),
        in_specs=[pl.BlockSpec(memory_space=pltpu.SMEM), VMEM, VMEM],
        out_specs=(VMEM, ANY, VMEM, ANY),
        scratch_shapes=[
            pltpu.VMEM((3 * HD, total), BF16),
            pltpu.VMEM((HD, total), F32),
            pltpu.SemaphoreType.DMA,
            pltpu.SemaphoreType.DMA((blocks,)),
            pltpu.VMEM((total, HD), BF16),
            pltpu.VMEM((1, blk), F32),
            pltpu.VMEM((1, blk), F32),
            pltpu.VMEM((HD, blk), F32),
        ],
        compiler_params=pltpu.CompilerParams(vmem_limit_bytes=60 << 20),
        cost_estimate=pl.CostEstimate(
            flops=8 * total * total * HD, bytes_accessed=8 << 20, transcendentals=total * total // 2
        ),
        name="attn_fwd",
    )(place, qkv, extra)


def attn_bwd_kernel(
    place_ref,
    seq_hbm,
    o32_hbm,
    lse_ref,
    do_ref,
    cos_hbm,
    sin_hbm,
    out_ref,
    seq_ref,
    o32_ref,
    cos_ref,
    sin_ref,
    in_sem,
    q_scr,
    k_scr,
    v_scr,
    do_scr,
    dot_scr,
    delta_scr,
    dq_scr,
    dk_scr,
    dv_scr,
    *,
    blocks,
    width,
):
    pieces = out_ref.shape[0]
    blk = pieces * width
    scale = HD**-0.5
    coef = LOG2E * scale
    half = HD // 2
    arriving = [
        pltpu.make_async_copy(src, dst, in_sem.at[i])
        for i, (src, dst) in enumerate(
            ((seq_hbm, seq_ref), (o32_hbm, o32_ref), (cos_hbm, cos_ref), (sin_hbm, sin_ref))
        )
    ]
    for c in arriving:
        c.start()
    for c in arriving[:2]:
        c.wait()
    for s in range(blocks):
        for j in range(pieces):
            lo = s * blk + j * width
            piece = do_ref[place_ref[1, s] * pieces + j, :HD]
            dot_scr[:, lo : lo + width] = piece
            do_scr[lo : lo + width, :] = piece.T
            delta_scr[:, lo : lo + width] = jnp.sum(
                piece.astype(F32) * o32_ref[:, lo : lo + width], axis=0, keepdims=True
            )
            q_scr[lo : lo + width, :] = seq_ref[:HD, lo : lo + width].T
            k_scr[lo : lo + width, :] = seq_ref[HD : 2 * HD, lo : lo + width].T
            v_scr[lo : lo + width, :] = seq_ref[2 * HD :, lo : lo + width].T
    dq_scr[...] = jnp.zeros_like(dq_scr)
    for c in arriving[2:]:
        c.wait()

    def turn_back(v, s):
        c = cos_ref[:, s * blk : (s + 1) * blk]
        n = sin_ref[:, s * blk : (s + 1) * blk]
        a, b = v[:half], v[half:]
        return jnp.concatenate([a * c + b * n, b * c - a * n], axis=0).astype(BF16)

    def put(v, s, row):
        at = pl.multiple_of(place_ref[0, s] * width, width)
        for j in range(pieces):
            out_ref[j, row * HD : (row + 1) * HD, pl.ds(at, width)] = v[:, j * width : (j + 1) * width]

    for kb in range(blocks):
        lo = kb * blk
        k = k_scr[lo : lo + blk, :]
        v = v_scr[lo : lo + blk, :]
        k_t = seq_ref[HD : 2 * HD, lo : lo + blk]

        def tile(qb, masked, wide=1):
            here = pl.ds(pl.multiple_of(qb * blk, blk), wide * blk)
            p = jnp.exp2(mxu(k, seq_ref[:HD, here]) * coef - lse_ref[:, here])
            if masked:
                p = jnp.where(causal(blk), p, 0.0)
            dp = mxu(v, dot_scr[:, here])
            ds = (p * (dp - delta_scr[:, here])).astype(BF16)
            dq_scr[:, here] += mxu(k_t, ds)
            return mxu(ds, q_scr[here, :]), mxu(p.astype(BF16), do_scr[here, :])

        dk_scr[...], dv_scr[...] = tile(kb, True)

        def add_tile(qb, wide):
            dk, dv = tile(qb, False, wide)
            dk_scr[...] += dk
            dv_scr[...] += dv

        qb = kb + 1
        while qb < blocks:
            wide = min(2, blocks - qb)
            add_tile(qb, wide)
            qb += wide

        put(turn_back(dq_scr[:, lo : lo + blk] * scale, kb), kb, 0)
        put(turn_back((dk_scr[...] * scale).T, kb), kb, 1)
        put(dv_scr[...].T.astype(BF16), kb, 2)


def attn_bwd(place, seq, o32, lse, do, cos, sin, blocks):
    pieces, width = do.shape[0] // blocks, do.shape[2]
    cols, total, blk = blocks * width, seq.shape[1], pieces * width
    return pl.pallas_call(
        functools.partial(attn_bwd_kernel, blocks=blocks, width=width),
        out_shape=jax.ShapeDtypeStruct((pieces, 3 * HD, cols), BF16),
        in_specs=[pl.BlockSpec(memory_space=pltpu.SMEM), ANY, ANY, VMEM, VMEM, ANY, ANY],
        out_specs=VMEM,
        scratch_shapes=[
            pltpu.VMEM(seq.shape, BF16),
            pltpu.VMEM(o32.shape, F32),
            pltpu.VMEM(cos.shape, F32),
            pltpu.VMEM(sin.shape, F32),
            pltpu.SemaphoreType.DMA((4,)),
        ]
        + [pltpu.VMEM((total, HD), BF16)] * 4
        + [
            pltpu.VMEM((HD, total), BF16),
            pltpu.VMEM((1, total), F32),
            pltpu.VMEM((HD, total), F32),
            pltpu.VMEM((blk, HD), F32),
            pltpu.VMEM((blk, HD), F32),
        ],
        compiler_params=pltpu.CompilerParams(vmem_limit_bytes=60 << 20),
        cost_estimate=pl.CostEstimate(
            flops=20 * total * total * HD, bytes_accessed=8 << 20, transcendentals=total * total // 2
        ),
        name="attn_bwd",
    )(place, seq, o32, lse, do, cos, sin)


def mxu_nt(a, b):
    return lax.dot_general(a, b, (((1,), (1,)), ((), ())), preferred_element_type=F32)


def mxu_tn(a, b):
    return lax.dot_general(a, b, (((0,), (0,)), ((), ())), preferred_element_type=F32)


def ffn_kernel(*refs, count, step):
    x, dy = refs[:count], refs[count : 2 * count]
    w_hbm = refs[2 * count : 2 * count + 3]
    dn, br = refs[2 * count + 3 : 3 * count + 3], refs[3 * count + 3 : 4 * count + 3]
    kept = refs[4 * count + 3 : 4 * count + 6]
    x_scr, dy_scr, gate_w, up_w, down_w, hid_scr, dgate_scr, dup_scr, act_scr, dn_scr, br_scr, in_sem, w_sem, out_sem, keep_sem = refs[4 * count + 6 :]
    tok, width = x[0].shape
    hidden = gate_w.shape[0]
    rows_in = [
        pltpu.make_async_copy(src[i], dst.at[i * tok : (i + 1) * tok], in_sem.at[k, i])
        for k, (src, dst) in enumerate(((x, x_scr), (dy, dy_scr)))
        for i in range(count)
    ]
    w_in = [
        pltpu.make_async_copy(src, dst, w_sem.at[k])
        for k, (src, dst) in enumerate(zip(w_hbm, (gate_w, up_w, down_w)))
    ]
    for c in rows_in[:count] + w_in[:2] + rows_in[count:] + w_in[2:]:
        c.start()
    for c in rows_in[:count] + w_in[:2]:
        c.wait()
    half = hidden // 2
    for h in range(2):
        part = slice(h * half, (h + 1) * half)
        gate = mxu_nt(x_scr[...], gate_w[part, :])
        up = mxu_nt(x_scr[...], up_w[part, :])
        sig = jax.nn.sigmoid(gate)
        act = gate * sig
        hid_scr[:, part] = (act * up).astype(BF16)
        act_scr[:, part] = act
        dgate_scr[:, part] = up * (sig * (1.0 + gate * (1.0 - sig)))
    for c in rows_in[count:] + w_in[2:]:
        c.wait()
    for h in range(2):
        part = slice(h * half, (h + 1) * half)
        dhidden = mxu_nt(dy_scr[...], down_w[part, :])
        dup_scr[1, :, part] = (dhidden * act_scr[:, part]).astype(BF16)
        dup_scr[0, :, part] = (dhidden * dgate_scr[:, part]).astype(BF16)
    keep = [
        pltpu.make_async_copy(src, dst, keep_sem.at[k])
        for k, (src, dst) in enumerate(zip((hid_scr, dup_scr.at[0], dup_scr.at[1]), kept))
    ]
    for c in keep:
        c.start()
    sent = []
    for n in range(width // step):
        part = slice(n * step, (n + 1) * step)
        total = mxu(dup_scr[0], gate_w[:, part]) + mxu(dup_scr[1], up_w[:, part])
        dn_scr[:, part] = total.astype(BF16)
        br_scr[:, part] = mxu(hid_scr[...], down_w[:, part]).astype(BF16)
        for i in range(count):
            rows = slice(i * tok, (i + 1) * tok)
            for k, (src, dst) in enumerate(((dn_scr, dn[i]), (br_scr, br[i]))):
                sent.append(pltpu.make_async_copy(src.at[rows, part], dst.at[:, part], out_sem.at[k, i, n]))
                sent[-1].start()
    for c in keep + sent:
        c.wait()


def ffn(x, dy, gate_w, up_w, down_w):
    count, (tok, width), hidden = len(x), x[0].shape, gate_w.shape[0]
    rows, step = count * tok, width // 4
    out = pl.pallas_call(
        functools.partial(ffn_kernel, count=count, step=step),
        in_specs=[ANY] * (2 * count + 3),
        out_specs=[ANY] * (2 * count + 3),
        out_shape=[jax.ShapeDtypeStruct((tok, width), BF16)] * (2 * count)
        + [jax.ShapeDtypeStruct((rows, hidden), BF16)] * 3,
        scratch_shapes=[pltpu.VMEM((rows, width), BF16)] * 2
        + [pltpu.VMEM((hidden, width), BF16)] * 3
        + [
            pltpu.VMEM((rows, hidden), BF16),
            pltpu.VMEM((rows, hidden), F32),
            pltpu.VMEM((2, rows, hidden), BF16),
            pltpu.VMEM((rows, hidden), F32),
            pltpu.VMEM((rows, width), BF16),
            pltpu.VMEM((rows, width), BF16),
            pltpu.SemaphoreType.DMA((2, count)),
            pltpu.SemaphoreType.DMA((3,)),
            pltpu.SemaphoreType.DMA((2, count, width // step)),
            pltpu.SemaphoreType.DMA((3,)),
        ],
        compiler_params=pltpu.CompilerParams(vmem_limit_bytes=60 << 20),
        cost_estimate=pl.CostEstimate(
            flops=12 * rows * hidden * width, bytes_accessed=6 * hidden * width + 16 * rows * width, transcendentals=rows * hidden
        ),
        name="ffn",
    )(*x, *dy, gate_w, up_w, down_w)
    return out[:count], out[count : 2 * count], out[2 * count :]


def outer_kernel(*refs, lefts, rights):
    order = refs[0]
    left, right = refs[1 : 1 + lefts], refs[1 + lefts : 1 + lefts + rights]
    send, keep, l_scr, r_scr, l_sem, r_sem = refs[1 + lefts + rights :]
    i = pl.program_id(0)

    def into(parts, scr, sem):
        at, out = 0, []
        for k, part in enumerate(parts):
            out.append(pltpu.make_async_copy(part, scr.at[at : at + part.shape[0]], sem.at[k]))
            at += part.shape[0]
        return out

    @pl.when(i == 0)
    def _():
        copies = into(left, l_scr, l_sem) + into(right, r_scr, r_sem)
        for c in copies:
            c.start()
        for c in copies:
            c.wait()

    tile = send.shape[1]
    l = l_scr[:, pl.ds(pl.multiple_of(order[i] * tile, tile), tile)]
    v = mxu_tn(l, r_scr[...]).astype(BF16)

    @pl.when(i < 2)
    def _():
        send[0] = v

    @pl.when(i >= 2)
    def _():
        keep[0] = v


def outer(order, left, right):
    cols, width = left[0].shape[1], right[0].shape[1]
    rows = sum(p.shape[0] for p in left)
    tile = cols // 4
    return pl.pallas_call(
        functools.partial(outer_kernel, lefts=len(left), rights=len(right)),
        grid=(4,),
        in_specs=[pl.BlockSpec(memory_space=pltpu.SMEM)] + [ANY] * (len(left) + len(right)),
        out_specs=[
            pl.BlockSpec((1, tile, width), lambda i: (jnp.minimum(i, 1), 0, 0)),
            pl.BlockSpec((1, tile, width), lambda i: (jnp.maximum(i - 2, 0), 0, 0)),
        ],
        out_shape=[jax.ShapeDtypeStruct((2, tile, width), BF16)] * 2,
        scratch_shapes=[
            pltpu.VMEM((rows, cols), BF16),
            pltpu.VMEM((rows, width), BF16),
            pltpu.SemaphoreType.DMA((len(left),)),
            pltpu.SemaphoreType.DMA((len(right),)),
        ],
        compiler_params=pltpu.CompilerParams(vmem_limit_bytes=60 << 20),
        cost_estimate=pl.CostEstimate(
            flops=2 * rows * cols * width, bytes_accessed=2 * (rows * (cols + width) + cols * width), transcendentals=0
        ),
        name="outer",
    )(order, *left, *right)


def qkv_kernel(near_ref, *refs, count):
    x, parts = refs[:count], refs[count : count + 4]
    cos_ref, sin_ref, out_ref, rows_ref, w_ref, x_scr, w_scr, x_sem, w_sem, out_sem = refs[count + 4 :]
    tok = x[0].shape[0]
    groups, depth, cols = parts[0].shape
    heads, half = out_ref.shape[0], HD // 2
    x_in = [
        pltpu.make_async_copy(x[i], x_scr.at[i * tok : (i + 1) * tok], x_sem.at[i])
        for i in range(count)
    ]
    w_in = [
        pltpu.make_async_copy(
            parts[r].at[g],
            w_scr.at[pl.ds(pl.multiple_of((g * 4 + (near_ref[0] ^ r)) * depth, depth), depth)],
            w_sem.at[r, g],
        )
        for r in range(4)
        for g in range(groups)
    ]
    for c in w_in + x_in:
        c.start()
    for c in w_in + x_in:
        c.wait()
    out = [
        pltpu.make_async_copy(x_scr, rows_ref, out_sem.at[0]),
        pltpu.make_async_copy(w_scr, w_ref, out_sem.at[1]),
    ]
    for c in out:
        c.start()
    group = heads * HD
    for i in range(3):
        y = mxu(x_scr[...], w_scr[:, i * group : (i + 1) * group]).T
        for h in range(heads):
            at = slice(i * HD, (i + 1) * HD)
            a, b = y[h * HD : h * HD + half], y[h * HD + half : (h + 1) * HD]
            if i < 2:
                c, s = cos_ref[...], sin_ref[...]
                a, b = a * c - b * s, b * c + a * s
            out_ref[h, at] = jnp.concatenate([a, b], axis=0).astype(BF16)
    for c in out:
        c.wait()


def qkv_of(near, x, parts, cos, sin):
    count, (tok, width) = len(x), x[0].shape
    groups, depth, cols = parts[0].shape
    heads = cols // (3 * HD)
    return pl.pallas_call(
        functools.partial(qkv_kernel, count=count),
        in_specs=[pl.BlockSpec(memory_space=pltpu.SMEM)] + [ANY] * (count + 4) + [VMEM] * 2,
        out_specs=[VMEM, ANY, ANY],
        out_shape=[
            jax.ShapeDtypeStruct((heads, 3 * HD, count * tok), BF16),
            jax.ShapeDtypeStruct((count * tok, width), BF16),
            jax.ShapeDtypeStruct((width, cols), BF16),
        ],
        scratch_shapes=[
            pltpu.VMEM((count * tok, width), BF16),
            pltpu.VMEM((width, cols), BF16),
            pltpu.SemaphoreType.DMA((count,)),
            pltpu.SemaphoreType.DMA((4, groups)),
            pltpu.SemaphoreType.DMA((2,)),
        ],
        compiler_params=pltpu.CompilerParams(vmem_limit_bytes=60 << 20),
        cost_estimate=pl.CostEstimate(
            flops=2 * count * tok * width * cols,
            bytes_accessed=4 * (count * tok * width + width * cols),
            transcendentals=0,
        ),
        name="qkv",
    )(near, *x, *parts, cos, sin)


def turned_rows(d_ref, d_scr, at, rows):
    heads = d_ref.shape[0]
    for i in range(3):
        for h in range(heads):
            top = (i * heads + h) * HD
            d_scr[top : top + HD] = d_ref[h, i * HD : (i + 1) * HD, at : at + rows]


def input_rows_kernel(d_hbm, w_hbm, out_ref, w_scr, d_scr, t_scr, sem, *, slot):
    rows = out_ref.shape[0]
    d_in = pltpu.make_async_copy(d_hbm.at[:, :, slot * rows : (slot + 1) * rows], d_scr, sem.at[0])
    w_in = pltpu.make_async_copy(w_hbm, w_scr, sem.at[1])
    d_in.start()
    w_in.start()
    d_in.wait()
    turned_rows(d_scr, t_scr, 0, rows)
    d = t_scr[...].T
    w_in.wait()
    out_ref[...] = mxu_nt(d, w_scr[...]).astype(BF16)


def input_rows(dqkv, w, slot, tok):
    width, cols = w.shape
    return pl.pallas_call(
        functools.partial(input_rows_kernel, slot=slot),
        in_specs=[ANY, ANY],
        out_specs=VMEM,
        out_shape=jax.ShapeDtypeStruct((tok, width), BF16),
        scratch_shapes=[
            pltpu.VMEM((width, cols), BF16),
            pltpu.VMEM((*dqkv.shape[:2], tok), BF16),
            pltpu.VMEM((cols, tok), BF16),
            pltpu.SemaphoreType.DMA((2,)),
        ],
        compiler_params=pltpu.CompilerParams(vmem_limit_bytes=60 << 20),
        cost_estimate=pl.CostEstimate(
            flops=2 * tok * width * cols, bytes_accessed=2 * width * cols, transcendentals=0
        ),
        name="input_rows",
    )(dqkv, w)


def heads_back_kernel(near_ref, d_ref, x_hbm, w_hbm, *refs, slots, step):
    count = len(slots)
    give_ref, keep_ref = refs[:2]
    out = refs[2 : 2 + count]
    x_scr, w_scr, d_scr, t_scr, y_scr, o_scr, in_sem, out_sem = refs[2 + count :]
    groups, depth = keep_ref.shape[1:3]
    tok, width = out[0].shape
    x_in = pltpu.make_async_copy(x_hbm, x_scr, in_sem.at[0])
    w_in = pltpu.make_async_copy(w_hbm, w_scr, in_sem.at[1])
    w_in.start()
    x_in.start()
    turned_rows(d_ref, d_scr, 0, d_scr.shape[1])
    t_scr[...] = d_scr[...].T
    w_in.wait()
    sent = []
    for n in range(width // step):
        part = slice(n * step, (n + 1) * step)
        o_scr[:, part] = mxu_nt(t_scr[...], w_scr[part, :]).astype(BF16)
        for i, slot in enumerate(slots):
            sent.append(
                pltpu.make_async_copy(
                    o_scr.at[slot * tok : (slot + 1) * tok, part],
                    out[i].at[:, part],
                    out_sem.at[n, i],
                )
            )
            sent[-1].start()
    x_in.wait()
    tile = 4 * depth
    for g in range(groups):
        y_scr[...] = mxu(d_scr[...], x_scr[:, g * tile : (g + 1) * tile]).astype(BF16).T
        for r in range(4):
            rows = pl.ds(pl.multiple_of((near_ref[0] ^ r) * depth, depth), depth)
            (give_ref if r % 2 else keep_ref)[r // 2, g] = y_scr[rows, :]
    for c in sent:
        c.wait()


def heads_back(near, dqkv, x, w, slots, tok):
    rows, width = x.shape
    cols = w.shape[1]
    depth = HD
    groups = width // (4 * depth)
    step = width // 4
    shape = jax.ShapeDtypeStruct((2, groups, depth, cols), BF16)
    out = pl.pallas_call(
        functools.partial(heads_back_kernel, slots=slots, step=step),
        in_specs=[pl.BlockSpec(memory_space=pltpu.SMEM), VMEM, ANY, ANY],
        out_specs=[VMEM, VMEM] + [ANY] * len(slots),
        out_shape=[shape, shape] + [jax.ShapeDtypeStruct((tok, width), BF16)] * len(slots),
        scratch_shapes=[
            pltpu.VMEM((rows, width), BF16),
            pltpu.VMEM((width, cols), BF16),
            pltpu.VMEM((cols, rows), BF16),
            pltpu.VMEM((rows, cols), BF16),
            pltpu.VMEM((4 * depth, cols), BF16),
            pltpu.VMEM((rows, width), BF16),
            pltpu.SemaphoreType.DMA((2,)),
            pltpu.SemaphoreType.DMA((width // step, len(slots))),
        ],
        compiler_params=pltpu.CompilerParams(vmem_limit_bytes=60 << 20),
        cost_estimate=pl.CostEstimate(
            flops=4 * rows * width * cols,
            bytes_accessed=2 * (2 * width * cols + rows * (2 * width + cols)),
            transcendentals=0,
        ),
        name="heads_back",
    )(near, dqkv, x, w)
    return out[:2], out[2:]


def mid_grad_kernel(
    own_ref, across_ref, ahead_ref, mid_ref, dy_ref, scale_ref, gain_ref, w_hbm, dmid_ref, low_ref, out_ref, w_scr, sem
):
    tiles = sem.shape[0]
    width = mid_ref.shape[1]
    rows = w_scr.shape[0] // tiles
    w_in = [
        pltpu.make_async_copy(w_hbm.at[i * rows : (i + 1) * rows], w_scr.at[i * rows : (i + 1) * rows], sem.at[i])
        for i in range(tiles)
    ]
    for c in w_in:
        c.start()
    dn = own_ref[...].astype(F32) + across_ref[...].astype(F32) + ahead_ref[...].astype(F32)
    mid, scale = mid_ref[...], scale_ref[...]
    scaled = gain_ref[...] * dn
    mean = jnp.sum(scaled * mid, axis=-1, keepdims=True) * (1.0 / width)
    dmid = dy_ref[...].astype(F32) + scale * scaled - mid * (scale * scale * scale * mean)
    dmid_ref[...] = dmid
    low = dmid.astype(BF16)
    low_ref[...] = low
    gain_term = jnp.sum(dn * mid * scale, axis=0, keepdims=True)
    high = gain_term.astype(BF16)
    rest = (gain_term - high.astype(F32)).astype(BF16)
    out_ref[:, HD:] = jnp.zeros((out_ref.shape[0], out_ref.shape[1] - HD, out_ref.shape[2]), BF16)
    for h in range(out_ref.shape[0]):
        at = slice(h * HD, (h + 1) * HD)
        out_ref[h, HD : HD + 1, : 2 * HD] = jnp.concatenate([high[:, at], rest[:, at]], axis=1)
    for i in range(tiles):
        w_in[i].wait()
        v = mxu_nt(w_scr[i * rows : (i + 1) * rows, :], low).astype(BF16)
        for j in range(rows // HD):
            out_ref[i * (rows // HD) + j, :HD] = v[j * HD : (j + 1) * HD]


def mid_grad(terms, mid, dy, scale, gain, w):
    tok, width = mid.shape
    owners = w.shape[0] // HD
    return pl.pallas_call(
        mid_grad_kernel,
        in_specs=[VMEM] * 7 + [ANY],
        out_specs=[VMEM] * 3,
        out_shape=[
            jax.ShapeDtypeStruct((tok, width), F32),
            jax.ShapeDtypeStruct((tok, width), BF16),
            jax.ShapeDtypeStruct((owners, HD + 16, tok), BF16),
        ],
        scratch_shapes=[pltpu.VMEM(w.shape, BF16), pltpu.SemaphoreType.DMA((4,))],
        compiler_params=pltpu.CompilerParams(vmem_limit_bytes=60 << 20),
        cost_estimate=pl.CostEstimate(
            flops=2 * tok * width * w.shape[0], bytes_accessed=2 * width * w.shape[0], transcendentals=0
        ),
        name="mid_grad",
    )(*terms, mid, dy, scale, gain, w)


FAR = ("ctx", "row")
NEAR = ("col", "core")


def swap(v, axis):
    return lax.ppermute(v, axis, [(0, 1), (1, 0)])


def shift(v):
    n = lax.axis_size("ctx")
    return lax.ppermute(v, "ctx", [(i, (i + 1) % n) for i in range(n)])


class Flow:
    def __init__(self, steps):
        self.steps = steps
        self.result = None
        self.pending = next(steps)

    def take(self, got):
        try:
            self.pending = self.steps.send(got)
        except StopIteration as end:
            self.pending, self.result = None, end.value

    def run_on(self):
        self.take(self.pending)


def stage(flows, values=(), then=None):
    got, values = lax.optimization_barrier(([f.pending for f in flows], values))
    if then is not None:
        then(values)
    for f, g in zip(flows, got, strict=True):
        f.take(g)
    return values


def spread(v, slots):
    slots[0, 0] = v
    n = lax.axis_size("ctx")
    for c in range(n - 1):
        slots[c + 1, 0], slots[c, 1] = yield shift(slots[c, 0]), swap(slots[c, 0], "row")
    slots[n - 1, 1] = yield swap(slots[n - 1, 0], "row")
    return slots


def spread_late(v, slots):
    slots[0, 0] = v
    n = lax.axis_size("ctx")
    slots[1, 0] = yield shift(v)
    for c in range(1, n - 2):
        slots[c + 1, 0], slots[c - 1, 1] = yield shift(slots[c, 0]), swap(slots[c - 1, 0], "row")
    slots[n - 1, 0], slots[n - 3, 1], slots[n - 2, 1] = yield (
        shift(slots[n - 2, 0]),
        swap(slots[n - 3, 0], "row"),
        swap(slots[n - 2, 0], "row"),
    )
    slots[n - 1, 1] = yield swap(slots[n - 1, 0], "row")
    return slots


def collect(terms, marks, early=False, open_end=False):
    n = lax.axis_size("ctx")
    across = yield swap(terms[1, 1], "row")
    total = terms[1, 0].astype(F32) + across.astype(F32)
    for c in [*range(2, n), 0]:
        send = total.astype(BF16)
        marks.append(send)
        if early and c == 2:
            ahead, across, last = yield (
                shift(send),
                swap(after(terms[c, 1], send), "row"),
                swap(after(terms[0, 1], send), "row"),
            )
        elif early and c == 0:
            ahead, across = (yield shift(send)), last
        else:
            ahead, across = yield shift(send), swap(after(terms[c, 1], send), "row")
        if open_end and c == 0:
            return terms[0, 0], across, ahead
        total = terms[c, 0].astype(F32) + across.astype(F32) + ahead.astype(F32)
    return total


def reduce_near(send, keep):
    got = yield swap(send, "core")
    (give,) = yield for_column(keep, got, 1)
    across = yield swap(give, "col")
    return keep, got, [across]


def for_column(keep, got, pieces):
    rows = keep.shape[1] // pieces
    return [
        (keep[0, p : p + rows].astype(F32) + got[0, p : p + rows].astype(F32)).astype(BF16)
        for p in range(0, keep.shape[1], rows)
    ]


def add_terms(keep, got, across):
    return keep[1].astype(F32) + got[1].astype(F32) + jnp.concatenate(across, axis=0).astype(F32)


def after(v, first):
    return lax.optimization_barrier((v, first))[0]


def beside(v, tok):
    return jnp.pad(v.reshape(*v.shape[:-1], 1, -1), [(0, 0)] * (v.ndim - 1) + [(0, 15), (0, tok - v.shape[-1])])


def by_side(index, mine, theirs):
    return jnp.where(index == 0, mine, theirs), jnp.where(index == 0, theirs, mine)


def to_near(v, col_at, core_at):
    keep, give = by_side(col_at, v[0], v[1])
    got = yield swap(give, "col")
    both = jnp.stack(by_side(col_at, keep, got))
    keep, give = by_side(core_at, both[:, 0], both[:, 1])
    got = yield swap(give, "core")
    return jnp.stack(by_side(core_at, keep, got), axis=1)


def sum_near(give, keep):
    got = yield swap(give, "core")
    other = (keep[1].astype(F32) + got[1].astype(F32)).astype(BF16)
    across = yield swap(other, "col")
    return keep[0].astype(F32) + got[0].astype(F32) + across.astype(F32)


def gather_heads(send):
    mine = yield lax.all_to_all(send, FAR, split_axis=0, concat_axis=0, tiled=True)
    part = mine.shape[0] // 2
    upper, mine_two = yield swap(mine[:part], "col"), swap(mine, "core")
    lower = yield swap(mine[part:], "col")
    other = jnp.concatenate([upper, lower], axis=0)
    other_two = yield swap(other, "core")
    return mine, mine_two, other, other_two


def per_device_split(
    tokens,
    pair_index,
    gain_attn,
    w_query,
    w_key,
    w_value,
    w_out,
    gain_ffn,
    w_gate,
    w_up,
    w_down,
    cotangent,
):
    n_ctx = lax.axis_size("ctx")
    near = lax.axis_size("col") * lax.axis_size("core")
    far = 2 * n_ctx
    tok, width = tokens.shape
    own_in = w_query.shape[0]
    ctx_at, row_at, col_at, core_at = (lax.axis_index(a) for a in ("ctx", "row", "col", "core"))
    near_at = col_at * lax.axis_size("core") + core_at
    blk = near * tok
    rows_here = far * tok
    group = near * HD

    slots = jnp.arange(far, dtype=jnp.int32)
    ctxs = jnp.arange(n_ctx, dtype=jnp.int32)

    def block_of(ctx, row):
        pair = jnp.sum(jnp.where(ctx[:, None] == ctxs[None, :], pair_index[None, :], 0), axis=1)
        return jnp.where(row == 0, pair, far - 1 - pair)

    def place_of_block(block):
        return jnp.sum(jnp.where(block[None, :] == slots[:, None], slots[None, :], 0), axis=1)

    slot_block = block_of((ctx_at - slots % n_ctx + n_ctx) % n_ctx, row_at ^ (slots // n_ctx))
    places = jnp.stack([place_of_block(slot_block), place_of_block(block_of(slots // 2, slots % 2))])
    freq = jnp.exp(jnp.arange(HD // 2, dtype=F32) * (-2.0 * math.log(THETA) / HD))
    token_places = (
        slot_block[:, None] * blk + near_at * tok + jnp.arange(tok, dtype=jnp.int32)[None, :]
    ).reshape(rows_here)
    angle = freq[:, None] * token_places.astype(F32)[None, :]
    cosine, sine = jnp.cos(angle), jnp.sin(angle)
    seq_angle = freq[:, None] * jnp.arange(far * blk, dtype=jnp.int32).astype(F32)[None, :]
    seq_cos, seq_sin = jnp.cos(seq_angle), jnp.sin(seq_angle)

    gain_one = gain_attn.astype(F32)[:, None]
    send = jnp.concatenate(
        [
            (w.astype(F32) * gain_one).astype(BF16).reshape(own_in, far, group)
            for w in (w_query, w_key, w_value)
        ],
        axis=2,
    ).transpose(1, 0, 2)
    x32 = tokens.astype(F32)
    scale_one = lax.rsqrt(jnp.mean(x32 * x32, axis=-1, keepdims=True) + EPS)
    gate_w = lax.all_gather(w_gate, NEAR, axis=0, tiled=True)

    one_flow = Flow(spread((x32 * scale_one).astype(BF16), {}))
    heads_flow = Flow(gather_heads(send))
    w_out = stage([one_flow, heads_flow], w_out)
    out_w = lax.all_gather(w_out, FAR + NEAR, axis=0, tiled=True)
    for _ in range(n_ctx - 3):
        cosine, sine = stage([one_flow, heads_flow], (cosine, sine))
    dy_low = stage([one_flow, heads_flow], cotangent)
    dy_by = {}
    dy_flow = Flow(spread_late(dy_low, dy_by))
    w_up = stage([one_flow, heads_flow], w_up)
    dy_flow.run_on()
    up_w = lax.all_gather(w_up, NEAR, axis=0, tiled=True)
    slot_names = [(c, r) for r in range(2) for c in range(n_ctx)]
    qkv, rows_one, w_heads = qkv_of(
        near_at.reshape(1),
        [one_flow.result[k] for k in slot_names],
        heads_flow.result,
        cosine,
        sine,
    )
    qkv_head, gate_w, seq_cos, seq_sin = stage(
        [dy_flow],
        (
            lax.all_to_all(qkv, NEAR, split_axis=0, concat_axis=0, tiled=True),
            gate_w,
            seq_cos,
            seq_sin,
        ),
    )
    down_w = lax.all_gather(after(w_down, qkv_head), NEAR, axis=0, tiled=True)
    (attn_head, o32, lse, seq), out_w = stage(
        [dy_flow], (attn_fwd(places, qkv_head, beside(gain_ffn, tok), far), out_w)
    )
    attn, up_w = stage(
        [dy_flow],
        (lax.all_to_all(attn_head, FAR + NEAR, split_axis=0, concat_axis=0, tiled=True), up_w),
    )
    gain_two = attn[:, HD, :own_in].reshape(1, width).astype(F32)
    attn_all = attn[:, :HD]
    attn = attn_all.reshape(width, tok)

    mid = x32 + jnp.einsum("et,ed->td", attn, out_w, preferred_element_type=F32)
    scale_two = lax.rsqrt(jnp.mean(mid * mid, axis=-1, keepdims=True) + EPS)
    normed_two = (mid * scale_two * gain_two).astype(BF16)
    side_flow = Flow(
        to_near(attn_all.reshape(far, 2, 2, HD, tok).transpose(1, 2, 0, 3, 4), col_at, core_at)
    )

    two, dn_by, br_by, kept = {}, {}, {}, []
    two_flow = Flow(spread(normed_two, two))

    def feed(cs, first=()):
        names = [(c, r) for c in cs for r in range(2)]
        rows = after([two[k] for k in names], first)
        dn, br, lefts = ffn(rows, [dy_by[k] for k in names], gate_w, up_w, down_w)
        return dict(zip(names, dn, strict=True)), dict(zip(names, br, strict=True)), lefts

    def fed(results):
        dn, br, lefts = results
        dn_by.update(dn)
        br_by.update(br)
        kept.append(lefts)

    stage([two_flow, side_flow])
    stage([two_flow, side_flow], feed([0]), fed)
    for c in range(1, n_ctx - 2):
        stage([two_flow], feed([c]), fed)
    marks = []
    dn_flow = Flow(collect(dn_by, marks, open_end=True))
    stage([two_flow, dn_flow], feed([n_ctx - 2]), fed)
    last = feed([n_ctx - 1], marks[-1])
    stage([dn_flow], last, fed)
    names = [(c, r) for c in range(n_ctx) for r in range(2)]
    two_rows, dy_rows = [two[k] for k in names], [dy_by[k] for k in names]
    tiles = near_at ^ jnp.array([3, 1, 2, 0], jnp.int32)
    lefts = [[k[i] for k in kept] for i in range(3)]
    for _ in range(n_ctx - 4):
        stage([dn_flow])
    gate_terms = outer(tiles, *after((lefts[1], two_rows), marks[-1]))
    gate_flow = Flow(reduce_near(*stage([dn_flow], gate_terms)))
    up_terms = outer(tiles, *after((lefts[2], two_rows), marks[-1]))
    up_terms, br_by = stage([dn_flow, gate_flow], (up_terms, br_by))
    up_send, up_keep = up_terms
    dmid, dmid_low, dattn = mid_grad(dn_flow.result, mid, cotangent, scale_two, gain_two, out_w)
    dmid_near = lax.all_gather(dmid_low, NEAR, axis=0, tiled=True)
    br_marks = []
    br_flow = Flow(collect(br_by, br_marks, early=True, open_end=True))
    down_terms = outer(tiles, *after((lefts[0], dy_rows), dattn))
    gate_flow.pending = after(gate_flow.pending, dattn)
    attn_side = side_flow.result.transpose(2, 3, 0, 1, 4).reshape(far, HD, blk)
    out_term = jnp.einsum(
        "gft,td->gfd", after(attn_side, dattn), dmid_near, preferred_element_type=F32
    )
    dattn_head, down_terms, out_term, up_got = stage(
        [gate_flow, br_flow],
        (
            lax.all_to_all(dattn, FAR + NEAR, split_axis=0, concat_axis=0, tiled=True),
            down_terms,
            out_term.astype(BF16),
            swap(up_send, "core"),
        ),
    )
    out_grad = lax.psum_scatter(
        out_term.reshape(far * HD, width), FAR, scatter_dimension=0, tiled=True
    )
    down_send, down_keep = down_terms
    gain_parts = dattn_head[:, HD, : 2 * own_in].astype(F32)
    dqkv_head, down_got = stage(
        [gate_flow, br_flow],
        (
            attn_bwd(places, seq, o32, lse, dattn_head, seq_cos, seq_sin, far),
            swap(down_send, "core"),
        ),
    )
    exchange = lax.all_to_all(dqkv_head, NEAR, split_axis=0, concat_axis=0, tiled=True)
    up_give = for_column(*after((up_keep, up_got), br_marks[-1]), 2)
    (down_keep, down_got) = after((down_keep, down_got), br_marks[-1])
    dqkv, up_give, down_give = stage(
        [br_flow], (exchange, up_give, for_column(down_keep, down_got, 1)[0])
    )
    dx = {(1, 1): input_rows(dqkv, w_heads, slot_names.index((1, 1)), tok)}
    dx_flow = Flow(collect(dx, marks))
    up_first, up_second = up_give
    rest = [i for i in range(far) if slot_names[i] != (1, 1)]

    def add_rows(values):
        dx.update({slot_names[i]: v for i, v in zip(rest, values[1], strict=True)})

    heads_terms, _, up_first = stage(
        [dx_flow, br_flow],
        (*heads_back(near_at.reshape(1), after(dqkv, dx[1, 1]), rows_one, w_heads, rest, tok), swap(up_first, "col")),
        add_rows,
    )
    heads_flow = Flow(sum_near(*heads_terms))
    stage([heads_flow])
    gate_terms, out_grad, up_second = stage(
        [dx_flow, heads_flow], (gate_flow.result, out_grad, up_second)
    )
    back = lax.all_to_all(
        heads_flow.result.astype(BF16), FAR, split_axis=0, concat_axis=0, tiled=True
    )
    gate_terms, down_give, up_second, branch = stage(
        [dx_flow], (gate_terms, down_give, swap(up_second, "col"), br_flow.result)
    )
    up_terms = up_keep, up_got, [up_first, up_second]
    gate_terms, up_terms, branch = after((gate_terms, up_terms, branch), marks[-1])
    gate_grad, up_grad = add_terms(*gate_terms), add_terms(*up_terms)
    back, down_across = stage([dx_flow], (back, swap(down_give, "col")))
    down_grad = add_terms(down_keep, down_got, [down_across])
    scaled_one = dx_flow.result
    input_grad = (
        dmid
        + scale_one * scaled_one
        - x32 * scale_one**3 * jnp.mean(scaled_one * x32, axis=-1, keepdims=True)
    )
    back = back.astype(F32)
    raw = [
        back[:, :, i * group : (i + 1) * group].transpose(1, 0, 2).reshape(own_in, -1)
        for i in range(3)
    ]
    gain_attn_grad = sum(
        jnp.sum(w.astype(F32) * g, axis=1)
        for w, g in zip((w_query, w_key, w_value), raw, strict=True)
    )
    query_grad, key_grad, value_grad = (g * gain_one for g in raw)
    gain_ffn_grad = jnp.sum(gain_parts[:, :own_in] + gain_parts[:, own_in:], axis=0)
    return (
        (mid + sum(v.astype(F32) for v in branch)).astype(BF16),
        input_grad,
        gain_attn_grad,
        query_grad,
        key_grad,
        value_grad,
        out_grad.astype(F32),
        gain_ffn_grad,
        gate_grad,
        up_grad,
        down_grad,
    )


def solution(mesh):
    n_ctx, n_fsdp = mesh.shape["ctx"], mesh.shape["fsdp"]

    def step(*args):
        if n_fsdp == 8 and n_ctx == 4 and n_ctx * n_fsdp * HD == args[3].shape[1]:
            body, axes = per_device_split, FAR + NEAR
            over = Mesh(np.asarray(mesh.devices).reshape(n_ctx, 2, 2, 2), axes)
        else:
            body, axes, over = per_device_any, ("ctx", "fsdp"), mesh
        rows, line = P(axes, None), P(axes)
        return jax.shard_map(
            body,
            mesh=over,
            in_specs=(rows, P(), line, rows, rows, rows, rows, line, rows, rows, rows, rows),
            out_specs=(rows, rows, line, rows, rows, rows, rows, line, rows, rows, rows),
            check_vma=False,
        )(*args)

    return step
```

```python
import functools
import math

import jax
import jax.numpy as jnp
import numpy as np
from jax import lax
from jax.experimental import pallas as pl
from jax.experimental.pallas import tpu as pltpu
from jax.sharding import Mesh
from jax.sharding import PartitionSpec as P

HD = 64


EPS = 1e-05
THETA = 130000.0


def place_of(rows, pair_index, n_groups, blk):
    group = rows // (2 * blk)
    within = rows % (2 * blk)
    match = group[:, None] == jnp.arange(n_groups, dtype=jnp.int32)[None, :]
    pair = jnp.sum(jnp.where(match, pair_index[None, :], 0), axis=1)
    block = jnp.where(within < blk, pair, 2 * n_groups - 1 - pair)
    return block * blk + within % blk


def tables(places, head_dim):
    freq = jnp.exp(
        jnp.arange(head_dim // 2, dtype=jnp.float32) * (-2.0 * math.log(THETA) / head_dim)
    )
    angle = places.astype(jnp.float32)[:, None] * freq[None, :]
    return (jnp.cos(angle), jnp.sin(angle))


def rotate(flat, cosine, sine, head_dim):
    rows = flat.shape[0]
    split = flat.reshape(rows, -1, head_dim)
    half = head_dim // 2
    first = split[..., :half]
    second = split[..., half:]
    cos_b = cosine[:, None, :]
    sin_b = sine[:, None, :]
    out = jnp.concatenate([first * cos_b - second * sin_b, second * cos_b + first * sin_b], axis=-1)
    return out.reshape(rows, -1)


def silu_parts(gate):
    sig = jax.nn.sigmoid(gate)
    return (gate * sig, sig * (1.0 + gate * (1.0 - sig)))


def rows_by(left, right):
    return jnp.einsum("td,fd->tf", left, right, preferred_element_type=jnp.float32)


def outer_sum(left, right):
    return jnp.einsum("tf,td->fd", left, right, preferred_element_type=jnp.float32)


def per_device_any(
    tokens,
    pair_index,
    gain_attn,
    w_query,
    w_key,
    w_value,
    w_out,
    gain_ffn,
    w_gate,
    w_up,
    w_down,
    cotangent,
):
    f32 = jnp.float32
    bf16 = jnp.bfloat16
    n_ctx = lax.axis_size("ctx")
    n_fsdp = lax.axis_size("fsdp")
    tok = tokens.shape[0]
    group_rows = tok * n_fsdp
    blk = group_rows // 2
    total = group_rows * n_ctx
    ctx_index = lax.axis_index("ctx")
    fsdp_index = lax.axis_index("fsdp")
    local_rows = (ctx_index * n_fsdp + fsdp_index) * tok + jnp.arange(tok, dtype=jnp.int32)
    local_places = place_of(local_rows, pair_index, n_ctx, blk)
    group_places = place_of(
        ctx_index * group_rows + jnp.arange(group_rows, dtype=jnp.int32), pair_index, n_ctx, blk
    )
    key_places = place_of(jnp.arange(total, dtype=jnp.int32), pair_index, n_ctx, blk)
    group_cos, group_sin = tables(group_places, HD)
    query_full, key_full, value_full, out_full, gain_one, gain_two = (
        lax.all_gather(w_query, ("ctx", "fsdp"), axis=0, tiled=True),
        lax.all_gather(w_key, ("ctx", "fsdp"), axis=0, tiled=True),
        lax.all_gather(w_value, ("ctx", "fsdp"), axis=0, tiled=True),
        lax.all_gather(w_out, ("ctx", "fsdp"), axis=0, tiled=True),
        lax.all_gather(gain_attn, ("ctx", "fsdp"), axis=0, tiled=True),
        lax.all_gather(gain_ffn, ("ctx", "fsdp"), axis=0, tiled=True),
    )
    gain_one = gain_one.astype(f32)
    gain_two = gain_two.astype(f32)
    x32 = tokens.astype(f32)
    scale_one = lax.rsqrt(jnp.mean(x32 * x32, axis=-1, keepdims=True) + EPS)
    normed_one = (x32 * scale_one * gain_one).astype(bf16)
    cosine, sine = tables(local_places, HD)
    query = rotate(
        jnp.dot(normed_one, query_full, preferred_element_type=f32), cosine, sine, HD
    ).astype(bf16)
    key = rotate(
        jnp.dot(normed_one, key_full, preferred_element_type=f32), cosine, sine, HD
    ).astype(bf16)
    value = jnp.dot(normed_one, value_full, preferred_element_type=f32).astype(bf16)
    query_heads, key_heads, value_heads = (
        lax.all_to_all(query, "fsdp", split_axis=1, concat_axis=0, tiled=True),
        lax.all_to_all(key, "fsdp", split_axis=1, concat_axis=0, tiled=True),
        lax.all_to_all(value, "fsdp", split_axis=1, concat_axis=0, tiled=True),
    )
    key_all, value_all = (
        lax.all_gather(key_heads, "ctx", axis=0, tiled=True),
        lax.all_gather(value_heads, "ctx", axis=0, tiled=True),
    )
    local_width = query_heads.shape[1]
    heads_here = local_width // HD
    scale = HD ** (-0.5)
    query_parts = query_heads.reshape(2, blk, heads_here, HD)
    query_place_tiles = group_places.reshape(2, blk)
    key_tiles = key_all.reshape(2 * n_ctx, blk, heads_here, HD)
    value_tiles = value_all.reshape(2 * n_ctx, blk, heads_here, HD)
    key_place_tiles = key_places.reshape(2 * n_ctx, blk)

    def tile_scores(slot, keys, k_place):
        raw = (
            jnp.einsum("qhd,khd->hqk", query_parts[slot], keys, preferred_element_type=f32) * scale
        )
        keep = k_place[None, None, :] <= query_place_tiles[slot][None, :, None]
        return jnp.where(keep, raw, -1e30)

    def is_live(slot, k_place):
        return jnp.min(k_place) <= jnp.max(query_place_tiles[slot])

    def first_pass(carry, tile):
        keys, k_place = tile
        highs, totals = carry
        new_highs = []
        new_totals = []
        for slot in range(2):

            def first_update(high, summed):
                masked = tile_scores(slot, keys, k_place)
                fresh = jnp.maximum(high, jnp.max(masked, axis=-1))
                summed = summed * jnp.exp(high - fresh) + jnp.sum(
                    jnp.exp(masked - fresh[..., None]), axis=-1
                )
                return (fresh, summed)

            def first_leave(high, summed):
                return (high, summed)

            high, summed = lax.cond(
                is_live(slot, k_place), first_update, first_leave, highs[slot], totals[slot]
            )
            new_highs.append(high)
            new_totals.append(summed)
        return ((jnp.stack(new_highs), jnp.stack(new_totals)), None)

    start_high = jnp.full((2, heads_here, blk), -1e30, f32)
    start_total = jnp.zeros((2, heads_here, blk), f32)
    (highs, totals), unused = lax.scan(
        first_pass, (start_high, start_total), (key_tiles, key_place_tiles)
    )
    log_total = highs + jnp.log(totals)

    def second_pass(carry, tile):
        keys, values, k_place = tile
        outs = []
        for slot in range(2):

            def second_update(acc):
                masked = tile_scores(slot, keys, k_place)
                prob_low = jnp.exp(masked - log_total[slot][..., None]).astype(bf16)
                return acc + jnp.einsum(
                    "hqk,khd->qhd", prob_low, values, preferred_element_type=f32
                )

            def second_leave(acc):
                return acc

            outs.append(lax.cond(is_live(slot, k_place), second_update, second_leave, carry[slot]))
        return (jnp.stack(outs), None)

    acc_start = jnp.zeros((2, blk, heads_here, HD), f32)
    attn_acc, unused = lax.scan(second_pass, acc_start, (key_tiles, value_tiles, key_place_tiles))
    attn32 = attn_acc.reshape(group_rows, local_width)
    attn_tokens = lax.all_to_all(
        attn32.astype(bf16), "fsdp", split_axis=0, concat_axis=1, tiled=True
    )
    mid = x32 + jnp.dot(attn_tokens, out_full, preferred_element_type=f32)
    scale_two = lax.rsqrt(jnp.mean(mid * mid, axis=-1, keepdims=True) + EPS)
    normed_two = (mid * scale_two * gain_two).astype(bf16)
    dy = cotangent.astype(f32)
    dy_low = dy.astype(bf16)
    gate_local, up_local, down_local = (
        lax.all_gather(w_gate, "ctx", axis=0, tiled=True),
        lax.all_gather(w_up, "ctx", axis=0, tiled=True),
        lax.all_gather(w_down, "ctx", axis=0, tiled=True),
    )
    rows_all = lax.all_gather(normed_two, "fsdp", axis=0, tiled=True)
    gate_all = rows_by(rows_all, gate_local)
    up_all = rows_by(rows_all, up_local)
    silu_all, unused_slope = silu_parts(gate_all)
    hidden_all = (silu_all * up_all).astype(bf16)
    branch = lax.psum_scatter(
        jnp.dot(hidden_all, down_local, preferred_element_type=f32).astype(jnp.bfloat16),
        "fsdp",
        scatter_dimension=0,
        tiled=True,
    ).astype(jnp.float32)
    block_out = (mid + branch).astype(bf16)
    grad_rows_all = lax.all_gather(dy_low, "fsdp", axis=0, tiled=True)
    dhidden = rows_by(grad_rows_all, down_local)
    silu_val, slope = silu_parts(gate_all)
    dgate = (dhidden * up_all * slope).astype(bf16)
    dup = (dhidden * silu_val).astype(bf16)
    gate_term = outer_sum(dgate, rows_all)
    up_term = outer_sum(dup, rows_all)
    down_term = outer_sum(hidden_all, grad_rows_all)
    gate_grad, up_grad, down_grad = (
        lax.psum_scatter(
            gate_term.astype(jnp.bfloat16), "ctx", scatter_dimension=0, tiled=True
        ).astype(jnp.float32),
        lax.psum_scatter(
            up_term.astype(jnp.bfloat16), "ctx", scatter_dimension=0, tiled=True
        ).astype(jnp.float32),
        lax.psum_scatter(
            down_term.astype(jnp.bfloat16), "ctx", scatter_dimension=0, tiled=True
        ).astype(jnp.float32),
    )
    dnormed_two = lax.psum_scatter(
        (
            jnp.dot(dgate, gate_local, preferred_element_type=f32)
            + jnp.dot(dup, up_local, preferred_element_type=f32)
        ).astype(jnp.bfloat16),
        "fsdp",
        scatter_dimension=0,
        tiled=True,
    ).astype(jnp.float32)
    gain_two_term = jnp.sum(dnormed_two * mid * scale_two, axis=0)
    scaled_two = gain_two * dnormed_two
    dmid = (
        dy
        + scale_two * scaled_two
        - mid * scale_two**3 * jnp.mean(scaled_two * mid, axis=-1, keepdims=True)
    )
    dmid_low = dmid.astype(bf16)
    out_term = jnp.einsum("td,te->de", attn_tokens, dmid_low, preferred_element_type=f32)
    dattn = jnp.einsum("te,de->td", dmid_low, out_full, preferred_element_type=f32).astype(bf16)
    dattn_heads = lax.all_to_all(dattn, "fsdp", split_axis=1, concat_axis=0, tiled=True)
    delta = jnp.sum((dattn_heads.astype(f32) * attn32).reshape(group_rows, heads_here, HD), axis=-1)
    delta_tiles = delta.reshape(2, blk, heads_here).transpose(0, 2, 1)
    grad_parts = dattn_heads.reshape(2, blk, heads_here, HD)

    def back_pass(carry, tile):
        keys, values, k_place = tile
        key_acc = jnp.zeros((blk, heads_here, HD), f32)
        value_acc = jnp.zeros((blk, heads_here, HD), f32)
        new_query = []
        for slot in range(2):

            def back_update(q_acc, k_acc, v_acc):
                masked = tile_scores(slot, keys, k_place)
                prob = jnp.exp(masked - log_total[slot][..., None])
                prob_low = prob.astype(bf16)
                dprob = jnp.einsum(
                    "qhd,khd->hqk", grad_parts[slot], values, preferred_element_type=f32
                )
                dscore = (prob * (dprob - delta_tiles[slot][..., None])).astype(bf16)
                q_acc = (
                    q_acc
                    + jnp.einsum("hqk,khd->qhd", dscore, keys, preferred_element_type=f32) * scale
                )
                k_acc = (
                    k_acc
                    + jnp.einsum(
                        "hqk,qhd->khd", dscore, query_parts[slot], preferred_element_type=f32
                    )
                    * scale
                )
                v_acc = v_acc + jnp.einsum(
                    "hqk,qhd->khd", prob_low, grad_parts[slot], preferred_element_type=f32
                )
                return (q_acc, k_acc, v_acc)

            def back_leave(q_acc, k_acc, v_acc):
                return (q_acc, k_acc, v_acc)

            q_acc, key_acc, value_acc = lax.cond(
                is_live(slot, k_place), back_update, back_leave, carry[slot], key_acc, value_acc
            )
            new_query.append(q_acc)
        return (jnp.stack(new_query), (key_acc, value_acc))

    dquery_start = jnp.zeros((2, blk, heads_here, HD), f32)
    dquery_acc, (dkey_tiles, dvalue_tiles) = lax.scan(
        back_pass, dquery_start, (key_tiles, value_tiles, key_place_tiles)
    )
    dkey_all = dkey_tiles.reshape(total, local_width)
    dvalue_all = dvalue_tiles.reshape(total, local_width)
    dkey_own, dvalue_own = (
        lax.psum_scatter(
            dkey_all.astype(jnp.bfloat16), "ctx", scatter_dimension=0, tiled=True
        ).astype(jnp.float32),
        lax.psum_scatter(
            dvalue_all.astype(jnp.bfloat16), "ctx", scatter_dimension=0, tiled=True
        ).astype(jnp.float32),
    )
    dquery_low = rotate(
        dquery_acc.reshape(group_rows, local_width), group_cos, -group_sin, HD
    ).astype(bf16)
    dkey_low = rotate(dkey_own, group_cos, -group_sin, HD).astype(bf16)
    dvalue_low = dvalue_own.astype(bf16)
    dquery_tok, dkey_tok, dvalue_tok = (
        lax.all_to_all(dquery_low, "fsdp", split_axis=0, concat_axis=1, tiled=True),
        lax.all_to_all(dkey_low, "fsdp", split_axis=0, concat_axis=1, tiled=True),
        lax.all_to_all(dvalue_low, "fsdp", split_axis=0, concat_axis=1, tiled=True),
    )
    dnormed_one = (
        jnp.einsum("te,de->td", dquery_tok, query_full, preferred_element_type=f32)
        + jnp.einsum("te,de->td", dkey_tok, key_full, preferred_element_type=f32)
        + jnp.einsum("te,de->td", dvalue_tok, value_full, preferred_element_type=f32)
    )
    query_term = jnp.einsum("td,te->de", normed_one, dquery_tok, preferred_element_type=f32)
    key_term = jnp.einsum("td,te->de", normed_one, dkey_tok, preferred_element_type=f32)
    value_term = jnp.einsum("td,te->de", normed_one, dvalue_tok, preferred_element_type=f32)
    gain_one_term = jnp.sum(dnormed_one * x32 * scale_one, axis=0)
    scaled_one = gain_one * dnormed_one
    input_grad = (
        dmid
        + scale_one * scaled_one
        - x32 * scale_one**3 * jnp.mean(scaled_one * x32, axis=-1, keepdims=True)
    )
    query_grad, key_grad, value_grad, out_grad, gain_attn_grad, gain_ffn_grad = (
        lax.psum_scatter(query_term, ("ctx", "fsdp"), scatter_dimension=0, tiled=True),
        lax.psum_scatter(key_term, ("ctx", "fsdp"), scatter_dimension=0, tiled=True),
        lax.psum_scatter(value_term, ("ctx", "fsdp"), scatter_dimension=0, tiled=True),
        lax.psum_scatter(out_term, ("ctx", "fsdp"), scatter_dimension=0, tiled=True),
        lax.psum_scatter(gain_one_term, ("ctx", "fsdp"), scatter_dimension=0, tiled=True),
        lax.psum_scatter(gain_two_term, ("ctx", "fsdp"), scatter_dimension=0, tiled=True),
    )
    return (
        block_out,
        input_grad,
        gain_attn_grad,
        query_grad,
        key_grad,
        value_grad,
        out_grad,
        gain_ffn_grad,
        gate_grad,
        up_grad,
        down_grad,
    )


BF16 = jnp.bfloat16
F32 = jnp.float32
LOG2E = math.log2(math.e)
VMEM = pl.BlockSpec(memory_space=pltpu.VMEM)
ANY = pl.BlockSpec(memory_space=pl.ANY)


def mxu(a, b):
    return jnp.dot(a, b, preferred_element_type=F32)


def causal(blk):
    row = lax.broadcasted_iota(jnp.int32, (blk, blk), 0)
    col = lax.broadcasted_iota(jnp.int32, (blk, blk), 1)
    return row <= col


def attn_fwd_kernel(
    place_ref,
    qkv_ref,
    extra_ref,
    out_ref,
    o32_hbm,
    lse_ref,
    seq_hbm,
    seq_ref,
    o32_ref,
    seq_sem,
    o32_sem,
    k_scr,
    m_scr,
    l_scr,
    acc_scr,
    *,
    blocks,
    width,
):
    pieces = qkv_ref.shape[0]
    blk = pieces * width
    coef = LOG2E * HD**-0.5
    for s in range(blocks):
        at = pl.multiple_of(place_ref[0, s] * width, width)
        for j in range(pieces):
            lo = s * blk + j * width
            piece = qkv_ref[j, :, pl.ds(at, width)]
            seq_ref[:, lo : lo + width] = piece
            k_scr[lo : lo + width, :] = piece[HD : 2 * HD].T

    leaving = [pltpu.make_async_copy(seq_ref, seq_hbm, seq_sem)]
    leaving[0].start()

    def tile(kb, q_t, masked, wide=1):
        keys = pl.ds(pl.multiple_of(kb * blk, blk), wide * blk)
        score = mxu(k_scr[keys, :], q_t) * coef
        if masked:
            score = jnp.where(causal(blk), score, -1e30)
        old = m_scr[...]
        new = jnp.maximum(old, jnp.max(score, axis=0, keepdims=True))
        p = jnp.exp2(score - new)
        fade = jnp.exp2(old - new)
        m_scr[...] = new
        l_scr[...] = l_scr[...] * fade + jnp.sum(p, axis=0, keepdims=True)
        acc_scr[...] = acc_scr[...] * fade + mxu(seq_ref[2 * HD :, keys], p.astype(BF16))

    for qb in range(blocks):
        lo = qb * blk
        q_t = seq_ref[:HD, lo : lo + blk]
        m_scr[...] = jnp.full_like(m_scr, -1e30)
        l_scr[...] = jnp.zeros_like(l_scr)
        acc_scr[...] = jnp.zeros_like(acc_scr)
        tile(qb, q_t, True)
        kb = 0
        while kb < qb:
            wide = min(4, qb - kb)
            tile(kb, q_t, False, wide)
            kb += wide

        o = acc_scr[...] / l_scr[...]
        o32_ref[:, lo : lo + blk] = o
        leaving.append(
            pltpu.make_async_copy(
                o32_ref.at[:, lo : lo + blk], o32_hbm.at[:, lo : lo + blk], o32_sem.at[qb]
            )
        )
        leaving[-1].start()
        lse_ref[:, lo : lo + blk] = m_scr[...] + jnp.log2(l_scr[...])
        low = o.astype(BF16)
        for j in range(pieces):
            owner = place_ref[1, qb] * pieces + j
            out_ref[owner, :HD] = low[:, j * width : (j + 1) * width]
            out_ref[owner, HD:] = extra_ref[...]
    for c in leaving:
        c.wait()


def attn_fwd(place, qkv, extra, blocks):
    pieces, _, cols = qkv.shape
    total = pieces * cols
    blk = total // blocks
    return pl.pallas_call(
        functools.partial(attn_fwd_kernel, blocks=blocks, width=cols // blocks),
        out_shape=(
            jax.ShapeDtypeStruct((blocks * pieces, HD + extra.shape[0], cols // blocks), BF16),
            jax.ShapeDtypeStruct((HD, total), F32),
            jax.ShapeDtypeStruct((1, total), F32),
            jax.ShapeDtypeStruct((3 * HD, total), BF16),
        ),
        in_specs=[pl.BlockSpec(memory_space=pltpu.SMEM), VMEM, VMEM],
        out_specs=(VMEM, ANY, VMEM, ANY),
        scratch_shapes=[
            pltpu.VMEM((3 * HD, total), BF16),
            pltpu.VMEM((HD, total), F32),
            pltpu.SemaphoreType.DMA,
            pltpu.SemaphoreType.DMA((blocks,)),
            pltpu.VMEM((total, HD), BF16),
            pltpu.VMEM((1, blk), F32),
            pltpu.VMEM((1, blk), F32),
            pltpu.VMEM((HD, blk), F32),
        ],
        compiler_params=pltpu.CompilerParams(vmem_limit_bytes=60 << 20),
        cost_estimate=pl.CostEstimate(
            flops=8 * total * total * HD, bytes_accessed=8 << 20, transcendentals=total * total // 2
        ),
        name="attn_fwd",
    )(place, qkv, extra)


def attn_bwd_kernel(
    place_ref,
    seq_hbm,
    o32_hbm,
    lse_ref,
    do_ref,
    cos_hbm,
    sin_hbm,
    out_ref,
    seq_ref,
    o32_ref,
    cos_ref,
    sin_ref,
    in_sem,
    q_scr,
    k_scr,
    v_scr,
    do_scr,
    dot_scr,
    delta_scr,
    dq_scr,
    dk_scr,
    dv_scr,
    *,
    blocks,
    width,
):
    pieces = out_ref.shape[0]
    blk = pieces * width
    scale = HD**-0.5
    coef = LOG2E * scale
    half = HD // 2
    arriving = [
        pltpu.make_async_copy(src, dst, in_sem.at[i])
        for i, (src, dst) in enumerate(
            ((seq_hbm, seq_ref), (o32_hbm, o32_ref), (cos_hbm, cos_ref), (sin_hbm, sin_ref))
        )
    ]
    for c in arriving:
        c.start()
    for c in arriving[:2]:
        c.wait()
    for s in range(blocks):
        for j in range(pieces):
            lo = s * blk + j * width
            piece = do_ref[place_ref[1, s] * pieces + j, :HD]
            dot_scr[:, lo : lo + width] = piece
            do_scr[lo : lo + width, :] = piece.T
            delta_scr[:, lo : lo + width] = jnp.sum(
                piece.astype(F32) * o32_ref[:, lo : lo + width], axis=0, keepdims=True
            )
            q_scr[lo : lo + width, :] = seq_ref[:HD, lo : lo + width].T
            k_scr[lo : lo + width, :] = seq_ref[HD : 2 * HD, lo : lo + width].T
            v_scr[lo : lo + width, :] = seq_ref[2 * HD :, lo : lo + width].T
    dq_scr[...] = jnp.zeros_like(dq_scr)
    for c in arriving[2:]:
        c.wait()

    def turn_back(v, s):
        c = cos_ref[:, s * blk : (s + 1) * blk]
        n = sin_ref[:, s * blk : (s + 1) * blk]
        a, b = v[:half], v[half:]
        return jnp.concatenate([a * c + b * n, b * c - a * n], axis=0).astype(BF16)

    def put(v, s, row):
        at = pl.multiple_of(place_ref[0, s] * width, width)
        for j in range(pieces):
            out_ref[j, row * HD : (row + 1) * HD, pl.ds(at, width)] = v[:, j * width : (j + 1) * width]

    for kb in range(blocks):
        lo = kb * blk
        k = k_scr[lo : lo + blk, :]
        v = v_scr[lo : lo + blk, :]
        k_t = seq_ref[HD : 2 * HD, lo : lo + blk]

        def tile(qb, masked, wide=1):
            here = pl.ds(pl.multiple_of(qb * blk, blk), wide * blk)
            p = jnp.exp2(mxu(k, seq_ref[:HD, here]) * coef - lse_ref[:, here])
            if masked:
                p = jnp.where(causal(blk), p, 0.0)
            dp = mxu(v, dot_scr[:, here])
            ds = (p * (dp - delta_scr[:, here])).astype(BF16)
            dq_scr[:, here] += mxu(k_t, ds)
            return mxu(ds, q_scr[here, :]), mxu(p.astype(BF16), do_scr[here, :])

        dk_scr[...], dv_scr[...] = tile(kb, True)

        def add_tile(qb, wide):
            dk, dv = tile(qb, False, wide)
            dk_scr[...] += dk
            dv_scr[...] += dv

        qb = kb + 1
        while qb < blocks:
            wide = min(2, blocks - qb)
            add_tile(qb, wide)
            qb += wide

        put(turn_back(dq_scr[:, lo : lo + blk] * scale, kb), kb, 0)
        put(turn_back((dk_scr[...] * scale).T, kb), kb, 1)
        put(dv_scr[...].T.astype(BF16), kb, 2)


def attn_bwd(place, seq, o32, lse, do, cos, sin, blocks):
    pieces, width = do.shape[0] // blocks, do.shape[2]
    cols, total, blk = blocks * width, seq.shape[1], pieces * width
    return pl.pallas_call(
        functools.partial(attn_bwd_kernel, blocks=blocks, width=width),
        out_shape=jax.ShapeDtypeStruct((pieces, 3 * HD, cols), BF16),
        in_specs=[pl.BlockSpec(memory_space=pltpu.SMEM), ANY, ANY, VMEM, VMEM, ANY, ANY],
        out_specs=VMEM,
        scratch_shapes=[
            pltpu.VMEM(seq.shape, BF16),
            pltpu.VMEM(o32.shape, F32),
            pltpu.VMEM(cos.shape, F32),
            pltpu.VMEM(sin.shape, F32),
            pltpu.SemaphoreType.DMA((4,)),
        ]
        + [pltpu.VMEM((total, HD), BF16)] * 4
        + [
            pltpu.VMEM((HD, total), BF16),
            pltpu.VMEM((1, total), F32),
            pltpu.VMEM((HD, total), F32),
            pltpu.VMEM((blk, HD), F32),
            pltpu.VMEM((blk, HD), F32),
        ],
        compiler_params=pltpu.CompilerParams(vmem_limit_bytes=60 << 20),
        cost_estimate=pl.CostEstimate(
            flops=20 * total * total * HD, bytes_accessed=8 << 20, transcendentals=total * total // 2
        ),
        name="attn_bwd",
    )(place, seq, o32, lse, do, cos, sin)


def mxu_nt(a, b):
    return lax.dot_general(a, b, (((1,), (1,)), ((), ())), preferred_element_type=F32)


def mxu_tn(a, b):
    return lax.dot_general(a, b, (((0,), (0,)), ((), ())), preferred_element_type=F32)


def ffn_kernel(*refs, count, step):
    x, dy = refs[:count], refs[count : 2 * count]
    gate_hbm, rest_hbm = refs[2 * count : 2 * count + 2]
    refs = refs[2 * count + 2 :]
    dn, br, kept = refs[:count], refs[count : 2 * count], refs[2 * count : 2 * count + 3]
    (
        x_scr,
        dy_scr,
        gate_w,
        up_w,
        down_w,
        hid_scr,
        dgate_scr,
        dup_scr,
        act_scr,
        dn_scr,
        br_scr,
        in_sem,
        w_sem,
        out_sem,
        keep_sem,
    ) = refs[2 * count + 3 :]
    tok, width = x[0].shape
    hidden, parts = gate_w.shape[0], w_sem.shape[1]
    part = hidden // parts
    rows_in = [
        pltpu.make_async_copy(src[i], dst.at[i * tok : (i + 1) * tok], in_sem.at[k, i])
        for k, (src, dst) in enumerate(((x, x_scr), (dy, dy_scr)))
        for i in range(count)
    ]
    gate_in, up_in, down_in = (
        [
            pltpu.make_async_copy(
                src.at[at(j) * part : (at(j) + 1) * part],
                dst.at[j * part : (j + 1) * part],
                w_sem.at[i, j],
            )
            for j in range(parts)
        ]
        for i, (src, at, dst) in enumerate(
            (
                (gate_hbm, lambda j: j, gate_w),
                (rest_hbm, lambda j: 2 * j, up_w),
                (rest_hbm, lambda j: 2 * j + 1, down_w),
            )
        )
    )
    for c in rows_in[:count]:
        c.start()
    for pair in zip(gate_in, up_in, strict=True):
        for c in pair:
            c.start()
    for c in rows_in[count:] + down_in:
        c.start()
    for c in rows_in[:count]:
        c.wait()
    for lo, hi in ((0, parts // 2), (parts // 2, parts)):
        for c in gate_in[lo:hi] + up_in[lo:hi]:
            c.wait()
        here = slice(lo * part, hi * part)
        gate = mxu_nt(x_scr[...], gate_w[here, :])
        up = mxu_nt(x_scr[...], up_w[here, :])
        sig = jax.nn.sigmoid(gate)
        act = gate * sig
        hid_scr[:, here] = (act * up).astype(BF16)
        act_scr[:, here] = act
        dgate_scr[:, here] = up * (sig * (1.0 + gate * (1.0 - sig)))
    for c in rows_in[count:]:
        c.wait()
    for lo, hi in ((0, parts // 2), (parts // 2, parts)):
        for c in down_in[lo:hi]:
            c.wait()
        here = slice(lo * part, hi * part)
        dhidden = mxu_nt(dy_scr[...], down_w[here, :])
        dup_scr[1, :, here] = (dhidden * act_scr[:, here]).astype(BF16)
        dup_scr[0, :, here] = (dhidden * dgate_scr[:, here]).astype(BF16)
    keep = [
        pltpu.make_async_copy(src, dst, keep_sem.at[k])
        for k, (src, dst) in enumerate(zip((hid_scr, dup_scr.at[0], dup_scr.at[1]), kept))
    ]
    for c in keep:
        c.start()
    sent = []
    for n in range(width // step):
        part = slice(n * step, (n + 1) * step)
        total = mxu(dup_scr[0], gate_w[:, part]) + mxu(dup_scr[1], up_w[:, part])
        dn_scr[:, part] = total.astype(BF16)
        br_scr[:, part] = mxu(hid_scr[...], down_w[:, part]).astype(BF16)
        for i in range(count):
            rows = slice(i * tok, (i + 1) * tok)
            for k, (src, dst) in enumerate(((dn_scr, dn[i]), (br_scr, br[i]))):
                sent.append(pltpu.make_async_copy(src.at[rows, part], dst.at[:, part], out_sem.at[k, i, n]))
                sent[-1].start()
    for c in keep + sent:
        c.wait()


def ffn(x, dy, gate_w, rest_w, parts):
    count, (tok, width), hidden = len(x), x[0].shape, gate_w.shape[0]
    rows, step = count * tok, width // 4
    out = pl.pallas_call(
        functools.partial(ffn_kernel, count=count, step=step),
        in_specs=[ANY] * (2 * count + 2),
        out_specs=[ANY] * (2 * count + 3),
        out_shape=[jax.ShapeDtypeStruct((tok, width), BF16)] * (2 * count)
        + [jax.ShapeDtypeStruct((rows, hidden), BF16)] * 3,
        scratch_shapes=[pltpu.VMEM((rows, width), BF16)] * 2
        + [pltpu.VMEM((hidden, width), BF16)] * 3
        + [
            pltpu.VMEM((rows, hidden), BF16),
            pltpu.VMEM((rows, hidden), F32),
            pltpu.VMEM((2, rows, hidden), BF16),
            pltpu.VMEM((rows, hidden), F32),
            pltpu.VMEM((rows, width), BF16),
            pltpu.VMEM((rows, width), BF16),
            pltpu.SemaphoreType.DMA((2, count)),
            pltpu.SemaphoreType.DMA((3, parts)),
            pltpu.SemaphoreType.DMA((2, count, width // step)),
            pltpu.SemaphoreType.DMA((3,)),
        ],
        compiler_params=pltpu.CompilerParams(vmem_limit_bytes=60 << 20),
        cost_estimate=pl.CostEstimate(
            flops=12 * rows * hidden * width, bytes_accessed=6 * hidden * width + 16 * rows * width, transcendentals=rows * hidden
        ),
        name="ffn",
    )(*x, *dy, gate_w, rest_w)
    return out[:count], out[count : 2 * count], out[2 * count :]


def outer_kernel(*refs, lefts, rights):
    order = refs[0]
    left, right = refs[1 : 1 + lefts], refs[1 + lefts : 1 + lefts + rights]
    send, keep, l_scr, r_scr, l_sem, r_sem = refs[1 + lefts + rights :]
    i = pl.program_id(0)

    def into(parts, scr, sem):
        at, out = 0, []
        for k, part in enumerate(parts):
            out.append(pltpu.make_async_copy(part, scr.at[at : at + part.shape[0]], sem.at[k]))
            at += part.shape[0]
        return out

    @pl.when(i == 0)
    def _():
        copies = into(left, l_scr, l_sem) + into(right, r_scr, r_sem)
        for c in copies:
            c.start()
        for c in copies:
            c.wait()

    tile = send.shape[1]
    l = l_scr[:, pl.ds(pl.multiple_of(order[i] * tile, tile), tile)]
    v = mxu_tn(l, r_scr[...]).astype(BF16)

    @pl.when(i < 2)
    def _():
        send[0] = v

    @pl.when(i >= 2)
    def _():
        keep[0] = v


def outer(order, left, right):
    cols, width = left[0].shape[1], right[0].shape[1]
    rows = sum(p.shape[0] for p in left)
    tile = cols // 4
    return pl.pallas_call(
        functools.partial(outer_kernel, lefts=len(left), rights=len(right)),
        grid=(4,),
        in_specs=[pl.BlockSpec(memory_space=pltpu.SMEM)] + [ANY] * (len(left) + len(right)),
        out_specs=[
            pl.BlockSpec((1, tile, width), lambda i: (jnp.minimum(i, 1), 0, 0)),
            pl.BlockSpec((1, tile, width), lambda i: (jnp.maximum(i - 2, 0), 0, 0)),
        ],
        out_shape=[jax.ShapeDtypeStruct((2, tile, width), BF16)] * 2,
        scratch_shapes=[
            pltpu.VMEM((rows, cols), BF16),
            pltpu.VMEM((rows, width), BF16),
            pltpu.SemaphoreType.DMA((len(left),)),
            pltpu.SemaphoreType.DMA((len(right),)),
        ],
        compiler_params=pltpu.CompilerParams(vmem_limit_bytes=60 << 20),
        cost_estimate=pl.CostEstimate(
            flops=2 * rows * cols * width, bytes_accessed=2 * (rows * (cols + width) + cols * width), transcendentals=0
        ),
        name="outer",
    )(order, *left, *right)


def qkv_kernel(near_ref, *refs, count):
    x, parts = refs[:count], refs[count : count + 4]
    cos_ref, sin_ref, out_ref, rows_ref, w_ref, x_scr, w_scr, x_sem, w_sem, out_sem = refs[count + 4 :]
    tok = x[0].shape[0]
    groups, depth, cols = parts[0].shape
    heads, half = out_ref.shape[0], HD // 2
    x_in = [
        pltpu.make_async_copy(x[i], x_scr.at[i * tok : (i + 1) * tok], x_sem.at[i])
        for i in range(count)
    ]
    w_in = [
        pltpu.make_async_copy(
            parts[r].at[g],
            w_scr.at[pl.ds(pl.multiple_of((g * 4 + (near_ref[0] ^ r)) * depth, depth), depth)],
            w_sem.at[r, g],
        )
        for r in range(4)
        for g in range(groups)
    ]
    for c in w_in + x_in:
        c.start()
    for c in w_in + x_in:
        c.wait()
    out = [
        pltpu.make_async_copy(x_scr, rows_ref, out_sem.at[0]),
        pltpu.make_async_copy(w_scr, w_ref, out_sem.at[1]),
    ]
    for c in out:
        c.start()
    group = heads * HD
    for i in range(3):
        y = mxu(x_scr[...], w_scr[:, i * group : (i + 1) * group]).T
        for h in range(heads):
            at = slice(i * HD, (i + 1) * HD)
            a, b = y[h * HD : h * HD + half], y[h * HD + half : (h + 1) * HD]
            if i < 2:
                c, s = cos_ref[...], sin_ref[...]
                a, b = a * c - b * s, b * c + a * s
            out_ref[h, at] = jnp.concatenate([a, b], axis=0).astype(BF16)
    for c in out:
        c.wait()


def qkv_of(near, x, parts, cos, sin):
    count, (tok, width) = len(x), x[0].shape
    groups, depth, cols = parts[0].shape
    heads = cols // (3 * HD)
    return pl.pallas_call(
        functools.partial(qkv_kernel, count=count),
        in_specs=[pl.BlockSpec(memory_space=pltpu.SMEM)] + [ANY] * (count + 4) + [VMEM] * 2,
        out_specs=[VMEM, ANY, ANY],
        out_shape=[
            jax.ShapeDtypeStruct((heads, 3 * HD, count * tok), BF16),
            jax.ShapeDtypeStruct((count * tok, width), BF16),
            jax.ShapeDtypeStruct((width, cols), BF16),
        ],
        scratch_shapes=[
            pltpu.VMEM((count * tok, width), BF16),
            pltpu.VMEM((width, cols), BF16),
            pltpu.SemaphoreType.DMA((count,)),
            pltpu.SemaphoreType.DMA((4, groups)),
            pltpu.SemaphoreType.DMA((2,)),
        ],
        compiler_params=pltpu.CompilerParams(vmem_limit_bytes=60 << 20),
        cost_estimate=pl.CostEstimate(
            flops=2 * count * tok * width * cols,
            bytes_accessed=4 * (count * tok * width + width * cols),
            transcendentals=0,
        ),
        name="qkv",
    )(near, *x, *parts, cos, sin)


def turned_rows(d_ref, d_scr, at, rows):
    heads = d_ref.shape[0]
    for i in range(3):
        for h in range(heads):
            top = (i * heads + h) * HD
            d_scr[top : top + HD] = d_ref[h, i * HD : (i + 1) * HD, at : at + rows]


def input_rows_kernel(d_hbm, w_hbm, out_ref, w_scr, d_scr, t_scr, sem, *, slot):
    rows = out_ref.shape[0]
    d_in = pltpu.make_async_copy(d_hbm.at[:, :, slot * rows : (slot + 1) * rows], d_scr, sem.at[0])
    w_in = pltpu.make_async_copy(w_hbm, w_scr, sem.at[1])
    d_in.start()
    w_in.start()
    d_in.wait()
    turned_rows(d_scr, t_scr, 0, rows)
    d = t_scr[...].T
    w_in.wait()
    out_ref[...] = mxu_nt(d, w_scr[...]).astype(BF16)


def input_rows(dqkv, w, slot, tok):
    width, cols = w.shape
    return pl.pallas_call(
        functools.partial(input_rows_kernel, slot=slot),
        in_specs=[ANY, ANY],
        out_specs=VMEM,
        out_shape=jax.ShapeDtypeStruct((tok, width), BF16),
        scratch_shapes=[
            pltpu.VMEM((width, cols), BF16),
            pltpu.VMEM((*dqkv.shape[:2], tok), BF16),
            pltpu.VMEM((cols, tok), BF16),
            pltpu.SemaphoreType.DMA((2,)),
        ],
        compiler_params=pltpu.CompilerParams(vmem_limit_bytes=60 << 20),
        cost_estimate=pl.CostEstimate(
            flops=2 * tok * width * cols, bytes_accessed=2 * width * cols, transcendentals=0
        ),
        name="input_rows",
    )(dqkv, w)


def heads_back_kernel(near_ref, d_ref, x_hbm, w_hbm, *refs, slots, step):
    count = len(slots)
    give_ref, keep_ref = refs[:2]
    out = refs[2 : 2 + count]
    x_scr, w_scr, d_scr, t_scr, y_scr, o_scr, in_sem, out_sem = refs[2 + count :]
    groups, depth = keep_ref.shape[1:3]
    tok, width = out[0].shape
    x_in = pltpu.make_async_copy(x_hbm, x_scr, in_sem.at[0])
    w_in = pltpu.make_async_copy(w_hbm, w_scr, in_sem.at[1])
    w_in.start()
    x_in.start()
    turned_rows(d_ref, d_scr, 0, d_scr.shape[1])
    t_scr[...] = d_scr[...].T
    w_in.wait()
    sent = []
    for n in range(width // step):
        part = slice(n * step, (n + 1) * step)
        o_scr[:, part] = mxu_nt(t_scr[...], w_scr[part, :]).astype(BF16)
        for i, slot in enumerate(slots):
            sent.append(
                pltpu.make_async_copy(
                    o_scr.at[slot * tok : (slot + 1) * tok, part],
                    out[i].at[:, part],
                    out_sem.at[n, i],
                )
            )
            sent[-1].start()
    x_in.wait()
    tile = 4 * depth
    for g in range(groups):
        y_scr[...] = mxu(d_scr[...], x_scr[:, g * tile : (g + 1) * tile]).astype(BF16).T
        for r in range(4):
            rows = pl.ds(pl.multiple_of((near_ref[0] ^ r) * depth, depth), depth)
            (give_ref if r % 2 else keep_ref)[r // 2, g] = y_scr[rows, :]
    for c in sent:
        c.wait()


def heads_back(near, dqkv, x, w, slots, tok):
    rows, width = x.shape
    cols = w.shape[1]
    depth = HD
    groups = width // (4 * depth)
    step = width // 4
    shape = jax.ShapeDtypeStruct((2, groups, depth, cols), BF16)
    out = pl.pallas_call(
        functools.partial(heads_back_kernel, slots=slots, step=step),
        in_specs=[pl.BlockSpec(memory_space=pltpu.SMEM), VMEM, ANY, ANY],
        out_specs=[VMEM, VMEM] + [ANY] * len(slots),
        out_shape=[shape, shape] + [jax.ShapeDtypeStruct((tok, width), BF16)] * len(slots),
        scratch_shapes=[
            pltpu.VMEM((rows, width), BF16),
            pltpu.VMEM((width, cols), BF16),
            pltpu.VMEM((cols, rows), BF16),
            pltpu.VMEM((rows, cols), BF16),
            pltpu.VMEM((4 * depth, cols), BF16),
            pltpu.VMEM((rows, width), BF16),
            pltpu.SemaphoreType.DMA((2,)),
            pltpu.SemaphoreType.DMA((width // step, len(slots))),
        ],
        compiler_params=pltpu.CompilerParams(vmem_limit_bytes=60 << 20),
        cost_estimate=pl.CostEstimate(
            flops=4 * rows * width * cols,
            bytes_accessed=2 * (2 * width * cols + rows * (2 * width + cols)),
            transcendentals=0,
        ),
        name="heads_back",
    )(near, dqkv, x, w)
    return out[:2], out[2:]


def mid_grad_kernel(
    own_ref, across_ref, ahead_ref, mid_ref, dy_ref, scale_ref, gain_ref, w_hbm, dmid_ref, low_ref, out_ref, w_scr, sem
):
    tiles = sem.shape[0]
    width = mid_ref.shape[1]
    rows = w_scr.shape[0] // tiles
    w_in = [
        pltpu.make_async_copy(w_hbm.at[i * rows : (i + 1) * rows], w_scr.at[i * rows : (i + 1) * rows], sem.at[i])
        for i in range(tiles)
    ]
    for c in w_in:
        c.start()
    dn = own_ref[...].astype(F32) + across_ref[...].astype(F32) + ahead_ref[...].astype(F32)
    mid, scale = mid_ref[...], scale_ref[...]
    scaled = gain_ref[...] * dn
    mean = jnp.sum(scaled * mid, axis=-1, keepdims=True) * (1.0 / width)
    dmid = dy_ref[...].astype(F32) + scale * scaled - mid * (scale * scale * scale * mean)
    dmid_ref[...] = dmid
    low = dmid.astype(BF16)
    low_ref[...] = low
    gain_term = jnp.sum(dn * mid * scale, axis=0, keepdims=True)
    high = gain_term.astype(BF16)
    rest = (gain_term - high.astype(F32)).astype(BF16)
    out_ref[:, HD:] = jnp.zeros((out_ref.shape[0], out_ref.shape[1] - HD, out_ref.shape[2]), BF16)
    for h in range(out_ref.shape[0]):
        at = slice(h * HD, (h + 1) * HD)
        out_ref[h, HD : HD + 1, : 2 * HD] = jnp.concatenate([high[:, at], rest[:, at]], axis=1)
    for i in range(tiles):
        w_in[i].wait()
        v = mxu_nt(w_scr[i * rows : (i + 1) * rows, :], low).astype(BF16)
        for j in range(rows // HD):
            out_ref[i * (rows // HD) + j, :HD] = v[j * HD : (j + 1) * HD]


def mid_grad(terms, mid, dy, scale, gain, w):
    tok, width = mid.shape
    owners = w.shape[0] // HD
    return pl.pallas_call(
        mid_grad_kernel,
        in_specs=[VMEM] * 7 + [ANY],
        out_specs=[VMEM] * 3,
        out_shape=[
            jax.ShapeDtypeStruct((tok, width), F32),
            jax.ShapeDtypeStruct((tok, width), BF16),
            jax.ShapeDtypeStruct((owners, HD + 16, tok), BF16),
        ],
        scratch_shapes=[pltpu.VMEM(w.shape, BF16), pltpu.SemaphoreType.DMA((4,))],
        compiler_params=pltpu.CompilerParams(vmem_limit_bytes=60 << 20),
        cost_estimate=pl.CostEstimate(
            flops=2 * tok * width * w.shape[0], bytes_accessed=2 * width * w.shape[0], transcendentals=0
        ),
        name="mid_grad",
    )(*terms, mid, dy, scale, gain, w)


FAR = ("ctx", "row")
NEAR = ("col", "core")


def swap(v, axis):
    return lax.ppermute(v, axis, [(0, 1), (1, 0)])


def shift(v):
    n = lax.axis_size("ctx")
    return lax.ppermute(v, "ctx", [(i, (i + 1) % n) for i in range(n)])


class Flow:
    def __init__(self, steps):
        self.steps = steps
        self.result = None
        self.pending = next(steps)

    def take(self, got):
        try:
            self.pending = self.steps.send(got)
        except StopIteration as end:
            self.pending, self.result = None, end.value

    def run_on(self):
        self.take(self.pending)


def stage(flows, values=(), then=None):
    got, values = lax.optimization_barrier(([f.pending for f in flows], values))
    if then is not None:
        then(values)
    for f, g in zip(flows, got, strict=True):
        f.take(g)
    return values


def spread(v, slots):
    slots[0, 0] = v
    n = lax.axis_size("ctx")
    for c in range(n - 1):
        slots[c + 1, 0], slots[c, 1] = yield shift(slots[c, 0]), swap(slots[c, 0], "row")
    slots[n - 1, 1] = yield swap(slots[n - 1, 0], "row")
    return slots


def spread_late(v, slots):
    slots[0, 0] = v
    n = lax.axis_size("ctx")
    slots[1, 0] = yield shift(v)
    for c in range(1, n - 2):
        slots[c + 1, 0], slots[c - 1, 1] = yield shift(slots[c, 0]), swap(slots[c - 1, 0], "row")
    slots[n - 1, 0], slots[n - 3, 1], slots[n - 2, 1] = yield (
        shift(slots[n - 2, 0]),
        swap(slots[n - 3, 0], "row"),
        swap(slots[n - 2, 0], "row"),
    )
    slots[n - 1, 1] = yield swap(slots[n - 1, 0], "row")
    return slots


def collect(terms, marks, early=False, open_end=False):
    n = lax.axis_size("ctx")
    across = yield swap(terms[1, 1], "row")
    total = terms[1, 0].astype(F32) + across.astype(F32)
    for c in [*range(2, n), 0]:
        send = total.astype(BF16)
        marks.append(send)
        if early and c == 2:
            ahead, across, last = yield (
                shift(send),
                swap(after(terms[c, 1], send), "row"),
                swap(after(terms[0, 1], send), "row"),
            )
        elif early and c == 0:
            ahead, across = (yield shift(send)), last
        else:
            ahead, across = yield shift(send), swap(after(terms[c, 1], send), "row")
        if open_end and c == 0:
            return terms[0, 0], across, ahead
        total = terms[c, 0].astype(F32) + across.astype(F32) + ahead.astype(F32)
    return total


def reduce_near(send, keep):
    got = yield swap(send, "core")
    (give,) = yield for_column(keep, got, 1)
    across = yield swap(give, "col")
    return keep, got, [across]


def for_column(keep, got, pieces):
    rows = keep.shape[1] // pieces
    return [
        (keep[0, p : p + rows].astype(F32) + got[0, p : p + rows].astype(F32)).astype(BF16)
        for p in range(0, keep.shape[1], rows)
    ]


def add_terms(keep, got, across):
    return keep[1].astype(F32) + got[1].astype(F32) + jnp.concatenate(across, axis=0).astype(F32)


def after(v, first):
    return lax.optimization_barrier((v, first))[0]


def beside(v, tok):
    return jnp.pad(v.reshape(*v.shape[:-1], 1, -1), [(0, 0)] * (v.ndim - 1) + [(0, 15), (0, tok - v.shape[-1])])


def by_side(index, mine, theirs):
    return jnp.where(index == 0, mine, theirs), jnp.where(index == 0, theirs, mine)


def to_near(v, col_at, core_at):
    keep, give = by_side(col_at, v[0], v[1])
    got = yield swap(give, "col")
    both = jnp.stack(by_side(col_at, keep, got))
    keep, give = by_side(core_at, both[:, 0], both[:, 1])
    got = yield swap(give, "core")
    return jnp.stack(by_side(core_at, keep, got), axis=1)


def sum_near(give, keep):
    got = yield swap(give, "core")
    other = (keep[1].astype(F32) + got[1].astype(F32)).astype(BF16)
    across = yield swap(other, "col")
    return keep[0].astype(F32) + got[0].astype(F32) + across.astype(F32)


def gather_heads(send):
    mine = yield lax.all_to_all(send, FAR, split_axis=0, concat_axis=0, tiled=True)
    part = mine.shape[0] // 2
    upper, mine_two = yield swap(mine[:part], "col"), swap(mine, "core")
    lower = yield swap(mine[part:], "col")
    other = jnp.concatenate([upper, lower], axis=0)
    other_two = yield swap(other, "core")
    return mine, mine_two, other, other_two


def per_device_split(
    tokens,
    pair_index,
    gain_attn,
    w_query,
    w_key,
    w_value,
    w_out,
    gain_ffn,
    w_gate,
    w_up,
    w_down,
    cotangent,
):
    n_ctx = lax.axis_size("ctx")
    near = lax.axis_size("col") * lax.axis_size("core")
    far = 2 * n_ctx
    tok, width = tokens.shape
    own_in = w_query.shape[0]
    ctx_at, row_at, col_at, core_at = (lax.axis_index(a) for a in ("ctx", "row", "col", "core"))
    near_at = col_at * lax.axis_size("core") + core_at
    blk = near * tok
    rows_here = far * tok
    group = near * HD

    slots = jnp.arange(far, dtype=jnp.int32)
    ctxs = jnp.arange(n_ctx, dtype=jnp.int32)

    def block_of(ctx, row):
        pair = jnp.sum(jnp.where(ctx[:, None] == ctxs[None, :], pair_index[None, :], 0), axis=1)
        return jnp.where(row == 0, pair, far - 1 - pair)

    def place_of_block(block):
        return jnp.sum(jnp.where(block[None, :] == slots[:, None], slots[None, :], 0), axis=1)

    slot_block = block_of((ctx_at - slots % n_ctx + n_ctx) % n_ctx, row_at ^ (slots // n_ctx))
    places = jnp.stack([place_of_block(slot_block), place_of_block(block_of(slots // 2, slots % 2))])
    freq = jnp.exp(jnp.arange(HD // 2, dtype=F32) * (-2.0 * math.log(THETA) / HD))
    token_places = (
        slot_block[:, None] * blk + near_at * tok + jnp.arange(tok, dtype=jnp.int32)[None, :]
    ).reshape(rows_here)
    angle = freq[:, None] * token_places.astype(F32)[None, :]
    cosine, sine = jnp.cos(angle), jnp.sin(angle)
    seq_angle = freq[:, None] * jnp.arange(far * blk, dtype=jnp.int32).astype(F32)[None, :]
    seq_cos, seq_sin = jnp.cos(seq_angle), jnp.sin(seq_angle)

    gain_one = gain_attn.astype(F32)[:, None]
    send = jnp.concatenate(
        [
            (w.astype(F32) * gain_one).astype(BF16).reshape(own_in, far, group)
            for w in (w_query, w_key, w_value)
        ],
        axis=2,
    ).transpose(1, 0, 2)
    x32 = tokens.astype(F32)
    scale_one = lax.rsqrt(jnp.mean(x32 * x32, axis=-1, keepdims=True) + EPS)
    gate_w = lax.all_gather(w_gate, NEAR, axis=0, tiled=True)

    one_flow = Flow(spread((x32 * scale_one).astype(BF16), {}))
    heads_flow = Flow(gather_heads(send))
    w_out = stage([one_flow, heads_flow], w_out)
    out_w = lax.all_gather(w_out, FAR + NEAR, axis=0, tiled=True)
    for _ in range(n_ctx - 3):
        cosine, sine = stage([one_flow, heads_flow], (cosine, sine))
    dy_low = stage([one_flow, heads_flow], cotangent)
    dy_by = {}
    dy_flow = Flow(spread_late(dy_low, dy_by))
    w_rest = stage([one_flow, heads_flow], jnp.concatenate([w_up, w_down], axis=0))
    dy_flow.run_on()
    rest_w = lax.all_gather(w_rest, NEAR, axis=0, tiled=True)
    slot_names = [(c, r) for r in range(2) for c in range(n_ctx)]
    qkv, rows_one, w_heads = qkv_of(
        near_at.reshape(1),
        [one_flow.result[k] for k in slot_names],
        heads_flow.result,
        cosine,
        sine,
    )
    qkv_head, gate_w, seq_cos, seq_sin = stage(
        [dy_flow],
        (
            lax.all_to_all(qkv, NEAR, split_axis=0, concat_axis=0, tiled=True),
            gate_w,
            seq_cos,
            seq_sin,
        ),
    )
    (attn_head, o32, lse, seq), out_w = stage(
        [dy_flow], (attn_fwd(places, qkv_head, beside(gain_ffn, tok), far), out_w)
    )
    attn = stage(
        [dy_flow], lax.all_to_all(attn_head, FAR + NEAR, split_axis=0, concat_axis=0, tiled=True)
    )
    gain_two = attn[:, HD, :own_in].reshape(1, width).astype(F32)
    attn_all = attn[:, :HD]
    attn = attn_all.reshape(width, tok)

    mid = x32 + jnp.einsum("et,ed->td", attn, out_w, preferred_element_type=F32)
    scale_two = lax.rsqrt(jnp.mean(mid * mid, axis=-1, keepdims=True) + EPS)
    normed_two = (mid * scale_two * gain_two).astype(BF16)
    side_flow = Flow(
        to_near(attn_all.reshape(far, 2, 2, HD, tok).transpose(1, 2, 0, 3, 4), col_at, core_at)
    )

    two, dn_by, br_by, kept = {}, {}, {}, []
    two_flow = Flow(spread(normed_two, two))

    def feed(cs, first=()):
        names = [(c, r) for c in cs for r in range(2)]
        rows = after([two[k] for k in names], first)
        dn, br, lefts = ffn(rows, [dy_by[k] for k in names], gate_w, rest_w, near)
        return dict(zip(names, dn, strict=True)), dict(zip(names, br, strict=True)), lefts

    def fed(results):
        dn, br, lefts = results
        dn_by.update(dn)
        br_by.update(br)
        kept.append(lefts)

    stage([two_flow])
    stage([two_flow], feed([0]), fed)
    for c in range(1, n_ctx - 2):
        stage([two_flow], feed([c]), fed)
    marks = []
    dn_flow = Flow(collect(dn_by, marks, open_end=True))
    stage([two_flow, dn_flow, side_flow], feed([n_ctx - 2]), fed)
    last = feed([n_ctx - 1], marks[-1])
    stage([dn_flow, side_flow], last, fed)
    names = [(c, r) for c in range(n_ctx) for r in range(2)]
    two_rows, dy_rows = [two[k] for k in names], [dy_by[k] for k in names]
    tiles = near_at ^ jnp.array([3, 1, 2, 0], jnp.int32)
    lefts = [[k[i] for k in kept] for i in range(3)]
    for _ in range(n_ctx - 4):
        stage([dn_flow])
    gate_terms = outer(tiles, *after((lefts[1], two_rows), marks[-1]))
    gate_flow = Flow(reduce_near(*stage([dn_flow], gate_terms)))
    up_terms = outer(tiles, *after((lefts[2], two_rows), marks[-1]))
    up_terms, br_by = stage([dn_flow, gate_flow], (up_terms, br_by))
    up_send, up_keep = up_terms
    dmid, dmid_low, dattn = mid_grad(dn_flow.result, mid, cotangent, scale_two, gain_two, out_w)
    dmid_near = lax.all_gather(dmid_low, NEAR, axis=0, tiled=True)
    br_marks = []
    br_flow = Flow(collect(br_by, br_marks, early=True, open_end=True))
    down_terms = outer(tiles, *after((lefts[0], dy_rows), dattn))
    gate_flow.pending = after(gate_flow.pending, dattn)
    attn_side = side_flow.result.transpose(2, 3, 0, 1, 4).reshape(far, HD, blk)
    out_term = jnp.einsum(
        "gft,td->gfd", after(attn_side, dattn), dmid_near, preferred_element_type=F32
    )
    dattn_head, down_terms, out_term, up_got = stage(
        [gate_flow, br_flow],
        (
            lax.all_to_all(dattn, FAR + NEAR, split_axis=0, concat_axis=0, tiled=True),
            down_terms,
            out_term.astype(BF16),
            swap(up_send, "core"),
        ),
    )
    out_grad = lax.psum_scatter(
        out_term.reshape(far * HD, width), FAR, scatter_dimension=0, tiled=True
    )
    down_send, down_keep = down_terms
    gain_parts = dattn_head[:, HD, : 2 * own_in].astype(F32)
    dqkv_head, down_got = stage(
        [gate_flow, br_flow],
        (
            attn_bwd(places, seq, o32, lse, dattn_head, seq_cos, seq_sin, far),
            swap(down_send, "core"),
        ),
    )
    exchange = lax.all_to_all(dqkv_head, NEAR, split_axis=0, concat_axis=0, tiled=True)
    up_give = for_column(*after((up_keep, up_got), br_marks[-1]), 2)
    (down_keep, down_got) = after((down_keep, down_got), br_marks[-1])
    dqkv, up_give, down_give = stage(
        [br_flow], (exchange, up_give, for_column(down_keep, down_got, 1)[0])
    )
    dx = {(1, 1): input_rows(dqkv, w_heads, slot_names.index((1, 1)), tok)}
    dx_flow = Flow(collect(dx, marks))
    up_first, up_second = up_give
    rest = [i for i in range(far) if slot_names[i] != (1, 1)]

    def add_rows(values):
        dx.update({slot_names[i]: v for i, v in zip(rest, values[1], strict=True)})

    heads_terms, _, up_first = stage(
        [dx_flow, br_flow],
        (*heads_back(near_at.reshape(1), after(dqkv, dx[1, 1]), rows_one, w_heads, rest, tok), swap(up_first, "col")),
        add_rows,
    )
    heads_flow = Flow(sum_near(*heads_terms))
    stage([heads_flow])
    gate_terms, out_grad, up_second = stage(
        [dx_flow, heads_flow], (gate_flow.result, out_grad, up_second)
    )
    back = lax.all_to_all(
        heads_flow.result.astype(BF16), FAR, split_axis=0, concat_axis=0, tiled=True
    )
    gate_terms, down_give, up_second, branch = stage(
        [dx_flow], (gate_terms, down_give, swap(up_second, "col"), br_flow.result)
    )
    up_terms = up_keep, up_got, [up_first, up_second]
    gate_terms, up_terms, branch = after((gate_terms, up_terms, branch), marks[-1])
    gate_grad, up_grad = add_terms(*gate_terms), add_terms(*up_terms)
    back, down_across = stage([dx_flow], (back, swap(down_give, "col")))
    down_grad = add_terms(down_keep, down_got, [down_across])
    scaled_one = dx_flow.result
    input_grad = (
        dmid
        + scale_one * scaled_one
        - x32 * scale_one**3 * jnp.mean(scaled_one * x32, axis=-1, keepdims=True)
    )
    back = back.astype(F32)
    raw = [
        back[:, :, i * group : (i + 1) * group].transpose(1, 0, 2).reshape(own_in, -1)
        for i in range(3)
    ]
    gain_attn_grad = sum(
        jnp.sum(w.astype(F32) * g, axis=1)
        for w, g in zip((w_query, w_key, w_value), raw, strict=True)
    )
    query_grad, key_grad, value_grad = (g * gain_one for g in raw)
    gain_ffn_grad = jnp.sum(gain_parts[:, :own_in] + gain_parts[:, own_in:], axis=0)
    return (
        (mid + sum(v.astype(F32) for v in branch)).astype(BF16),
        input_grad,
        gain_attn_grad,
        query_grad,
        key_grad,
        value_grad,
        out_grad.astype(F32),
        gain_ffn_grad,
        gate_grad,
        up_grad,
        down_grad,
    )


def solution(mesh):
    n_ctx, n_fsdp = mesh.shape["ctx"], mesh.shape["fsdp"]

    def step(*args):
        if n_fsdp == 8 and n_ctx == 4 and n_ctx * n_fsdp * HD == args[3].shape[1]:
            body, axes = per_device_split, FAR + NEAR
            over = Mesh(np.asarray(mesh.devices).reshape(n_ctx, 2, 2, 2), axes)
        else:
            body, axes, over = per_device_any, ("ctx", "fsdp"), mesh
        rows, line = P(axes, None), P(axes)
        return jax.shard_map(
            body,
            mesh=over,
            in_specs=(rows, P(), line, rows, rows, rows, rows, line, rows, rows, rows, rows),
            out_specs=(rows, rows, line, rows, rows, rows, rows, line, rows, rows, rows),
            check_vma=False,
        )(*args)

    return step
```

```python
import functools
import math

import jax
import jax.numpy as jnp
import numpy as np
from jax import lax
from jax.experimental import pallas as pl
from jax.experimental.pallas import tpu as pltpu
from jax.sharding import Mesh
from jax.sharding import PartitionSpec as P

HD = 64


EPS = 1e-05
THETA = 130000.0


def place_of(rows, pair_index, n_groups, blk):
    group = rows // (2 * blk)
    within = rows % (2 * blk)
    match = group[:, None] == jnp.arange(n_groups, dtype=jnp.int32)[None, :]
    pair = jnp.sum(jnp.where(match, pair_index[None, :], 0), axis=1)
    block = jnp.where(within < blk, pair, 2 * n_groups - 1 - pair)
    return block * blk + within % blk


def tables(places, head_dim):
    freq = jnp.exp(
        jnp.arange(head_dim // 2, dtype=jnp.float32) * (-2.0 * math.log(THETA) / head_dim)
    )
    angle = places.astype(jnp.float32)[:, None] * freq[None, :]
    return (jnp.cos(angle), jnp.sin(angle))


def rotate(flat, cosine, sine, head_dim):
    rows = flat.shape[0]
    split = flat.reshape(rows, -1, head_dim)
    half = head_dim // 2
    first = split[..., :half]
    second = split[..., half:]
    cos_b = cosine[:, None, :]
    sin_b = sine[:, None, :]
    out = jnp.concatenate([first * cos_b - second * sin_b, second * cos_b + first * sin_b], axis=-1)
    return out.reshape(rows, -1)


def silu_parts(gate):
    sig = jax.nn.sigmoid(gate)
    return (gate * sig, sig * (1.0 + gate * (1.0 - sig)))


def rows_by(left, right):
    return jnp.einsum("td,fd->tf", left, right, preferred_element_type=jnp.float32)


def outer_sum(left, right):
    return jnp.einsum("tf,td->fd", left, right, preferred_element_type=jnp.float32)


def per_device_any(
    tokens,
    pair_index,
    gain_attn,
    w_query,
    w_key,
    w_value,
    w_out,
    gain_ffn,
    w_gate,
    w_up,
    w_down,
    cotangent,
):
    f32 = jnp.float32
    bf16 = jnp.bfloat16
    n_ctx = lax.axis_size("ctx")
    n_fsdp = lax.axis_size("fsdp")
    tok = tokens.shape[0]
    group_rows = tok * n_fsdp
    blk = group_rows // 2
    total = group_rows * n_ctx
    ctx_index = lax.axis_index("ctx")
    fsdp_index = lax.axis_index("fsdp")
    local_rows = (ctx_index * n_fsdp + fsdp_index) * tok + jnp.arange(tok, dtype=jnp.int32)
    local_places = place_of(local_rows, pair_index, n_ctx, blk)
    group_places = place_of(
        ctx_index * group_rows + jnp.arange(group_rows, dtype=jnp.int32), pair_index, n_ctx, blk
    )
    key_places = place_of(jnp.arange(total, dtype=jnp.int32), pair_index, n_ctx, blk)
    group_cos, group_sin = tables(group_places, HD)
    query_full, key_full, value_full, out_full, gain_one, gain_two = (
        lax.all_gather(w_query, ("ctx", "fsdp"), axis=0, tiled=True),
        lax.all_gather(w_key, ("ctx", "fsdp"), axis=0, tiled=True),
        lax.all_gather(w_value, ("ctx", "fsdp"), axis=0, tiled=True),
        lax.all_gather(w_out, ("ctx", "fsdp"), axis=0, tiled=True),
        lax.all_gather(gain_attn, ("ctx", "fsdp"), axis=0, tiled=True),
        lax.all_gather(gain_ffn, ("ctx", "fsdp"), axis=0, tiled=True),
    )
    gain_one = gain_one.astype(f32)
    gain_two = gain_two.astype(f32)
    x32 = tokens.astype(f32)
    scale_one = lax.rsqrt(jnp.mean(x32 * x32, axis=-1, keepdims=True) + EPS)
    normed_one = (x32 * scale_one * gain_one).astype(bf16)
    cosine, sine = tables(local_places, HD)
    query = rotate(
        jnp.dot(normed_one, query_full, preferred_element_type=f32), cosine, sine, HD
    ).astype(bf16)
    key = rotate(
        jnp.dot(normed_one, key_full, preferred_element_type=f32), cosine, sine, HD
    ).astype(bf16)
    value = jnp.dot(normed_one, value_full, preferred_element_type=f32).astype(bf16)
    query_heads, key_heads, value_heads = (
        lax.all_to_all(query, "fsdp", split_axis=1, concat_axis=0, tiled=True),
        lax.all_to_all(key, "fsdp", split_axis=1, concat_axis=0, tiled=True),
        lax.all_to_all(value, "fsdp", split_axis=1, concat_axis=0, tiled=True),
    )
    key_all, value_all = (
        lax.all_gather(key_heads, "ctx", axis=0, tiled=True),
        lax.all_gather(value_heads, "ctx", axis=0, tiled=True),
    )
    local_width = query_heads.shape[1]
    heads_here = local_width // HD
    scale = HD ** (-0.5)
    query_parts = query_heads.reshape(2, blk, heads_here, HD)
    query_place_tiles = group_places.reshape(2, blk)
    key_tiles = key_all.reshape(2 * n_ctx, blk, heads_here, HD)
    value_tiles = value_all.reshape(2 * n_ctx, blk, heads_here, HD)
    key_place_tiles = key_places.reshape(2 * n_ctx, blk)

    def tile_scores(slot, keys, k_place):
        raw = (
            jnp.einsum("qhd,khd->hqk", query_parts[slot], keys, preferred_element_type=f32) * scale
        )
        keep = k_place[None, None, :] <= query_place_tiles[slot][None, :, None]
        return jnp.where(keep, raw, -1e30)

    def is_live(slot, k_place):
        return jnp.min(k_place) <= jnp.max(query_place_tiles[slot])

    def first_pass(carry, tile):
        keys, k_place = tile
        highs, totals = carry
        new_highs = []
        new_totals = []
        for slot in range(2):

            def first_update(high, summed):
                masked = tile_scores(slot, keys, k_place)
                fresh = jnp.maximum(high, jnp.max(masked, axis=-1))
                summed = summed * jnp.exp(high - fresh) + jnp.sum(
                    jnp.exp(masked - fresh[..., None]), axis=-1
                )
                return (fresh, summed)

            def first_leave(high, summed):
                return (high, summed)

            high, summed = lax.cond(
                is_live(slot, k_place), first_update, first_leave, highs[slot], totals[slot]
            )
            new_highs.append(high)
            new_totals.append(summed)
        return ((jnp.stack(new_highs), jnp.stack(new_totals)), None)

    start_high = jnp.full((2, heads_here, blk), -1e30, f32)
    start_total = jnp.zeros((2, heads_here, blk), f32)
    (highs, totals), unused = lax.scan(
        first_pass, (start_high, start_total), (key_tiles, key_place_tiles)
    )
    log_total = highs + jnp.log(totals)

    def second_pass(carry, tile):
        keys, values, k_place = tile
        outs = []
        for slot in range(2):

            def second_update(acc):
                masked = tile_scores(slot, keys, k_place)
                prob_low = jnp.exp(masked - log_total[slot][..., None]).astype(bf16)
                return acc + jnp.einsum(
                    "hqk,khd->qhd", prob_low, values, preferred_element_type=f32
                )

            def second_leave(acc):
                return acc

            outs.append(lax.cond(is_live(slot, k_place), second_update, second_leave, carry[slot]))
        return (jnp.stack(outs), None)

    acc_start = jnp.zeros((2, blk, heads_here, HD), f32)
    attn_acc, unused = lax.scan(second_pass, acc_start, (key_tiles, value_tiles, key_place_tiles))
    attn32 = attn_acc.reshape(group_rows, local_width)
    attn_tokens = lax.all_to_all(
        attn32.astype(bf16), "fsdp", split_axis=0, concat_axis=1, tiled=True
    )
    mid = x32 + jnp.dot(attn_tokens, out_full, preferred_element_type=f32)
    scale_two = lax.rsqrt(jnp.mean(mid * mid, axis=-1, keepdims=True) + EPS)
    normed_two = (mid * scale_two * gain_two).astype(bf16)
    dy = cotangent.astype(f32)
    dy_low = dy.astype(bf16)
    gate_local, up_local, down_local = (
        lax.all_gather(w_gate, "ctx", axis=0, tiled=True),
        lax.all_gather(w_up, "ctx", axis=0, tiled=True),
        lax.all_gather(w_down, "ctx", axis=0, tiled=True),
    )
    rows_all = lax.all_gather(normed_two, "fsdp", axis=0, tiled=True)
    gate_all = rows_by(rows_all, gate_local)
    up_all = rows_by(rows_all, up_local)
    silu_all, unused_slope = silu_parts(gate_all)
    hidden_all = (silu_all * up_all).astype(bf16)
    branch = lax.psum_scatter(
        jnp.dot(hidden_all, down_local, preferred_element_type=f32).astype(jnp.bfloat16),
        "fsdp",
        scatter_dimension=0,
        tiled=True,
    ).astype(jnp.float32)
    block_out = (mid + branch).astype(bf16)
    grad_rows_all = lax.all_gather(dy_low, "fsdp", axis=0, tiled=True)
    dhidden = rows_by(grad_rows_all, down_local)
    silu_val, slope = silu_parts(gate_all)
    dgate = (dhidden * up_all * slope).astype(bf16)
    dup = (dhidden * silu_val).astype(bf16)
    gate_term = outer_sum(dgate, rows_all)
    up_term = outer_sum(dup, rows_all)
    down_term = outer_sum(hidden_all, grad_rows_all)
    gate_grad, up_grad, down_grad = (
        lax.psum_scatter(
            gate_term.astype(jnp.bfloat16), "ctx", scatter_dimension=0, tiled=True
        ).astype(jnp.float32),
        lax.psum_scatter(
            up_term.astype(jnp.bfloat16), "ctx", scatter_dimension=0, tiled=True
        ).astype(jnp.float32),
        lax.psum_scatter(
            down_term.astype(jnp.bfloat16), "ctx", scatter_dimension=0, tiled=True
        ).astype(jnp.float32),
    )
    dnormed_two = lax.psum_scatter(
        (
            jnp.dot(dgate, gate_local, preferred_element_type=f32)
            + jnp.dot(dup, up_local, preferred_element_type=f32)
        ).astype(jnp.bfloat16),
        "fsdp",
        scatter_dimension=0,
        tiled=True,
    ).astype(jnp.float32)
    gain_two_term = jnp.sum(dnormed_two * mid * scale_two, axis=0)
    scaled_two = gain_two * dnormed_two
    dmid = (
        dy
        + scale_two * scaled_two
        - mid * scale_two**3 * jnp.mean(scaled_two * mid, axis=-1, keepdims=True)
    )
    dmid_low = dmid.astype(bf16)
    out_term = jnp.einsum("td,te->de", attn_tokens, dmid_low, preferred_element_type=f32)
    dattn = jnp.einsum("te,de->td", dmid_low, out_full, preferred_element_type=f32).astype(bf16)
    dattn_heads = lax.all_to_all(dattn, "fsdp", split_axis=1, concat_axis=0, tiled=True)
    delta = jnp.sum((dattn_heads.astype(f32) * attn32).reshape(group_rows, heads_here, HD), axis=-1)
    delta_tiles = delta.reshape(2, blk, heads_here).transpose(0, 2, 1)
    grad_parts = dattn_heads.reshape(2, blk, heads_here, HD)

    def back_pass(carry, tile):
        keys, values, k_place = tile
        key_acc = jnp.zeros((blk, heads_here, HD), f32)
        value_acc = jnp.zeros((blk, heads_here, HD), f32)
        new_query = []
        for slot in range(2):

            def back_update(q_acc, k_acc, v_acc):
                masked = tile_scores(slot, keys, k_place)
                prob = jnp.exp(masked - log_total[slot][..., None])
                prob_low = prob.astype(bf16)
                dprob = jnp.einsum(
                    "qhd,khd->hqk", grad_parts[slot], values, preferred_element_type=f32
                )
                dscore = (prob * (dprob - delta_tiles[slot][..., None])).astype(bf16)
                q_acc = (
                    q_acc
                    + jnp.einsum("hqk,khd->qhd", dscore, keys, preferred_element_type=f32) * scale
                )
                k_acc = (
                    k_acc
                    + jnp.einsum(
                        "hqk,qhd->khd", dscore, query_parts[slot], preferred_element_type=f32
                    )
                    * scale
                )
                v_acc = v_acc + jnp.einsum(
                    "hqk,qhd->khd", prob_low, grad_parts[slot], preferred_element_type=f32
                )
                return (q_acc, k_acc, v_acc)

            def back_leave(q_acc, k_acc, v_acc):
                return (q_acc, k_acc, v_acc)

            q_acc, key_acc, value_acc = lax.cond(
                is_live(slot, k_place), back_update, back_leave, carry[slot], key_acc, value_acc
            )
            new_query.append(q_acc)
        return (jnp.stack(new_query), (key_acc, value_acc))

    dquery_start = jnp.zeros((2, blk, heads_here, HD), f32)
    dquery_acc, (dkey_tiles, dvalue_tiles) = lax.scan(
        back_pass, dquery_start, (key_tiles, value_tiles, key_place_tiles)
    )
    dkey_all = dkey_tiles.reshape(total, local_width)
    dvalue_all = dvalue_tiles.reshape(total, local_width)
    dkey_own, dvalue_own = (
        lax.psum_scatter(
            dkey_all.astype(jnp.bfloat16), "ctx", scatter_dimension=0, tiled=True
        ).astype(jnp.float32),
        lax.psum_scatter(
            dvalue_all.astype(jnp.bfloat16), "ctx", scatter_dimension=0, tiled=True
        ).astype(jnp.float32),
    )
    dquery_low = rotate(
        dquery_acc.reshape(group_rows, local_width), group_cos, -group_sin, HD
    ).astype(bf16)
    dkey_low = rotate(dkey_own, group_cos, -group_sin, HD).astype(bf16)
    dvalue_low = dvalue_own.astype(bf16)
    dquery_tok, dkey_tok, dvalue_tok = (
        lax.all_to_all(dquery_low, "fsdp", split_axis=0, concat_axis=1, tiled=True),
        lax.all_to_all(dkey_low, "fsdp", split_axis=0, concat_axis=1, tiled=True),
        lax.all_to_all(dvalue_low, "fsdp", split_axis=0, concat_axis=1, tiled=True),
    )
    dnormed_one = (
        jnp.einsum("te,de->td", dquery_tok, query_full, preferred_element_type=f32)
        + jnp.einsum("te,de->td", dkey_tok, key_full, preferred_element_type=f32)
        + jnp.einsum("te,de->td", dvalue_tok, value_full, preferred_element_type=f32)
    )
    query_term = jnp.einsum("td,te->de", normed_one, dquery_tok, preferred_element_type=f32)
    key_term = jnp.einsum("td,te->de", normed_one, dkey_tok, preferred_element_type=f32)
    value_term = jnp.einsum("td,te->de", normed_one, dvalue_tok, preferred_element_type=f32)
    gain_one_term = jnp.sum(dnormed_one * x32 * scale_one, axis=0)
    scaled_one = gain_one * dnormed_one
    input_grad = (
        dmid
        + scale_one * scaled_one
        - x32 * scale_one**3 * jnp.mean(scaled_one * x32, axis=-1, keepdims=True)
    )
    query_grad, key_grad, value_grad, out_grad, gain_attn_grad, gain_ffn_grad = (
        lax.psum_scatter(query_term, ("ctx", "fsdp"), scatter_dimension=0, tiled=True),
        lax.psum_scatter(key_term, ("ctx", "fsdp"), scatter_dimension=0, tiled=True),
        lax.psum_scatter(value_term, ("ctx", "fsdp"), scatter_dimension=0, tiled=True),
        lax.psum_scatter(out_term, ("ctx", "fsdp"), scatter_dimension=0, tiled=True),
        lax.psum_scatter(gain_one_term, ("ctx", "fsdp"), scatter_dimension=0, tiled=True),
        lax.psum_scatter(gain_two_term, ("ctx", "fsdp"), scatter_dimension=0, tiled=True),
    )
    return (
        block_out,
        input_grad,
        gain_attn_grad,
        query_grad,
        key_grad,
        value_grad,
        out_grad,
        gain_ffn_grad,
        gate_grad,
        up_grad,
        down_grad,
    )


BF16 = jnp.bfloat16
F32 = jnp.float32
LOG2E = math.log2(math.e)
VMEM = pl.BlockSpec(memory_space=pltpu.VMEM)
ANY = pl.BlockSpec(memory_space=pl.ANY)


def mxu(a, b):
    return jnp.dot(a, b, preferred_element_type=F32)


def causal(blk):
    row = lax.broadcasted_iota(jnp.int32, (blk, blk), 0)
    col = lax.broadcasted_iota(jnp.int32, (blk, blk), 1)
    return row <= col


def attn_fwd_kernel(
    place_ref,
    qkv_ref,
    extra_ref,
    out_ref,
    o32_hbm,
    lse_ref,
    seq_hbm,
    seq_ref,
    o32_ref,
    seq_sem,
    o32_sem,
    k_scr,
    m_scr,
    l_scr,
    acc_scr,
    *,
    blocks,
    width,
):
    pieces = qkv_ref.shape[0]
    blk = pieces * width
    coef = LOG2E * HD**-0.5
    for s in range(blocks):
        at = pl.multiple_of(place_ref[0, s] * width, width)
        for j in range(pieces):
            lo = s * blk + j * width
            piece = qkv_ref[j, :, pl.ds(at, width)]
            seq_ref[:, lo : lo + width] = piece
            k_scr[lo : lo + width, :] = piece[HD : 2 * HD].T

    leaving = [pltpu.make_async_copy(seq_ref, seq_hbm, seq_sem)]
    leaving[0].start()

    def tile(kb, q_t, masked, wide=1):
        keys = pl.ds(pl.multiple_of(kb * blk, blk), wide * blk)
        score = mxu(k_scr[keys, :], q_t) * coef
        if masked:
            score = jnp.where(causal(blk), score, -1e30)
        old = m_scr[...]
        new = jnp.maximum(old, jnp.max(score, axis=0, keepdims=True))
        p = jnp.exp2(score - new)
        fade = jnp.exp2(old - new)
        m_scr[...] = new
        l_scr[...] = l_scr[...] * fade + jnp.sum(p, axis=0, keepdims=True)
        acc_scr[...] = acc_scr[...] * fade + mxu(seq_ref[2 * HD :, keys], p.astype(BF16))

    for qb in range(blocks):
        lo = qb * blk
        q_t = seq_ref[:HD, lo : lo + blk]
        m_scr[...] = jnp.full_like(m_scr, -1e30)
        l_scr[...] = jnp.zeros_like(l_scr)
        acc_scr[...] = jnp.zeros_like(acc_scr)
        tile(qb, q_t, True)
        kb = 0
        while kb < qb:
            wide = min(4, qb - kb)
            tile(kb, q_t, False, wide)
            kb += wide

        o = acc_scr[...] / l_scr[...]
        o32_ref[:, lo : lo + blk] = o
        leaving.append(
            pltpu.make_async_copy(
                o32_ref.at[:, lo : lo + blk], o32_hbm.at[:, lo : lo + blk], o32_sem.at[qb]
            )
        )
        leaving[-1].start()
        lse_ref[:, lo : lo + blk] = m_scr[...] + jnp.log2(l_scr[...])
        low = o.astype(BF16)
        for j in range(pieces):
            owner = place_ref[1, qb] * pieces + j
            out_ref[owner, :HD] = low[:, j * width : (j + 1) * width]
            out_ref[owner, HD:] = extra_ref[...]
    for c in leaving:
        c.wait()


def attn_fwd(place, qkv, extra, blocks):
    pieces, _, cols = qkv.shape
    total = pieces * cols
    blk = total // blocks
    return pl.pallas_call(
        functools.partial(attn_fwd_kernel, blocks=blocks, width=cols // blocks),
        out_shape=(
            jax.ShapeDtypeStruct((blocks * pieces, HD + extra.shape[0], cols // blocks), BF16),
            jax.ShapeDtypeStruct((HD, total), F32),
            jax.ShapeDtypeStruct((1, total), F32),
            jax.ShapeDtypeStruct((3 * HD, total), BF16),
        ),
        in_specs=[pl.BlockSpec(memory_space=pltpu.SMEM), VMEM, VMEM],
        out_specs=(VMEM, ANY, VMEM, ANY),
        scratch_shapes=[
            pltpu.VMEM((3 * HD, total), BF16),
            pltpu.VMEM((HD, total), F32),
            pltpu.SemaphoreType.DMA,
            pltpu.SemaphoreType.DMA((blocks,)),
            pltpu.VMEM((total, HD), BF16),
            pltpu.VMEM((1, blk), F32),
            pltpu.VMEM((1, blk), F32),
            pltpu.VMEM((HD, blk), F32),
        ],
        compiler_params=pltpu.CompilerParams(vmem_limit_bytes=60 << 20),
        cost_estimate=pl.CostEstimate(
            flops=8 * total * total * HD, bytes_accessed=8 << 20, transcendentals=total * total // 2
        ),
        name="attn_fwd",
    )(place, qkv, extra)


def attn_bwd_kernel(
    place_ref,
    seq_hbm,
    o32_hbm,
    lse_ref,
    do_ref,
    cos_hbm,
    sin_hbm,
    out_ref,
    seq_ref,
    o32_ref,
    cos_ref,
    sin_ref,
    in_sem,
    q_scr,
    k_scr,
    v_scr,
    do_scr,
    dot_scr,
    delta_scr,
    dq_scr,
    dk_scr,
    dv_scr,
    *,
    blocks,
    width,
):
    pieces = out_ref.shape[0]
    blk = pieces * width
    scale = HD**-0.5
    coef = LOG2E * scale
    half = HD // 2
    arriving = [
        pltpu.make_async_copy(src, dst, in_sem.at[i])
        for i, (src, dst) in enumerate(
            ((seq_hbm, seq_ref), (o32_hbm, o32_ref), (cos_hbm, cos_ref), (sin_hbm, sin_ref))
        )
    ]
    for c in arriving:
        c.start()
    for c in arriving[:2]:
        c.wait()
    for s in range(blocks):
        for j in range(pieces):
            lo = s * blk + j * width
            piece = do_ref[place_ref[1, s] * pieces + j, :HD]
            dot_scr[:, lo : lo + width] = piece
            do_scr[lo : lo + width, :] = piece.T
            delta_scr[:, lo : lo + width] = jnp.sum(
                piece.astype(F32) * o32_ref[:, lo : lo + width], axis=0, keepdims=True
            )
            q_scr[lo : lo + width, :] = seq_ref[:HD, lo : lo + width].T
            k_scr[lo : lo + width, :] = seq_ref[HD : 2 * HD, lo : lo + width].T
            v_scr[lo : lo + width, :] = seq_ref[2 * HD :, lo : lo + width].T
    dq_scr[...] = jnp.zeros_like(dq_scr)
    for c in arriving[2:]:
        c.wait()

    def turn_back(v, s):
        c = cos_ref[:, s * blk : (s + 1) * blk]
        n = sin_ref[:, s * blk : (s + 1) * blk]
        a, b = v[:half], v[half:]
        return jnp.concatenate([a * c + b * n, b * c - a * n], axis=0).astype(BF16)

    def put(v, s, row):
        at = pl.multiple_of(place_ref[0, s] * width, width)
        for j in range(pieces):
            out_ref[j, row * HD : (row + 1) * HD, pl.ds(at, width)] = v[:, j * width : (j + 1) * width]

    for kb in range(blocks):
        lo = kb * blk
        k = k_scr[lo : lo + blk, :]
        v = v_scr[lo : lo + blk, :]
        k_t = seq_ref[HD : 2 * HD, lo : lo + blk]

        def tile(qb, masked, wide=1):
            here = pl.ds(pl.multiple_of(qb * blk, blk), wide * blk)
            p = jnp.exp2(mxu(k, seq_ref[:HD, here]) * coef - lse_ref[:, here])
            if masked:
                p = jnp.where(causal(blk), p, 0.0)
            dp = mxu(v, dot_scr[:, here])
            ds = (p * (dp - delta_scr[:, here])).astype(BF16)
            dq_scr[:, here] += mxu(k_t, ds)
            return mxu(ds, q_scr[here, :]), mxu(p.astype(BF16), do_scr[here, :])

        dk_scr[...], dv_scr[...] = tile(kb, True)

        def add_tile(qb, wide):
            dk, dv = tile(qb, False, wide)
            dk_scr[...] += dk
            dv_scr[...] += dv

        qb = kb + 1
        while qb < blocks:
            wide = min(2, blocks - qb)
            add_tile(qb, wide)
            qb += wide

        put(turn_back(dq_scr[:, lo : lo + blk] * scale, kb), kb, 0)
        put(turn_back((dk_scr[...] * scale).T, kb), kb, 1)
        put(dv_scr[...].T.astype(BF16), kb, 2)


def attn_bwd(place, seq, o32, lse, do, cos, sin, blocks):
    pieces, width = do.shape[0] // blocks, do.shape[2]
    cols, total, blk = blocks * width, seq.shape[1], pieces * width
    return pl.pallas_call(
        functools.partial(attn_bwd_kernel, blocks=blocks, width=width),
        out_shape=jax.ShapeDtypeStruct((pieces, 3 * HD, cols), BF16),
        in_specs=[pl.BlockSpec(memory_space=pltpu.SMEM), ANY, ANY, VMEM, VMEM, ANY, ANY],
        out_specs=VMEM,
        scratch_shapes=[
            pltpu.VMEM(seq.shape, BF16),
            pltpu.VMEM(o32.shape, F32),
            pltpu.VMEM(cos.shape, F32),
            pltpu.VMEM(sin.shape, F32),
            pltpu.SemaphoreType.DMA((4,)),
        ]
        + [pltpu.VMEM((total, HD), BF16)] * 4
        + [
            pltpu.VMEM((HD, total), BF16),
            pltpu.VMEM((1, total), F32),
            pltpu.VMEM((HD, total), F32),
            pltpu.VMEM((blk, HD), F32),
            pltpu.VMEM((blk, HD), F32),
        ],
        compiler_params=pltpu.CompilerParams(vmem_limit_bytes=60 << 20),
        cost_estimate=pl.CostEstimate(
            flops=20 * total * total * HD, bytes_accessed=8 << 20, transcendentals=total * total // 2
        ),
        name="attn_bwd",
    )(place, seq, o32, lse, do, cos, sin)


def mxu_nt(a, b):
    return lax.dot_general(a, b, (((1,), (1,)), ((), ())), preferred_element_type=F32)


def mxu_tn(a, b):
    return lax.dot_general(a, b, (((0,), (0,)), ((), ())), preferred_element_type=F32)


def ffn_kernel(*refs, count, step):
    x, dy = refs[:count], refs[count : 2 * count]
    gate_hbm, rest_hbm = refs[2 * count : 2 * count + 2]
    refs = refs[2 * count + 2 :]
    dn, br, kept = refs[:count], refs[count : 2 * count], refs[2 * count : 2 * count + 3]
    (
        x_scr,
        dy_scr,
        gate_w,
        up_w,
        down_w,
        hid_scr,
        dgate_scr,
        dup_scr,
        act_scr,
        dn_scr,
        br_scr,
        in_sem,
        w_sem,
        out_sem,
        keep_sem,
    ) = refs[2 * count + 3 :]
    tok, width = x[0].shape
    hidden, parts = gate_w.shape[0], w_sem.shape[1]
    part = hidden // parts
    rows_in = [
        pltpu.make_async_copy(src[i], dst.at[i * tok : (i + 1) * tok], in_sem.at[k, i])
        for k, (src, dst) in enumerate(((x, x_scr), (dy, dy_scr)))
        for i in range(count)
    ]
    gate_in, up_in, down_in = (
        [
            pltpu.make_async_copy(
                src.at[at(j) * part : (at(j) + 1) * part],
                dst.at[j * part : (j + 1) * part],
                w_sem.at[i, j],
            )
            for j in range(parts)
        ]
        for i, (src, at, dst) in enumerate(
            (
                (gate_hbm, lambda j: j, gate_w),
                (rest_hbm, lambda j: 2 * j, up_w),
                (rest_hbm, lambda j: 2 * j + 1, down_w),
            )
        )
    )
    for c in rows_in[:count]:
        c.start()
    for pair in zip(gate_in, up_in, strict=True):
        for c in pair:
            c.start()
    for c in rows_in[count:] + down_in:
        c.start()
    for c in rows_in[:count]:
        c.wait()
    for lo, hi in ((0, parts // 2), (parts // 2, parts)):
        for c in gate_in[lo:hi] + up_in[lo:hi]:
            c.wait()
        here = slice(lo * part, hi * part)
        gate = mxu_nt(x_scr[...], gate_w[here, :])
        up = mxu_nt(x_scr[...], up_w[here, :])
        sig = jax.nn.sigmoid(gate)
        act = gate * sig
        hid_scr[:, here] = (act * up).astype(BF16)
        act_scr[:, here] = act
        dgate_scr[:, here] = up * (sig * (1.0 + gate * (1.0 - sig)))
    for c in rows_in[count:]:
        c.wait()
    for lo, hi in ((0, parts // 2), (parts // 2, parts)):
        for c in down_in[lo:hi]:
            c.wait()
        here = slice(lo * part, hi * part)
        dhidden = mxu_nt(dy_scr[...], down_w[here, :])
        dup_scr[1, :, here] = (dhidden * act_scr[:, here]).astype(BF16)
        dup_scr[0, :, here] = (dhidden * dgate_scr[:, here]).astype(BF16)
    keep = [
        pltpu.make_async_copy(src, dst, keep_sem.at[k])
        for k, (src, dst) in enumerate(zip((hid_scr, dup_scr.at[0], dup_scr.at[1]), kept))
    ]
    for c in keep:
        c.start()
    sent = []
    for n in range(width // step):
        part = slice(n * step, (n + 1) * step)
        total = mxu(dup_scr[0], gate_w[:, part]) + mxu(dup_scr[1], up_w[:, part])
        dn_scr[:, part] = total.astype(BF16)
        br_scr[:, part] = mxu(hid_scr[...], down_w[:, part]).astype(BF16)
        for i in range(count):
            rows = slice(i * tok, (i + 1) * tok)
            for k, (src, dst) in enumerate(((dn_scr, dn[i]), (br_scr, br[i]))):
                sent.append(pltpu.make_async_copy(src.at[rows, part], dst.at[:, part], out_sem.at[k, i, n]))
                sent[-1].start()
    for c in keep + sent:
        c.wait()


def ffn(x, dy, gate_w, rest_w, parts):
    count, (tok, width), hidden = len(x), x[0].shape, gate_w.shape[0]
    rows, step = count * tok, width // 4
    out = pl.pallas_call(
        functools.partial(ffn_kernel, count=count, step=step),
        in_specs=[ANY] * (2 * count + 2),
        out_specs=[ANY] * (2 * count + 3),
        out_shape=[jax.ShapeDtypeStruct((tok, width), BF16)] * (2 * count)
        + [jax.ShapeDtypeStruct((rows, hidden), BF16)] * 3,
        scratch_shapes=[pltpu.VMEM((rows, width), BF16)] * 2
        + [pltpu.VMEM((hidden, width), BF16)] * 3
        + [
            pltpu.VMEM((rows, hidden), BF16),
            pltpu.VMEM((rows, hidden), F32),
            pltpu.VMEM((2, rows, hidden), BF16),
            pltpu.VMEM((rows, hidden), F32),
            pltpu.VMEM((rows, width), BF16),
            pltpu.VMEM((rows, width), BF16),
            pltpu.SemaphoreType.DMA((2, count)),
            pltpu.SemaphoreType.DMA((3, parts)),
            pltpu.SemaphoreType.DMA((2, count, width // step)),
            pltpu.SemaphoreType.DMA((3,)),
        ],
        compiler_params=pltpu.CompilerParams(vmem_limit_bytes=60 << 20),
        cost_estimate=pl.CostEstimate(
            flops=12 * rows * hidden * width, bytes_accessed=6 * hidden * width + 16 * rows * width, transcendentals=rows * hidden
        ),
        name="ffn",
    )(*x, *dy, gate_w, rest_w)
    return out[:count], out[count : 2 * count], out[2 * count :]


def outer_kernel(*refs, lefts, rights):
    order = refs[0]
    left, right = refs[1 : 1 + lefts], refs[1 + lefts : 1 + lefts + rights]
    send, keep, l_scr, r_scr, l_sem, r_sem = refs[1 + lefts + rights :]
    i = pl.program_id(0)

    def into(parts, scr, sem):
        at, out = 0, []
        for k, part in enumerate(parts):
            out.append(pltpu.make_async_copy(part, scr.at[at : at + part.shape[0]], sem.at[k]))
            at += part.shape[0]
        return out

    @pl.when(i == 0)
    def _():
        copies = into(left, l_scr, l_sem) + into(right, r_scr, r_sem)
        for c in copies:
            c.start()
        for c in copies:
            c.wait()

    tile = send.shape[1]
    l = l_scr[:, pl.ds(pl.multiple_of(order[i] * tile, tile), tile)]
    v = mxu_tn(l, r_scr[...]).astype(BF16)

    @pl.when(i < 2)
    def _():
        send[0] = v

    @pl.when(i >= 2)
    def _():
        keep[0] = v


def outer(order, left, right):
    cols, width = left[0].shape[1], right[0].shape[1]
    rows = sum(p.shape[0] for p in left)
    tile = cols // 4
    return pl.pallas_call(
        functools.partial(outer_kernel, lefts=len(left), rights=len(right)),
        grid=(4,),
        in_specs=[pl.BlockSpec(memory_space=pltpu.SMEM)] + [ANY] * (len(left) + len(right)),
        out_specs=[
            pl.BlockSpec((1, tile, width), lambda i: (jnp.minimum(i, 1), 0, 0)),
            pl.BlockSpec((1, tile, width), lambda i: (jnp.maximum(i - 2, 0), 0, 0)),
        ],
        out_shape=[jax.ShapeDtypeStruct((2, tile, width), BF16)] * 2,
        scratch_shapes=[
            pltpu.VMEM((rows, cols), BF16),
            pltpu.VMEM((rows, width), BF16),
            pltpu.SemaphoreType.DMA((len(left),)),
            pltpu.SemaphoreType.DMA((len(right),)),
        ],
        compiler_params=pltpu.CompilerParams(vmem_limit_bytes=60 << 20),
        cost_estimate=pl.CostEstimate(
            flops=2 * rows * cols * width, bytes_accessed=2 * (rows * (cols + width) + cols * width), transcendentals=0
        ),
        name="outer",
    )(order, *left, *right)


def qkv_kernel(near_ref, *refs, count):
    x, parts = refs[:count], refs[count : count + 4]
    cos_ref, sin_ref, out_ref, rows_ref, w_ref, x_scr, w_scr, x_sem, w_sem, out_sem = refs[count + 4 :]
    tok = x[0].shape[0]
    groups, depth, cols = parts[0].shape
    heads, half = out_ref.shape[0], HD // 2
    x_in = [
        pltpu.make_async_copy(x[i], x_scr.at[i * tok : (i + 1) * tok], x_sem.at[i])
        for i in range(count)
    ]
    w_in = [
        pltpu.make_async_copy(
            parts[r].at[g],
            w_scr.at[pl.ds(pl.multiple_of((g * 4 + (near_ref[0] ^ r)) * depth, depth), depth)],
            w_sem.at[r, g],
        )
        for r in range(4)
        for g in range(groups)
    ]
    for c in w_in + x_in:
        c.start()
    for c in w_in + x_in:
        c.wait()
    out = [
        pltpu.make_async_copy(x_scr, rows_ref, out_sem.at[0]),
        pltpu.make_async_copy(w_scr, w_ref, out_sem.at[1]),
    ]
    for c in out:
        c.start()
    group = heads * HD
    for i in range(3):
        y = mxu(x_scr[...], w_scr[:, i * group : (i + 1) * group]).T
        for h in range(heads):
            at = slice(i * HD, (i + 1) * HD)
            a, b = y[h * HD : h * HD + half], y[h * HD + half : (h + 1) * HD]
            if i < 2:
                c, s = cos_ref[...], sin_ref[...]
                a, b = a * c - b * s, b * c + a * s
            out_ref[h, at] = jnp.concatenate([a, b], axis=0).astype(BF16)
    for c in out:
        c.wait()


def qkv_of(near, x, parts, cos, sin):
    count, (tok, width) = len(x), x[0].shape
    groups, depth, cols = parts[0].shape
    heads = cols // (3 * HD)
    return pl.pallas_call(
        functools.partial(qkv_kernel, count=count),
        in_specs=[pl.BlockSpec(memory_space=pltpu.SMEM)] + [ANY] * (count + 4) + [VMEM] * 2,
        out_specs=[VMEM, ANY, ANY],
        out_shape=[
            jax.ShapeDtypeStruct((heads, 3 * HD, count * tok), BF16),
            jax.ShapeDtypeStruct((count * tok, width), BF16),
            jax.ShapeDtypeStruct((width, cols), BF16),
        ],
        scratch_shapes=[
            pltpu.VMEM((count * tok, width), BF16),
            pltpu.VMEM((width, cols), BF16),
            pltpu.SemaphoreType.DMA((count,)),
            pltpu.SemaphoreType.DMA((4, groups)),
            pltpu.SemaphoreType.DMA((2,)),
        ],
        compiler_params=pltpu.CompilerParams(vmem_limit_bytes=60 << 20),
        cost_estimate=pl.CostEstimate(
            flops=2 * count * tok * width * cols,
            bytes_accessed=4 * (count * tok * width + width * cols),
            transcendentals=0,
        ),
        name="qkv",
    )(near, *x, *parts, cos, sin)


def turned_rows(d_ref, d_scr, at, rows):
    heads = d_ref.shape[0]
    for i in range(3):
        for h in range(heads):
            top = (i * heads + h) * HD
            d_scr[top : top + HD] = d_ref[h, i * HD : (i + 1) * HD, at : at + rows]


def input_rows_kernel(d_hbm, w_hbm, out_ref, w_scr, d_scr, t_scr, sem, *, slot):
    rows = out_ref.shape[0]
    d_in = pltpu.make_async_copy(d_hbm.at[:, :, slot * rows : (slot + 1) * rows], d_scr, sem.at[0])
    w_in = pltpu.make_async_copy(w_hbm, w_scr, sem.at[1])
    d_in.start()
    w_in.start()
    d_in.wait()
    turned_rows(d_scr, t_scr, 0, rows)
    d = t_scr[...].T
    w_in.wait()
    out_ref[...] = mxu_nt(d, w_scr[...]).astype(BF16)


def input_rows(dqkv, w, slot, tok):
    width, cols = w.shape
    return pl.pallas_call(
        functools.partial(input_rows_kernel, slot=slot),
        in_specs=[ANY, ANY],
        out_specs=VMEM,
        out_shape=jax.ShapeDtypeStruct((tok, width), BF16),
        scratch_shapes=[
            pltpu.VMEM((width, cols), BF16),
            pltpu.VMEM((*dqkv.shape[:2], tok), BF16),
            pltpu.VMEM((cols, tok), BF16),
            pltpu.SemaphoreType.DMA((2,)),
        ],
        compiler_params=pltpu.CompilerParams(vmem_limit_bytes=60 << 20),
        cost_estimate=pl.CostEstimate(
            flops=2 * tok * width * cols, bytes_accessed=2 * width * cols, transcendentals=0
        ),
        name="input_rows",
    )(dqkv, w)


def heads_back_kernel(near_ref, d_ref, x_hbm, w_hbm, *refs, slots, step):
    count = len(slots)
    give_ref, keep_ref = refs[:2]
    out = refs[2 : 2 + count]
    x_scr, w_scr, d_scr, t_scr, y_scr, o_scr, in_sem, out_sem = refs[2 + count :]
    groups, depth = keep_ref.shape[1:3]
    tok, width = out[0].shape
    x_in = pltpu.make_async_copy(x_hbm, x_scr, in_sem.at[0])
    w_in = pltpu.make_async_copy(w_hbm, w_scr, in_sem.at[1])
    w_in.start()
    x_in.start()
    turned_rows(d_ref, d_scr, 0, d_scr.shape[1])
    t_scr[...] = d_scr[...].T
    w_in.wait()
    sent = []
    for n in range(width // step):
        part = slice(n * step, (n + 1) * step)
        o_scr[:, part] = mxu_nt(t_scr[...], w_scr[part, :]).astype(BF16)
        for i, slot in enumerate(slots):
            sent.append(
                pltpu.make_async_copy(
                    o_scr.at[slot * tok : (slot + 1) * tok, part],
                    out[i].at[:, part],
                    out_sem.at[n, i],
                )
            )
            sent[-1].start()
    x_in.wait()
    tile = 4 * depth
    for g in range(groups):
        y_scr[...] = mxu(d_scr[...], x_scr[:, g * tile : (g + 1) * tile]).astype(BF16).T
        for r in range(4):
            rows = pl.ds(pl.multiple_of((near_ref[0] ^ r) * depth, depth), depth)
            (give_ref if r % 2 else keep_ref)[r // 2, g] = y_scr[rows, :]
    for c in sent:
        c.wait()


def heads_back(near, dqkv, x, w, slots, tok):
    rows, width = x.shape
    cols = w.shape[1]
    depth = HD
    groups = width // (4 * depth)
    step = width // 4
    shape = jax.ShapeDtypeStruct((2, groups, depth, cols), BF16)
    out = pl.pallas_call(
        functools.partial(heads_back_kernel, slots=slots, step=step),
        in_specs=[pl.BlockSpec(memory_space=pltpu.SMEM), VMEM, ANY, ANY],
        out_specs=[VMEM, VMEM] + [ANY] * len(slots),
        out_shape=[shape, shape] + [jax.ShapeDtypeStruct((tok, width), BF16)] * len(slots),
        scratch_shapes=[
            pltpu.VMEM((rows, width), BF16),
            pltpu.VMEM((width, cols), BF16),
            pltpu.VMEM((cols, rows), BF16),
            pltpu.VMEM((rows, cols), BF16),
            pltpu.VMEM((4 * depth, cols), BF16),
            pltpu.VMEM((rows, width), BF16),
            pltpu.SemaphoreType.DMA((2,)),
            pltpu.SemaphoreType.DMA((width // step, len(slots))),
        ],
        compiler_params=pltpu.CompilerParams(vmem_limit_bytes=60 << 20),
        cost_estimate=pl.CostEstimate(
            flops=4 * rows * width * cols,
            bytes_accessed=2 * (2 * width * cols + rows * (2 * width + cols)),
            transcendentals=0,
        ),
        name="heads_back",
    )(near, dqkv, x, w)
    return out[:2], out[2:]


def mid_grad_kernel(
    own_ref, across_ref, ahead_ref, mid_ref, dy_ref, scale_ref, gain_ref, w_hbm, dmid_ref, low_ref, out_ref, w_scr, sem
):
    tiles = sem.shape[0]
    width = mid_ref.shape[1]
    rows = w_scr.shape[0] // tiles
    w_in = [
        pltpu.make_async_copy(w_hbm.at[i * rows : (i + 1) * rows], w_scr.at[i * rows : (i + 1) * rows], sem.at[i])
        for i in range(tiles)
    ]
    for c in w_in:
        c.start()
    dn = own_ref[...].astype(F32) + across_ref[...].astype(F32) + ahead_ref[...].astype(F32)
    mid, scale = mid_ref[...], scale_ref[...]
    scaled = gain_ref[...] * dn
    mean = jnp.sum(scaled * mid, axis=-1, keepdims=True) * (1.0 / width)
    dmid = dy_ref[...].astype(F32) + scale * scaled - mid * (scale * scale * scale * mean)
    dmid_ref[...] = dmid
    low = dmid.astype(BF16)
    low_ref[...] = low
    gain_term = jnp.sum(dn * mid * scale, axis=0, keepdims=True)
    high = gain_term.astype(BF16)
    rest = (gain_term - high.astype(F32)).astype(BF16)
    out_ref[:, HD:] = jnp.zeros((out_ref.shape[0], out_ref.shape[1] - HD, out_ref.shape[2]), BF16)
    for h in range(out_ref.shape[0]):
        at = slice(h * HD, (h + 1) * HD)
        out_ref[h, HD : HD + 1, : 2 * HD] = jnp.concatenate([high[:, at], rest[:, at]], axis=1)
    for i in range(tiles):
        w_in[i].wait()
        v = mxu_nt(w_scr[i * rows : (i + 1) * rows, :], low).astype(BF16)
        for j in range(rows // HD):
            out_ref[i * (rows // HD) + j, :HD] = v[j * HD : (j + 1) * HD]


def mid_grad(terms, mid, dy, scale, gain, w):
    tok, width = mid.shape
    owners = w.shape[0] // HD
    return pl.pallas_call(
        mid_grad_kernel,
        in_specs=[VMEM] * 7 + [ANY],
        out_specs=[VMEM] * 3,
        out_shape=[
            jax.ShapeDtypeStruct((tok, width), F32),
            jax.ShapeDtypeStruct((tok, width), BF16),
            jax.ShapeDtypeStruct((owners, HD + 16, tok), BF16),
        ],
        scratch_shapes=[pltpu.VMEM(w.shape, BF16), pltpu.SemaphoreType.DMA((4,))],
        compiler_params=pltpu.CompilerParams(vmem_limit_bytes=60 << 20),
        cost_estimate=pl.CostEstimate(
            flops=2 * tok * width * w.shape[0], bytes_accessed=2 * width * w.shape[0], transcendentals=0
        ),
        name="mid_grad",
    )(*terms, mid, dy, scale, gain, w)


FAR = ("ctx", "row")
NEAR = ("col", "core")


def swap(v, axis):
    return lax.ppermute(v, axis, [(0, 1), (1, 0)])


def shift(v):
    n = lax.axis_size("ctx")
    return lax.ppermute(v, "ctx", [(i, (i + 1) % n) for i in range(n)])


class Flow:
    def __init__(self, steps):
        self.steps = steps
        self.result = None
        self.pending = next(steps)

    def take(self, got):
        try:
            self.pending = self.steps.send(got)
        except StopIteration as end:
            self.pending, self.result = None, end.value

    def run_on(self):
        self.take(self.pending)


def stage(flows, values=(), then=None):
    got, values = lax.optimization_barrier(([f.pending for f in flows], values))
    if then is not None:
        then(values)
    for f, g in zip(flows, got, strict=True):
        f.take(g)
    return values


def spread(v, slots):
    slots[0, 0] = v
    n = lax.axis_size("ctx")
    for c in range(n - 1):
        slots[c + 1, 0], slots[c, 1] = yield shift(slots[c, 0]), swap(slots[c, 0], "row")
    slots[n - 1, 1] = yield swap(slots[n - 1, 0], "row")
    return slots


def spread_late(v, slots):
    slots[0, 0] = v
    n = lax.axis_size("ctx")
    slots[1, 0] = yield shift(v)
    for c in range(1, n - 2):
        slots[c + 1, 0], slots[c - 1, 1] = yield shift(slots[c, 0]), swap(slots[c - 1, 0], "row")
    slots[n - 1, 0], slots[n - 3, 1], slots[n - 2, 1] = yield (
        shift(slots[n - 2, 0]),
        swap(slots[n - 3, 0], "row"),
        swap(slots[n - 2, 0], "row"),
    )
    slots[n - 1, 1] = yield swap(slots[n - 1, 0], "row")
    return slots


def collect(terms, marks, early=False, open_end=False):
    n = lax.axis_size("ctx")
    across = yield swap(terms[1, 1], "row")
    total = terms[1, 0].astype(F32) + across.astype(F32)
    for c in [*range(2, n), 0]:
        send = total.astype(BF16)
        marks.append(send)
        if early and c == 2:
            ahead, across, last = yield (
                shift(send),
                swap(after(terms[c, 1], send), "row"),
                swap(after(terms[0, 1], send), "row"),
            )
        elif early and c == 0:
            ahead, across = (yield shift(send)), last
        else:
            ahead, across = yield shift(send), swap(after(terms[c, 1], send), "row")
        if open_end and c == 0:
            return terms[0, 0], across, ahead
        total = terms[c, 0].astype(F32) + across.astype(F32) + ahead.astype(F32)
    return total


def reduce_near(send, keep):
    got = yield swap(send, "core")
    (give,) = yield for_column(keep, got, 1)
    across = yield swap(give, "col")
    return keep, got, [across]


def for_column(keep, got, pieces):
    rows = keep.shape[1] // pieces
    return [
        (keep[0, p : p + rows].astype(F32) + got[0, p : p + rows].astype(F32)).astype(BF16)
        for p in range(0, keep.shape[1], rows)
    ]


def add_terms(keep, got, across):
    return keep[1].astype(F32) + got[1].astype(F32) + jnp.concatenate(across, axis=0).astype(F32)


def after(v, first):
    return lax.optimization_barrier((v, first))[0]


def beside(v, tok):
    return jnp.pad(v.reshape(*v.shape[:-1], 1, -1), [(0, 0)] * (v.ndim - 1) + [(0, 15), (0, tok - v.shape[-1])])


def by_side(index, mine, theirs):
    return jnp.where(index == 0, mine, theirs), jnp.where(index == 0, theirs, mine)


def to_near(v, col_at, core_at):
    keep, give = by_side(col_at, v[0], v[1])
    got = yield swap(give, "col")
    both = jnp.stack(by_side(col_at, keep, got))
    keep, give = by_side(core_at, both[:, 0], both[:, 1])
    got = yield swap(give, "core")
    return jnp.stack(by_side(core_at, keep, got), axis=1)


def sum_near(give, keep):
    got = yield swap(give, "core")
    other = (keep[1].astype(F32) + got[1].astype(F32)).astype(BF16)
    across = yield swap(other, "col")
    return keep[0].astype(F32) + got[0].astype(F32) + across.astype(F32)


def gather_heads(send):
    mine = yield lax.all_to_all(send, FAR, split_axis=0, concat_axis=0, tiled=True)
    part = mine.shape[0] // 2
    upper, mine_two = yield swap(mine[:part], "col"), swap(mine, "core")
    lower = yield swap(mine[part:], "col")
    other = jnp.concatenate([upper, lower], axis=0)
    other_two = yield swap(other, "core")
    return mine, mine_two, other, other_two


def per_device_split(
    tokens,
    pair_index,
    gain_attn,
    w_query,
    w_key,
    w_value,
    w_out,
    gain_ffn,
    w_gate,
    w_up,
    w_down,
    cotangent,
):
    n_ctx = lax.axis_size("ctx")
    near = lax.axis_size("col") * lax.axis_size("core")
    far = 2 * n_ctx
    tok, width = tokens.shape
    own_in = w_query.shape[0]
    ctx_at, row_at, col_at, core_at = (lax.axis_index(a) for a in ("ctx", "row", "col", "core"))
    near_at = col_at * lax.axis_size("core") + core_at
    blk = near * tok
    rows_here = far * tok
    group = near * HD

    slots = jnp.arange(far, dtype=jnp.int32)
    ctxs = jnp.arange(n_ctx, dtype=jnp.int32)

    def block_of(ctx, row):
        pair = jnp.sum(jnp.where(ctx[:, None] == ctxs[None, :], pair_index[None, :], 0), axis=1)
        return jnp.where(row == 0, pair, far - 1 - pair)

    def place_of_block(block):
        return jnp.sum(jnp.where(block[None, :] == slots[:, None], slots[None, :], 0), axis=1)

    slot_block = block_of((ctx_at - slots % n_ctx + n_ctx) % n_ctx, row_at ^ (slots // n_ctx))
    places = jnp.stack([place_of_block(slot_block), place_of_block(block_of(slots // 2, slots % 2))])
    freq = jnp.exp(jnp.arange(HD // 2, dtype=F32) * (-2.0 * math.log(THETA) / HD))
    token_places = (
        slot_block[:, None] * blk + near_at * tok + jnp.arange(tok, dtype=jnp.int32)[None, :]
    ).reshape(rows_here)
    angle = freq[:, None] * token_places.astype(F32)[None, :]
    cosine, sine = jnp.cos(angle), jnp.sin(angle)
    seq_angle = freq[:, None] * jnp.arange(far * blk, dtype=jnp.int32).astype(F32)[None, :]
    seq_cos, seq_sin = jnp.cos(seq_angle), jnp.sin(seq_angle)

    gain_one = gain_attn.astype(F32)[:, None]
    send = jnp.concatenate(
        [
            (w.astype(F32) * gain_one).astype(BF16).reshape(own_in, far, group)
            for w in (w_query, w_key, w_value)
        ],
        axis=2,
    ).transpose(1, 0, 2)
    x32 = tokens.astype(F32)
    scale_one = lax.rsqrt(jnp.mean(x32 * x32, axis=-1, keepdims=True) + EPS)
    gate_w = lax.all_gather(w_gate, NEAR, axis=0, tiled=True)

    one_flow = Flow(spread((x32 * scale_one).astype(BF16), {}))
    heads_flow = Flow(gather_heads(send))
    w_out = stage([one_flow, heads_flow], w_out)
    out_w = lax.all_gather(w_out, FAR + NEAR, axis=0, tiled=True)
    for _ in range(n_ctx - 3):
        cosine, sine = stage([one_flow, heads_flow], (cosine, sine))
    dy_low = stage([one_flow, heads_flow], cotangent)
    dy_by = {}
    dy_flow = Flow(spread_late(dy_low, dy_by))
    w_rest = stage([one_flow, heads_flow], jnp.concatenate([w_up, w_down], axis=0))
    dy_flow.run_on()
    rest_w = lax.all_gather(w_rest, NEAR, axis=0, tiled=True)
    slot_names = [(c, r) for r in range(2) for c in range(n_ctx)]
    qkv, rows_one, w_heads = qkv_of(
        near_at.reshape(1),
        [one_flow.result[k] for k in slot_names],
        heads_flow.result,
        cosine,
        sine,
    )
    qkv_head, gate_w, seq_cos, seq_sin = stage(
        [dy_flow],
        (
            lax.all_to_all(qkv, NEAR, split_axis=0, concat_axis=0, tiled=True),
            gate_w,
            seq_cos,
            seq_sin,
        ),
    )
    (attn_head, o32, lse, seq), out_w = stage(
        [dy_flow], (attn_fwd(places, qkv_head, beside(gain_ffn, tok), far), out_w)
    )
    attn = stage(
        [dy_flow], lax.all_to_all(attn_head, FAR + NEAR, split_axis=0, concat_axis=0, tiled=True)
    )
    gain_two = attn[:, HD, :own_in].reshape(1, width).astype(F32)
    attn_all = attn[:, :HD]
    attn = attn_all.reshape(width, tok)

    mid = x32 + jnp.einsum("et,ed->td", attn, out_w, preferred_element_type=F32)
    scale_two = lax.rsqrt(jnp.mean(mid * mid, axis=-1, keepdims=True) + EPS)
    normed_two = (mid * scale_two * gain_two).astype(BF16)
    side_flow = Flow(
        to_near(attn_all.reshape(far, 2, 2, HD, tok).transpose(1, 2, 0, 3, 4), col_at, core_at)
    )

    two, dn_by, br_by, kept = {}, {}, {}, []
    two_flow = Flow(spread(normed_two, two))

    def feed(cs, first=()):
        names = [(c, r) for c in cs for r in range(2)]
        rows = after([two[k] for k in names], first)
        dn, br, lefts = ffn(rows, [dy_by[k] for k in names], gate_w, rest_w, near)
        return dict(zip(names, dn, strict=True)), dict(zip(names, br, strict=True)), lefts

    def fed(results):
        dn, br, lefts = results
        dn_by.update(dn)
        br_by.update(br)
        kept.append(lefts)

    stage([two_flow])
    stage([two_flow], feed([0]), fed)
    for c in range(1, n_ctx - 2):
        stage([two_flow], feed([c]), fed)
    marks = []
    dn_flow = Flow(collect(dn_by, marks, open_end=True))
    stage([two_flow, dn_flow, side_flow], feed([n_ctx - 2]), fed)
    last = feed([n_ctx - 1], marks[-1])
    stage([dn_flow, side_flow], last, fed)
    names = [(c, r) for c in range(n_ctx) for r in range(2)]
    two_rows, dy_rows = [two[k] for k in names], [dy_by[k] for k in names]
    tiles = near_at ^ jnp.array([3, 1, 2, 0], jnp.int32)
    lefts = [[k[i] for k in kept] for i in range(3)]
    for _ in range(n_ctx - 4):
        stage([dn_flow])
    gate_terms = outer(tiles, *after((lefts[1], two_rows), marks[-1]))
    gate_flow = Flow(reduce_near(*stage([dn_flow], gate_terms)))
    up_terms = outer(tiles, *after((lefts[2], two_rows), marks[-1]))
    up_terms, br_by = stage([dn_flow, gate_flow], (up_terms, br_by))
    up_send, up_keep = up_terms
    dmid, dmid_low, dattn = mid_grad(dn_flow.result, mid, cotangent, scale_two, gain_two, out_w)
    dmid_near = lax.all_gather(dmid_low, NEAR, axis=0, tiled=True)
    br_marks = []
    br_flow = Flow(collect(br_by, br_marks, early=True, open_end=True))
    down_terms = outer(tiles, *after((lefts[0], dy_rows), dattn))
    gate_flow.pending = after(gate_flow.pending, dattn)
    attn_side = after(side_flow.result, dattn).transpose(2, 3, 0, 1, 4).reshape(far, HD, blk)
    out_term = jnp.einsum("gft,td->gfd", attn_side, dmid_near, preferred_element_type=F32)
    dattn_head, down_terms, out_term, up_got = stage(
        [gate_flow, br_flow],
        (
            lax.all_to_all(dattn, FAR + NEAR, split_axis=0, concat_axis=0, tiled=True),
            down_terms,
            out_term.astype(BF16),
            swap(up_send, "core"),
        ),
    )
    out_grad = lax.psum_scatter(
        out_term.reshape(far * HD, width), FAR, scatter_dimension=0, tiled=True
    )
    down_send, down_keep = down_terms
    gain_parts = dattn_head[:, HD, : 2 * own_in].astype(F32)
    dqkv_head, down_got = stage(
        [gate_flow, br_flow],
        (
            attn_bwd(places, seq, o32, lse, dattn_head, seq_cos, seq_sin, far),
            swap(down_send, "core"),
        ),
    )
    exchange = lax.all_to_all(dqkv_head, NEAR, split_axis=0, concat_axis=0, tiled=True)
    up_give = for_column(*after((up_keep, up_got), br_marks[-1]), 2)
    (down_keep, down_got) = after((down_keep, down_got), br_marks[-1])
    dqkv, up_give, down_give = stage(
        [br_flow], (exchange, up_give, for_column(down_keep, down_got, 1)[0])
    )
    dx = {(1, 1): input_rows(dqkv, w_heads, slot_names.index((1, 1)), tok)}
    dx_flow = Flow(collect(dx, marks))
    up_first, up_second = up_give
    rest = [i for i in range(far) if slot_names[i] != (1, 1)]

    def add_rows(values):
        dx.update({slot_names[i]: v for i, v in zip(rest, values[1], strict=True)})

    heads_terms, _, up_first = stage(
        [dx_flow, br_flow],
        (*heads_back(near_at.reshape(1), after(dqkv, dx[1, 1]), rows_one, w_heads, rest, tok), swap(up_first, "col")),
        add_rows,
    )
    heads_flow = Flow(sum_near(*heads_terms))
    stage([heads_flow])
    gate_terms, out_grad, up_second = stage(
        [dx_flow, heads_flow], (gate_flow.result, out_grad, up_second)
    )
    back = lax.all_to_all(
        heads_flow.result.astype(BF16), FAR, split_axis=0, concat_axis=0, tiled=True
    )
    gate_terms, down_give, up_second, branch = stage(
        [dx_flow], (gate_terms, down_give, swap(up_second, "col"), br_flow.result)
    )
    up_terms = up_keep, up_got, [up_first, up_second]
    gate_terms, up_terms, branch = after((gate_terms, up_terms, branch), marks[-1])
    gate_grad, up_grad = add_terms(*gate_terms), add_terms(*up_terms)
    down_across = stage([dx_flow], swap(down_give, "col"))
    down_grad = add_terms(down_keep, down_got, [down_across])
    scaled_one = dx_flow.result
    input_grad = (
        dmid
        + scale_one * scaled_one
        - x32 * scale_one**3 * jnp.mean(scaled_one * x32, axis=-1, keepdims=True)
    )
    back, input_grad, down_grad = lax.optimization_barrier((back, input_grad, down_grad))
    back = back.astype(F32)
    raw = [
        back[:, :, i * group : (i + 1) * group].transpose(1, 0, 2).reshape(own_in, -1)
        for i in range(3)
    ]
    gain_attn_grad = sum(
        jnp.sum(w.astype(F32) * g, axis=1)
        for w, g in zip((w_query, w_key, w_value), raw, strict=True)
    )
    query_grad, key_grad, value_grad = (g * gain_one for g in raw)
    gain_ffn_grad = jnp.sum(gain_parts[:, :own_in] + gain_parts[:, own_in:], axis=0)
    return (
        (mid + sum(v.astype(F32) for v in branch)).astype(BF16),
        input_grad,
        gain_attn_grad,
        query_grad,
        key_grad,
        value_grad,
        out_grad.astype(F32),
        gain_ffn_grad,
        gate_grad,
        up_grad,
        down_grad,
    )


def solution(mesh):
    n_ctx, n_fsdp = mesh.shape["ctx"], mesh.shape["fsdp"]

    def step(*args):
        if n_fsdp == 8 and n_ctx == 4 and n_ctx * n_fsdp * HD == args[3].shape[1]:
            body, axes = per_device_split, FAR + NEAR
            over = Mesh(np.asarray(mesh.devices).reshape(n_ctx, 2, 2, 2), axes)
        else:
            body, axes, over = per_device_any, ("ctx", "fsdp"), mesh
        rows, line = P(axes, None), P(axes)
        return jax.shard_map(
            body,
            mesh=over,
            in_specs=(rows, P(), line, rows, rows, rows, rows, line, rows, rows, rows, rows),
            out_specs=(rows, rows, line, rows, rows, rows, rows, line, rows, rows, rows),
            check_vma=False,
        )(*args)

    return step
```

```python
import functools
import math

import jax
import jax.numpy as jnp
import numpy as np
from jax import lax
from jax.experimental import pallas as pl
from jax.experimental.pallas import tpu as pltpu
from jax.sharding import Mesh
from jax.sharding import PartitionSpec as P

HD = 64


EPS = 1e-05
THETA = 130000.0


def place_of(rows, pair_index, n_groups, blk):
    group = rows // (2 * blk)
    within = rows % (2 * blk)
    match = group[:, None] == jnp.arange(n_groups, dtype=jnp.int32)[None, :]
    pair = jnp.sum(jnp.where(match, pair_index[None, :], 0), axis=1)
    block = jnp.where(within < blk, pair, 2 * n_groups - 1 - pair)
    return block * blk + within % blk


def tables(places, head_dim):
    freq = jnp.exp(
        jnp.arange(head_dim // 2, dtype=jnp.float32) * (-2.0 * math.log(THETA) / head_dim)
    )
    angle = places.astype(jnp.float32)[:, None] * freq[None, :]
    return (jnp.cos(angle), jnp.sin(angle))


def rotate(flat, cosine, sine, head_dim):
    rows = flat.shape[0]
    split = flat.reshape(rows, -1, head_dim)
    half = head_dim // 2
    first = split[..., :half]
    second = split[..., half:]
    cos_b = cosine[:, None, :]
    sin_b = sine[:, None, :]
    out = jnp.concatenate([first * cos_b - second * sin_b, second * cos_b + first * sin_b], axis=-1)
    return out.reshape(rows, -1)


def silu_parts(gate):
    sig = jax.nn.sigmoid(gate)
    return (gate * sig, sig * (1.0 + gate * (1.0 - sig)))


def rows_by(left, right):
    return jnp.einsum("td,fd->tf", left, right, preferred_element_type=jnp.float32)


def outer_sum(left, right):
    return jnp.einsum("tf,td->fd", left, right, preferred_element_type=jnp.float32)


def per_device_any(
    tokens,
    pair_index,
    gain_attn,
    w_query,
    w_key,
    w_value,
    w_out,
    gain_ffn,
    w_gate,
    w_up,
    w_down,
    cotangent,
):
    f32 = jnp.float32
    bf16 = jnp.bfloat16
    n_ctx = lax.axis_size("ctx")
    n_fsdp = lax.axis_size("fsdp")
    tok = tokens.shape[0]
    group_rows = tok * n_fsdp
    blk = group_rows // 2
    total = group_rows * n_ctx
    ctx_index = lax.axis_index("ctx")
    fsdp_index = lax.axis_index("fsdp")
    local_rows = (ctx_index * n_fsdp + fsdp_index) * tok + jnp.arange(tok, dtype=jnp.int32)
    local_places = place_of(local_rows, pair_index, n_ctx, blk)
    group_places = place_of(
        ctx_index * group_rows + jnp.arange(group_rows, dtype=jnp.int32), pair_index, n_ctx, blk
    )
    key_places = place_of(jnp.arange(total, dtype=jnp.int32), pair_index, n_ctx, blk)
    group_cos, group_sin = tables(group_places, HD)
    query_full, key_full, value_full, out_full, gain_one, gain_two = (
        lax.all_gather(w_query, ("ctx", "fsdp"), axis=0, tiled=True),
        lax.all_gather(w_key, ("ctx", "fsdp"), axis=0, tiled=True),
        lax.all_gather(w_value, ("ctx", "fsdp"), axis=0, tiled=True),
        lax.all_gather(w_out, ("ctx", "fsdp"), axis=0, tiled=True),
        lax.all_gather(gain_attn, ("ctx", "fsdp"), axis=0, tiled=True),
        lax.all_gather(gain_ffn, ("ctx", "fsdp"), axis=0, tiled=True),
    )
    gain_one = gain_one.astype(f32)
    gain_two = gain_two.astype(f32)
    x32 = tokens.astype(f32)
    scale_one = lax.rsqrt(jnp.mean(x32 * x32, axis=-1, keepdims=True) + EPS)
    normed_one = (x32 * scale_one * gain_one).astype(bf16)
    cosine, sine = tables(local_places, HD)
    query = rotate(
        jnp.dot(normed_one, query_full, preferred_element_type=f32), cosine, sine, HD
    ).astype(bf16)
    key = rotate(
        jnp.dot(normed_one, key_full, preferred_element_type=f32), cosine, sine, HD
    ).astype(bf16)
    value = jnp.dot(normed_one, value_full, preferred_element_type=f32).astype(bf16)
    query_heads, key_heads, value_heads = (
        lax.all_to_all(query, "fsdp", split_axis=1, concat_axis=0, tiled=True),
        lax.all_to_all(key, "fsdp", split_axis=1, concat_axis=0, tiled=True),
        lax.all_to_all(value, "fsdp", split_axis=1, concat_axis=0, tiled=True),
    )
    key_all, value_all = (
        lax.all_gather(key_heads, "ctx", axis=0, tiled=True),
        lax.all_gather(value_heads, "ctx", axis=0, tiled=True),
    )
    local_width = query_heads.shape[1]
    heads_here = local_width // HD
    scale = HD ** (-0.5)
    query_parts = query_heads.reshape(2, blk, heads_here, HD)
    query_place_tiles = group_places.reshape(2, blk)
    key_tiles = key_all.reshape(2 * n_ctx, blk, heads_here, HD)
    value_tiles = value_all.reshape(2 * n_ctx, blk, heads_here, HD)
    key_place_tiles = key_places.reshape(2 * n_ctx, blk)

    def tile_scores(slot, keys, k_place):
        raw = (
            jnp.einsum("qhd,khd->hqk", query_parts[slot], keys, preferred_element_type=f32) * scale
        )
        keep = k_place[None, None, :] <= query_place_tiles[slot][None, :, None]
        return jnp.where(keep, raw, -1e30)

    def is_live(slot, k_place):
        return jnp.min(k_place) <= jnp.max(query_place_tiles[slot])

    def first_pass(carry, tile):
        keys, k_place = tile
        highs, totals = carry
        new_highs = []
        new_totals = []
        for slot in range(2):

            def first_update(high, summed):
                masked = tile_scores(slot, keys, k_place)
                fresh = jnp.maximum(high, jnp.max(masked, axis=-1))
                summed = summed * jnp.exp(high - fresh) + jnp.sum(
                    jnp.exp(masked - fresh[..., None]), axis=-1
                )
                return (fresh, summed)

            def first_leave(high, summed):
                return (high, summed)

            high, summed = lax.cond(
                is_live(slot, k_place), first_update, first_leave, highs[slot], totals[slot]
            )
            new_highs.append(high)
            new_totals.append(summed)
        return ((jnp.stack(new_highs), jnp.stack(new_totals)), None)

    start_high = jnp.full((2, heads_here, blk), -1e30, f32)
    start_total = jnp.zeros((2, heads_here, blk), f32)
    (highs, totals), unused = lax.scan(
        first_pass, (start_high, start_total), (key_tiles, key_place_tiles)
    )
    log_total = highs + jnp.log(totals)

    def second_pass(carry, tile):
        keys, values, k_place = tile
        outs = []
        for slot in range(2):

            def second_update(acc):
                masked = tile_scores(slot, keys, k_place)
                prob_low = jnp.exp(masked - log_total[slot][..., None]).astype(bf16)
                return acc + jnp.einsum(
                    "hqk,khd->qhd", prob_low, values, preferred_element_type=f32
                )

            def second_leave(acc):
                return acc

            outs.append(lax.cond(is_live(slot, k_place), second_update, second_leave, carry[slot]))
        return (jnp.stack(outs), None)

    acc_start = jnp.zeros((2, blk, heads_here, HD), f32)
    attn_acc, unused = lax.scan(second_pass, acc_start, (key_tiles, value_tiles, key_place_tiles))
    attn32 = attn_acc.reshape(group_rows, local_width)
    attn_tokens = lax.all_to_all(
        attn32.astype(bf16), "fsdp", split_axis=0, concat_axis=1, tiled=True
    )
    mid = x32 + jnp.dot(attn_tokens, out_full, preferred_element_type=f32)
    scale_two = lax.rsqrt(jnp.mean(mid * mid, axis=-1, keepdims=True) + EPS)
    normed_two = (mid * scale_two * gain_two).astype(bf16)
    dy = cotangent.astype(f32)
    dy_low = dy.astype(bf16)
    gate_local, up_local, down_local = (
        lax.all_gather(w_gate, "ctx", axis=0, tiled=True),
        lax.all_gather(w_up, "ctx", axis=0, tiled=True),
        lax.all_gather(w_down, "ctx", axis=0, tiled=True),
    )
    rows_all = lax.all_gather(normed_two, "fsdp", axis=0, tiled=True)
    gate_all = rows_by(rows_all, gate_local)
    up_all = rows_by(rows_all, up_local)
    silu_all, unused_slope = silu_parts(gate_all)
    hidden_all = (silu_all * up_all).astype(bf16)
    branch = lax.psum_scatter(
        jnp.dot(hidden_all, down_local, preferred_element_type=f32).astype(jnp.bfloat16),
        "fsdp",
        scatter_dimension=0,
        tiled=True,
    ).astype(jnp.float32)
    block_out = (mid + branch).astype(bf16)
    grad_rows_all = lax.all_gather(dy_low, "fsdp", axis=0, tiled=True)
    dhidden = rows_by(grad_rows_all, down_local)
    silu_val, slope = silu_parts(gate_all)
    dgate = (dhidden * up_all * slope).astype(bf16)
    dup = (dhidden * silu_val).astype(bf16)
    gate_term = outer_sum(dgate, rows_all)
    up_term = outer_sum(dup, rows_all)
    down_term = outer_sum(hidden_all, grad_rows_all)
    gate_grad, up_grad, down_grad = (
        lax.psum_scatter(
            gate_term.astype(jnp.bfloat16), "ctx", scatter_dimension=0, tiled=True
        ).astype(jnp.float32),
        lax.psum_scatter(
            up_term.astype(jnp.bfloat16), "ctx", scatter_dimension=0, tiled=True
        ).astype(jnp.float32),
        lax.psum_scatter(
            down_term.astype(jnp.bfloat16), "ctx", scatter_dimension=0, tiled=True
        ).astype(jnp.float32),
    )
    dnormed_two = lax.psum_scatter(
        (
            jnp.dot(dgate, gate_local, preferred_element_type=f32)
            + jnp.dot(dup, up_local, preferred_element_type=f32)
        ).astype(jnp.bfloat16),
        "fsdp",
        scatter_dimension=0,
        tiled=True,
    ).astype(jnp.float32)
    gain_two_term = jnp.sum(dnormed_two * mid * scale_two, axis=0)
    scaled_two = gain_two * dnormed_two
    dmid = (
        dy
        + scale_two * scaled_two
        - mid * scale_two**3 * jnp.mean(scaled_two * mid, axis=-1, keepdims=True)
    )
    dmid_low = dmid.astype(bf16)
    out_term = jnp.einsum("td,te->de", attn_tokens, dmid_low, preferred_element_type=f32)
    dattn = jnp.einsum("te,de->td", dmid_low, out_full, preferred_element_type=f32).astype(bf16)
    dattn_heads = lax.all_to_all(dattn, "fsdp", split_axis=1, concat_axis=0, tiled=True)
    delta = jnp.sum((dattn_heads.astype(f32) * attn32).reshape(group_rows, heads_here, HD), axis=-1)
    delta_tiles = delta.reshape(2, blk, heads_here).transpose(0, 2, 1)
    grad_parts = dattn_heads.reshape(2, blk, heads_here, HD)

    def back_pass(carry, tile):
        keys, values, k_place = tile
        key_acc = jnp.zeros((blk, heads_here, HD), f32)
        value_acc = jnp.zeros((blk, heads_here, HD), f32)
        new_query = []
        for slot in range(2):

            def back_update(q_acc, k_acc, v_acc):
                masked = tile_scores(slot, keys, k_place)
                prob = jnp.exp(masked - log_total[slot][..., None])
                prob_low = prob.astype(bf16)
                dprob = jnp.einsum(
                    "qhd,khd->hqk", grad_parts[slot], values, preferred_element_type=f32
                )
                dscore = (prob * (dprob - delta_tiles[slot][..., None])).astype(bf16)
                q_acc = (
                    q_acc
                    + jnp.einsum("hqk,khd->qhd", dscore, keys, preferred_element_type=f32) * scale
                )
                k_acc = (
                    k_acc
                    + jnp.einsum(
                        "hqk,qhd->khd", dscore, query_parts[slot], preferred_element_type=f32
                    )
                    * scale
                )
                v_acc = v_acc + jnp.einsum(
                    "hqk,qhd->khd", prob_low, grad_parts[slot], preferred_element_type=f32
                )
                return (q_acc, k_acc, v_acc)

            def back_leave(q_acc, k_acc, v_acc):
                return (q_acc, k_acc, v_acc)

            q_acc, key_acc, value_acc = lax.cond(
                is_live(slot, k_place), back_update, back_leave, carry[slot], key_acc, value_acc
            )
            new_query.append(q_acc)
        return (jnp.stack(new_query), (key_acc, value_acc))

    dquery_start = jnp.zeros((2, blk, heads_here, HD), f32)
    dquery_acc, (dkey_tiles, dvalue_tiles) = lax.scan(
        back_pass, dquery_start, (key_tiles, value_tiles, key_place_tiles)
    )
    dkey_all = dkey_tiles.reshape(total, local_width)
    dvalue_all = dvalue_tiles.reshape(total, local_width)
    dkey_own, dvalue_own = (
        lax.psum_scatter(
            dkey_all.astype(jnp.bfloat16), "ctx", scatter_dimension=0, tiled=True
        ).astype(jnp.float32),
        lax.psum_scatter(
            dvalue_all.astype(jnp.bfloat16), "ctx", scatter_dimension=0, tiled=True
        ).astype(jnp.float32),
    )
    dquery_low = rotate(
        dquery_acc.reshape(group_rows, local_width), group_cos, -group_sin, HD
    ).astype(bf16)
    dkey_low = rotate(dkey_own, group_cos, -group_sin, HD).astype(bf16)
    dvalue_low = dvalue_own.astype(bf16)
    dquery_tok, dkey_tok, dvalue_tok = (
        lax.all_to_all(dquery_low, "fsdp", split_axis=0, concat_axis=1, tiled=True),
        lax.all_to_all(dkey_low, "fsdp", split_axis=0, concat_axis=1, tiled=True),
        lax.all_to_all(dvalue_low, "fsdp", split_axis=0, concat_axis=1, tiled=True),
    )
    dnormed_one = (
        jnp.einsum("te,de->td", dquery_tok, query_full, preferred_element_type=f32)
        + jnp.einsum("te,de->td", dkey_tok, key_full, preferred_element_type=f32)
        + jnp.einsum("te,de->td", dvalue_tok, value_full, preferred_element_type=f32)
    )
    query_term = jnp.einsum("td,te->de", normed_one, dquery_tok, preferred_element_type=f32)
    key_term = jnp.einsum("td,te->de", normed_one, dkey_tok, preferred_element_type=f32)
    value_term = jnp.einsum("td,te->de", normed_one, dvalue_tok, preferred_element_type=f32)
    gain_one_term = jnp.sum(dnormed_one * x32 * scale_one, axis=0)
    scaled_one = gain_one * dnormed_one
    input_grad = (
        dmid
        + scale_one * scaled_one
        - x32 * scale_one**3 * jnp.mean(scaled_one * x32, axis=-1, keepdims=True)
    )
    query_grad, key_grad, value_grad, out_grad, gain_attn_grad, gain_ffn_grad = (
        lax.psum_scatter(query_term, ("ctx", "fsdp"), scatter_dimension=0, tiled=True),
        lax.psum_scatter(key_term, ("ctx", "fsdp"), scatter_dimension=0, tiled=True),
        lax.psum_scatter(value_term, ("ctx", "fsdp"), scatter_dimension=0, tiled=True),
        lax.psum_scatter(out_term, ("ctx", "fsdp"), scatter_dimension=0, tiled=True),
        lax.psum_scatter(gain_one_term, ("ctx", "fsdp"), scatter_dimension=0, tiled=True),
        lax.psum_scatter(gain_two_term, ("ctx", "fsdp"), scatter_dimension=0, tiled=True),
    )
    return (
        block_out,
        input_grad,
        gain_attn_grad,
        query_grad,
        key_grad,
        value_grad,
        out_grad,
        gain_ffn_grad,
        gate_grad,
        up_grad,
        down_grad,
    )


BF16 = jnp.bfloat16
F32 = jnp.float32
LOG2E = math.log2(math.e)
VMEM = pl.BlockSpec(memory_space=pltpu.VMEM)
ANY = pl.BlockSpec(memory_space=pl.ANY)


def mxu(a, b):
    return jnp.dot(a, b, preferred_element_type=F32)


def causal(blk):
    row = lax.broadcasted_iota(jnp.int32, (blk, blk), 0)
    col = lax.broadcasted_iota(jnp.int32, (blk, blk), 1)
    return row <= col


def attn_fwd_kernel(
    place_ref,
    qkv_ref,
    extra_ref,
    out_ref,
    o32_hbm,
    lse_ref,
    seq_hbm,
    seq_ref,
    o32_ref,
    seq_sem,
    o32_sem,
    k_scr,
    m_scr,
    l_scr,
    acc_scr,
    *,
    blocks,
    width,
):
    pieces = qkv_ref.shape[0]
    blk = pieces * width
    coef = LOG2E * HD**-0.5
    for s in range(blocks):
        at = pl.multiple_of(place_ref[0, s] * width, width)
        for j in range(pieces):
            lo = s * blk + j * width
            piece = qkv_ref[j, :, pl.ds(at, width)]
            seq_ref[:, lo : lo + width] = piece
            k_scr[lo : lo + width, :] = piece[HD : 2 * HD].T

    leaving = [pltpu.make_async_copy(seq_ref, seq_hbm, seq_sem)]
    leaving[0].start()

    def tile(kb, q_t, masked, wide=1):
        keys = pl.ds(pl.multiple_of(kb * blk, blk), wide * blk)
        score = mxu(k_scr[keys, :], q_t) * coef
        if masked:
            score = jnp.where(causal(blk), score, -1e30)
        old = m_scr[...]
        new = jnp.maximum(old, jnp.max(score, axis=0, keepdims=True))
        p = jnp.exp2(score - new)
        fade = jnp.exp2(old - new)
        m_scr[...] = new
        l_scr[...] = l_scr[...] * fade + jnp.sum(p, axis=0, keepdims=True)
        acc_scr[...] = acc_scr[...] * fade + mxu(seq_ref[2 * HD :, keys], p.astype(BF16))

    for qb in range(blocks):
        lo = qb * blk
        q_t = seq_ref[:HD, lo : lo + blk]
        m_scr[...] = jnp.full_like(m_scr, -1e30)
        l_scr[...] = jnp.zeros_like(l_scr)
        acc_scr[...] = jnp.zeros_like(acc_scr)
        tile(qb, q_t, True)
        kb = 0
        while kb < qb:
            wide = min(4, qb - kb)
            tile(kb, q_t, False, wide)
            kb += wide

        o = acc_scr[...] / l_scr[...]
        o32_ref[:, lo : lo + blk] = o
        leaving.append(
            pltpu.make_async_copy(
                o32_ref.at[:, lo : lo + blk], o32_hbm.at[:, lo : lo + blk], o32_sem.at[qb]
            )
        )
        leaving[-1].start()
        lse_ref[:, lo : lo + blk] = m_scr[...] + jnp.log2(l_scr[...])
        low = o.astype(BF16)
        for j in range(pieces):
            owner = place_ref[1, qb] * pieces + j
            out_ref[owner, :HD] = low[:, j * width : (j + 1) * width]
            out_ref[owner, HD:] = extra_ref[...]
    for c in leaving:
        c.wait()


def attn_fwd(place, qkv, extra, blocks):
    pieces, _, cols = qkv.shape
    total = pieces * cols
    blk = total // blocks
    return pl.pallas_call(
        functools.partial(attn_fwd_kernel, blocks=blocks, width=cols // blocks),
        out_shape=(
            jax.ShapeDtypeStruct((blocks * pieces, HD + extra.shape[0], cols // blocks), BF16),
            jax.ShapeDtypeStruct((HD, total), F32),
            jax.ShapeDtypeStruct((1, total), F32),
            jax.ShapeDtypeStruct((3 * HD, total), BF16),
        ),
        in_specs=[pl.BlockSpec(memory_space=pltpu.SMEM), VMEM, VMEM],
        out_specs=(VMEM, ANY, VMEM, ANY),
        scratch_shapes=[
            pltpu.VMEM((3 * HD, total), BF16),
            pltpu.VMEM((HD, total), F32),
            pltpu.SemaphoreType.DMA,
            pltpu.SemaphoreType.DMA((blocks,)),
            pltpu.VMEM((total, HD), BF16),
            pltpu.VMEM((1, blk), F32),
            pltpu.VMEM((1, blk), F32),
            pltpu.VMEM((HD, blk), F32),
        ],
        compiler_params=pltpu.CompilerParams(vmem_limit_bytes=60 << 20),
        cost_estimate=pl.CostEstimate(
            flops=8 * total * total * HD, bytes_accessed=8 << 20, transcendentals=total * total // 2
        ),
        name="attn_fwd",
    )(place, qkv, extra)


def attn_bwd_kernel(
    place_ref,
    seq_hbm,
    o32_hbm,
    lse_ref,
    do_ref,
    cos_hbm,
    sin_hbm,
    out_ref,
    seq_ref,
    o32_ref,
    cos_ref,
    sin_ref,
    in_sem,
    q_scr,
    k_scr,
    v_scr,
    do_scr,
    dot_scr,
    delta_scr,
    dq_scr,
    dk_scr,
    dv_scr,
    *,
    blocks,
    width,
):
    pieces = out_ref.shape[0]
    blk = pieces * width
    scale = HD**-0.5
    coef = LOG2E * scale
    half = HD // 2
    arriving = [
        pltpu.make_async_copy(src, dst, in_sem.at[i])
        for i, (src, dst) in enumerate(
            ((seq_hbm, seq_ref), (o32_hbm, o32_ref), (cos_hbm, cos_ref), (sin_hbm, sin_ref))
        )
    ]
    for c in arriving:
        c.start()
    for c in arriving[:2]:
        c.wait()
    for s in range(blocks):
        for j in range(pieces):
            lo = s * blk + j * width
            piece = do_ref[place_ref[1, s] * pieces + j, :HD]
            dot_scr[:, lo : lo + width] = piece
            do_scr[lo : lo + width, :] = piece.T
            delta_scr[:, lo : lo + width] = jnp.sum(
                piece.astype(F32) * o32_ref[:, lo : lo + width], axis=0, keepdims=True
            )
            q_scr[lo : lo + width, :] = seq_ref[:HD, lo : lo + width].T
            k_scr[lo : lo + width, :] = seq_ref[HD : 2 * HD, lo : lo + width].T
            v_scr[lo : lo + width, :] = seq_ref[2 * HD :, lo : lo + width].T
    dq_scr[...] = jnp.zeros_like(dq_scr)
    for c in arriving[2:]:
        c.wait()

    def turn_back(v, s):
        c = cos_ref[:, s * blk : (s + 1) * blk]
        n = sin_ref[:, s * blk : (s + 1) * blk]
        a, b = v[:half], v[half:]
        return jnp.concatenate([a * c + b * n, b * c - a * n], axis=0).astype(BF16)

    def put(v, s, row):
        at = pl.multiple_of(place_ref[0, s] * width, width)
        for j in range(pieces):
            out_ref[j, row * HD : (row + 1) * HD, pl.ds(at, width)] = v[:, j * width : (j + 1) * width]

    for kb in range(blocks):
        lo = kb * blk
        k = k_scr[lo : lo + blk, :]
        v = v_scr[lo : lo + blk, :]
        k_t = seq_ref[HD : 2 * HD, lo : lo + blk]

        def tile(qb, masked, wide=1):
            here = pl.ds(pl.multiple_of(qb * blk, blk), wide * blk)
            p = jnp.exp2(mxu(k, seq_ref[:HD, here]) * coef - lse_ref[:, here])
            if masked:
                p = jnp.where(causal(blk), p, 0.0)
            dp = mxu(v, dot_scr[:, here])
            ds = (p * (dp - delta_scr[:, here])).astype(BF16)
            dq_scr[:, here] += mxu(k_t, ds)
            return mxu(ds, q_scr[here, :]), mxu(p.astype(BF16), do_scr[here, :])

        dk_scr[...], dv_scr[...] = tile(kb, True)

        def add_tile(qb, wide):
            dk, dv = tile(qb, False, wide)
            dk_scr[...] += dk
            dv_scr[...] += dv

        qb = kb + 1
        while qb < blocks:
            wide = min(2, blocks - qb)
            add_tile(qb, wide)
            qb += wide

        put(turn_back(dq_scr[:, lo : lo + blk] * scale, kb), kb, 0)
        put(turn_back((dk_scr[...] * scale).T, kb), kb, 1)
        put(dv_scr[...].T.astype(BF16), kb, 2)


def attn_bwd(place, seq, o32, lse, do, cos, sin, blocks):
    pieces, width = do.shape[0] // blocks, do.shape[2]
    cols, total, blk = blocks * width, seq.shape[1], pieces * width
    return pl.pallas_call(
        functools.partial(attn_bwd_kernel, blocks=blocks, width=width),
        out_shape=jax.ShapeDtypeStruct((pieces, 3 * HD, cols), BF16),
        in_specs=[pl.BlockSpec(memory_space=pltpu.SMEM), ANY, ANY, VMEM, VMEM, ANY, ANY],
        out_specs=VMEM,
        scratch_shapes=[
            pltpu.VMEM(seq.shape, BF16),
            pltpu.VMEM(o32.shape, F32),
            pltpu.VMEM(cos.shape, F32),
            pltpu.VMEM(sin.shape, F32),
            pltpu.SemaphoreType.DMA((4,)),
        ]
        + [pltpu.VMEM((total, HD), BF16)] * 4
        + [
            pltpu.VMEM((HD, total), BF16),
            pltpu.VMEM((1, total), F32),
            pltpu.VMEM((HD, total), F32),
            pltpu.VMEM((blk, HD), F32),
            pltpu.VMEM((blk, HD), F32),
        ],
        compiler_params=pltpu.CompilerParams(vmem_limit_bytes=60 << 20),
        cost_estimate=pl.CostEstimate(
            flops=20 * total * total * HD, bytes_accessed=8 << 20, transcendentals=total * total // 2
        ),
        name="attn_bwd",
    )(place, seq, o32, lse, do, cos, sin)


def mxu_nt(a, b):
    return lax.dot_general(a, b, (((1,), (1,)), ((), ())), preferred_element_type=F32)


def mxu_tn(a, b):
    return lax.dot_general(a, b, (((0,), (0,)), ((), ())), preferred_element_type=F32)


def ffn_kernel(*refs, count, step):
    x, dy = refs[:count], refs[count : 2 * count]
    gate_hbm, rest_hbm = refs[2 * count : 2 * count + 2]
    refs = refs[2 * count + 2 :]
    dn, br, kept = refs[:count], refs[count : 2 * count], refs[2 * count : 2 * count + 3]
    (
        x_scr,
        dy_scr,
        gate_w,
        up_w,
        down_w,
        hid_scr,
        dgate_scr,
        dup_scr,
        act_scr,
        dn_scr,
        br_scr,
        in_sem,
        w_sem,
        out_sem,
        keep_sem,
    ) = refs[2 * count + 3 :]
    tok, width = x[0].shape
    hidden, parts = gate_w.shape[0], w_sem.shape[1]
    part = hidden // parts
    rows_in = [
        pltpu.make_async_copy(src[i], dst.at[i * tok : (i + 1) * tok], in_sem.at[k, i])
        for k, (src, dst) in enumerate(((x, x_scr), (dy, dy_scr)))
        for i in range(count)
    ]
    gate_in, up_in, down_in = (
        [
            pltpu.make_async_copy(
                src.at[at(j) * part : (at(j) + 1) * part],
                dst.at[j * part : (j + 1) * part],
                w_sem.at[i, j],
            )
            for j in range(parts)
        ]
        for i, (src, at, dst) in enumerate(
            (
                (gate_hbm, lambda j: j, gate_w),
                (rest_hbm, lambda j: 2 * j, up_w),
                (rest_hbm, lambda j: 2 * j + 1, down_w),
            )
        )
    )
    for c in rows_in[:count]:
        c.start()
    for pair in zip(gate_in, up_in, strict=True):
        for c in pair:
            c.start()
    for c in rows_in[count:] + down_in:
        c.start()
    for c in rows_in[:count]:
        c.wait()
    for lo, hi in ((0, parts // 2), (parts // 2, parts)):
        for c in gate_in[lo:hi] + up_in[lo:hi]:
            c.wait()
        here = slice(lo * part, hi * part)
        gate = mxu_nt(x_scr[...], gate_w[here, :])
        up = mxu_nt(x_scr[...], up_w[here, :])
        sig = jax.nn.sigmoid(gate)
        act = gate * sig
        hid_scr[:, here] = (act * up).astype(BF16)
        act_scr[:, here] = act
        dgate_scr[:, here] = up * (sig * (1.0 + gate * (1.0 - sig)))
    for c in rows_in[count:]:
        c.wait()
    for lo, hi in ((0, parts // 2), (parts // 2, parts)):
        for c in down_in[lo:hi]:
            c.wait()
        here = slice(lo * part, hi * part)
        dhidden = mxu_nt(dy_scr[...], down_w[here, :])
        dup_scr[1, :, here] = (dhidden * act_scr[:, here]).astype(BF16)
        dup_scr[0, :, here] = (dhidden * dgate_scr[:, here]).astype(BF16)
    keep = [
        pltpu.make_async_copy(src, dst, keep_sem.at[k])
        for k, (src, dst) in enumerate(zip((hid_scr, dup_scr.at[0], dup_scr.at[1]), kept))
    ]
    for c in keep:
        c.start()
    sent = []
    for n in range(width // step):
        part = slice(n * step, (n + 1) * step)
        total = mxu(dup_scr[0], gate_w[:, part]) + mxu(dup_scr[1], up_w[:, part])
        dn_scr[:, part] = total.astype(BF16)
        br_scr[:, part] = mxu(hid_scr[...], down_w[:, part]).astype(BF16)
        for i in range(count):
            rows = slice(i * tok, (i + 1) * tok)
            for k, (src, dst) in enumerate(((dn_scr, dn[i]), (br_scr, br[i]))):
                sent.append(pltpu.make_async_copy(src.at[rows, part], dst.at[:, part], out_sem.at[k, i, n]))
                sent[-1].start()
    for c in keep + sent:
        c.wait()


def ffn(x, dy, gate_w, rest_w, parts):
    count, (tok, width), hidden = len(x), x[0].shape, gate_w.shape[0]
    rows, step = count * tok, width // 4
    out = pl.pallas_call(
        functools.partial(ffn_kernel, count=count, step=step),
        in_specs=[ANY] * (2 * count + 2),
        out_specs=[ANY] * (2 * count + 3),
        out_shape=[jax.ShapeDtypeStruct((tok, width), BF16)] * (2 * count)
        + [jax.ShapeDtypeStruct((rows, hidden), BF16)] * 3,
        scratch_shapes=[pltpu.VMEM((rows, width), BF16)] * 2
        + [pltpu.VMEM((hidden, width), BF16)] * 3
        + [
            pltpu.VMEM((rows, hidden), BF16),
            pltpu.VMEM((rows, hidden), F32),
            pltpu.VMEM((2, rows, hidden), BF16),
            pltpu.VMEM((rows, hidden), F32),
            pltpu.VMEM((rows, width), BF16),
            pltpu.VMEM((rows, width), BF16),
            pltpu.SemaphoreType.DMA((2, count)),
            pltpu.SemaphoreType.DMA((3, parts)),
            pltpu.SemaphoreType.DMA((2, count, width // step)),
            pltpu.SemaphoreType.DMA((3,)),
        ],
        compiler_params=pltpu.CompilerParams(vmem_limit_bytes=60 << 20),
        cost_estimate=pl.CostEstimate(
            flops=12 * rows * hidden * width, bytes_accessed=6 * hidden * width + 16 * rows * width, transcendentals=rows * hidden
        ),
        name="ffn",
    )(*x, *dy, gate_w, rest_w)
    return out[:count], out[count : 2 * count], out[2 * count :]


def outer_kernel(*refs, lefts, rights):
    order = refs[0]
    left, right = refs[1 : 1 + lefts], refs[1 + lefts : 1 + lefts + rights]
    send, keep, l_scr, r_scr, l_sem, r_sem = refs[1 + lefts + rights :]
    i = pl.program_id(0)

    def into(parts, scr, sem):
        at, out = 0, []
        for k, part in enumerate(parts):
            out.append(pltpu.make_async_copy(part, scr.at[at : at + part.shape[0]], sem.at[k]))
            at += part.shape[0]
        return out

    @pl.when(i == 0)
    def _():
        copies = into(left, l_scr, l_sem) + into(right, r_scr, r_sem)
        for c in copies:
            c.start()
        for c in copies:
            c.wait()

    tile = send.shape[1]
    l = l_scr[:, pl.ds(pl.multiple_of(order[i] * tile, tile), tile)]
    v = mxu_tn(l, r_scr[...]).astype(BF16)

    @pl.when(i < 2)
    def _():
        send[0] = v

    @pl.when(i >= 2)
    def _():
        keep[0] = v


def outer(order, left, right):
    cols, width = left[0].shape[1], right[0].shape[1]
    rows = sum(p.shape[0] for p in left)
    tile = cols // 4
    return pl.pallas_call(
        functools.partial(outer_kernel, lefts=len(left), rights=len(right)),
        grid=(4,),
        in_specs=[pl.BlockSpec(memory_space=pltpu.SMEM)] + [ANY] * (len(left) + len(right)),
        out_specs=[
            pl.BlockSpec((1, tile, width), lambda i: (jnp.minimum(i, 1), 0, 0)),
            pl.BlockSpec((1, tile, width), lambda i: (jnp.maximum(i - 2, 0), 0, 0)),
        ],
        out_shape=[jax.ShapeDtypeStruct((2, tile, width), BF16)] * 2,
        scratch_shapes=[
            pltpu.VMEM((rows, cols), BF16),
            pltpu.VMEM((rows, width), BF16),
            pltpu.SemaphoreType.DMA((len(left),)),
            pltpu.SemaphoreType.DMA((len(right),)),
        ],
        compiler_params=pltpu.CompilerParams(vmem_limit_bytes=60 << 20),
        cost_estimate=pl.CostEstimate(
            flops=2 * rows * cols * width, bytes_accessed=2 * (rows * (cols + width) + cols * width), transcendentals=0
        ),
        name="outer",
    )(order, *left, *right)


def qkv_kernel(near_ref, *refs, count):
    x, parts = refs[:count], refs[count : count + 4]
    cos_ref, sin_ref, out_ref, rows_ref, w_ref, x_scr, w_scr, x_sem, w_sem, out_sem = refs[count + 4 :]
    tok = x[0].shape[0]
    groups, depth, cols = parts[0].shape
    heads, half = out_ref.shape[0], HD // 2
    x_in = [
        pltpu.make_async_copy(x[i], x_scr.at[i * tok : (i + 1) * tok], x_sem.at[i])
        for i in range(count)
    ]
    w_in = [
        pltpu.make_async_copy(
            parts[r].at[g],
            w_scr.at[pl.ds(pl.multiple_of((g * 4 + (near_ref[0] ^ r)) * depth, depth), depth)],
            w_sem.at[r, g],
        )
        for r in range(4)
        for g in range(groups)
    ]
    for c in w_in + x_in:
        c.start()
    for c in w_in:
        c.wait()
    leaving = [pltpu.make_async_copy(w_scr, w_ref, out_sem.at[0])]
    leaving[0].start()
    group = heads * HD
    some = count * tok // 2
    for t in range(2):
        rows = slice(t * some, (t + 1) * some)
        for c in x_in[t * count // 2 : (t + 1) * count // 2]:
            c.wait()
        leaving.append(pltpu.make_async_copy(x_scr.at[rows], rows_ref.at[rows], out_sem.at[1 + t]))
        leaving[-1].start()
        for i in range(3):
            y = mxu(x_scr[rows, :], w_scr[:, i * group : (i + 1) * group]).T
            for h in range(heads):
                at = slice(i * HD, (i + 1) * HD)
                a, b = y[h * HD : h * HD + half], y[h * HD + half : (h + 1) * HD]
                if i < 2:
                    c, s = cos_ref[:, rows], sin_ref[:, rows]
                    a, b = a * c - b * s, b * c + a * s
                out_ref[h, at, rows] = jnp.concatenate([a, b], axis=0).astype(BF16)
    for c in leaving:
        c.wait()


def qkv_of(near, x, parts, cos, sin):
    count, (tok, width) = len(x), x[0].shape
    groups, depth, cols = parts[0].shape
    heads = cols // (3 * HD)
    return pl.pallas_call(
        functools.partial(qkv_kernel, count=count),
        in_specs=[pl.BlockSpec(memory_space=pltpu.SMEM)] + [ANY] * (count + 4) + [VMEM] * 2,
        out_specs=[VMEM, ANY, ANY],
        out_shape=[
            jax.ShapeDtypeStruct((heads, 3 * HD, count * tok), BF16),
            jax.ShapeDtypeStruct((count * tok, width), BF16),
            jax.ShapeDtypeStruct((width, cols), BF16),
        ],
        scratch_shapes=[
            pltpu.VMEM((count * tok, width), BF16),
            pltpu.VMEM((width, cols), BF16),
            pltpu.SemaphoreType.DMA((count,)),
            pltpu.SemaphoreType.DMA((4, groups)),
            pltpu.SemaphoreType.DMA((3,)),
        ],
        compiler_params=pltpu.CompilerParams(vmem_limit_bytes=60 << 20),
        cost_estimate=pl.CostEstimate(
            flops=2 * count * tok * width * cols,
            bytes_accessed=4 * (count * tok * width + width * cols),
            transcendentals=0,
        ),
        name="qkv",
    )(near, *x, *parts, cos, sin)


def turned_rows(d_ref, d_scr, at, rows):
    heads = d_ref.shape[0]
    for i in range(3):
        for h in range(heads):
            top = (i * heads + h) * HD
            d_scr[top : top + HD] = d_ref[h, i * HD : (i + 1) * HD, at : at + rows]


def input_rows_kernel(d_hbm, w_hbm, out_ref, w_scr, d_scr, t_scr, sem, *, slot):
    rows = out_ref.shape[0]
    d_in = pltpu.make_async_copy(d_hbm.at[:, :, slot * rows : (slot + 1) * rows], d_scr, sem.at[0])
    w_in = pltpu.make_async_copy(w_hbm, w_scr, sem.at[1])
    d_in.start()
    w_in.start()
    d_in.wait()
    turned_rows(d_scr, t_scr, 0, rows)
    d = t_scr[...].T
    w_in.wait()
    out_ref[...] = mxu_nt(d, w_scr[...]).astype(BF16)


def input_rows(dqkv, w, slot, tok):
    width, cols = w.shape
    return pl.pallas_call(
        functools.partial(input_rows_kernel, slot=slot),
        in_specs=[ANY, ANY],
        out_specs=VMEM,
        out_shape=jax.ShapeDtypeStruct((tok, width), BF16),
        scratch_shapes=[
            pltpu.VMEM((width, cols), BF16),
            pltpu.VMEM((*dqkv.shape[:2], tok), BF16),
            pltpu.VMEM((cols, tok), BF16),
            pltpu.SemaphoreType.DMA((2,)),
        ],
        compiler_params=pltpu.CompilerParams(vmem_limit_bytes=60 << 20),
        cost_estimate=pl.CostEstimate(
            flops=2 * tok * width * cols, bytes_accessed=2 * width * cols, transcendentals=0
        ),
        name="input_rows",
    )(dqkv, w)


def heads_back_kernel(near_ref, d_ref, x_hbm, w_hbm, *refs, slots, step):
    count = len(slots)
    give_ref, keep_ref = refs[:2]
    out = refs[2 : 2 + count]
    x_scr, w_scr, d_scr, t_scr, y_scr, o_scr, in_sem, out_sem = refs[2 + count :]
    groups, depth = keep_ref.shape[1:3]
    tok, width = out[0].shape
    x_in = pltpu.make_async_copy(x_hbm, x_scr, in_sem.at[0])
    w_in = pltpu.make_async_copy(w_hbm, w_scr, in_sem.at[1])
    w_in.start()
    x_in.start()
    turned_rows(d_ref, d_scr, 0, d_scr.shape[1])
    t_scr[...] = d_scr[...].T
    w_in.wait()
    sent = []
    for n in range(width // step):
        part = slice(n * step, (n + 1) * step)
        o_scr[:, part] = mxu_nt(t_scr[...], w_scr[part, :]).astype(BF16)
        for i, slot in enumerate(slots):
            sent.append(
                pltpu.make_async_copy(
                    o_scr.at[slot * tok : (slot + 1) * tok, part],
                    out[i].at[:, part],
                    out_sem.at[n, i],
                )
            )
            sent[-1].start()
    x_in.wait()
    tile = 4 * depth
    for g in range(groups):
        y_scr[...] = mxu(d_scr[...], x_scr[:, g * tile : (g + 1) * tile]).astype(BF16).T
        for r in range(4):
            rows = pl.ds(pl.multiple_of((near_ref[0] ^ r) * depth, depth), depth)
            (give_ref if r % 2 else keep_ref)[r // 2, g] = y_scr[rows, :]
    for c in sent:
        c.wait()


def heads_back(near, dqkv, x, w, slots, tok):
    rows, width = x.shape
    cols = w.shape[1]
    depth = HD
    groups = width // (4 * depth)
    step = width // 4
    shape = jax.ShapeDtypeStruct((2, groups, depth, cols), BF16)
    out = pl.pallas_call(
        functools.partial(heads_back_kernel, slots=slots, step=step),
        in_specs=[pl.BlockSpec(memory_space=pltpu.SMEM), VMEM, ANY, ANY],
        out_specs=[VMEM, VMEM] + [ANY] * len(slots),
        out_shape=[shape, shape] + [jax.ShapeDtypeStruct((tok, width), BF16)] * len(slots),
        scratch_shapes=[
            pltpu.VMEM((rows, width), BF16),
            pltpu.VMEM((width, cols), BF16),
            pltpu.VMEM((cols, rows), BF16),
            pltpu.VMEM((rows, cols), BF16),
            pltpu.VMEM((4 * depth, cols), BF16),
            pltpu.VMEM((rows, width), BF16),
            pltpu.SemaphoreType.DMA((2,)),
            pltpu.SemaphoreType.DMA((width // step, len(slots))),
        ],
        compiler_params=pltpu.CompilerParams(vmem_limit_bytes=60 << 20),
        cost_estimate=pl.CostEstimate(
            flops=4 * rows * width * cols,
            bytes_accessed=2 * (2 * width * cols + rows * (2 * width + cols)),
            transcendentals=0,
        ),
        name="heads_back",
    )(near, dqkv, x, w)
    return out[:2], out[2:]


def mid_grad_kernel(
    own_ref, across_ref, ahead_ref, mid_ref, dy_ref, scale_ref, gain_ref, w_hbm, dmid_ref, low_ref, out_ref, w_scr, sem
):
    tiles = sem.shape[0]
    width = mid_ref.shape[1]
    rows = w_scr.shape[0] // tiles
    w_in = [
        pltpu.make_async_copy(w_hbm.at[i * rows : (i + 1) * rows], w_scr.at[i * rows : (i + 1) * rows], sem.at[i])
        for i in range(tiles)
    ]
    for c in w_in:
        c.start()
    dn = own_ref[...].astype(F32) + across_ref[...].astype(F32) + ahead_ref[...].astype(F32)
    mid, scale = mid_ref[...], scale_ref[...]
    scaled = gain_ref[...] * dn
    mean = jnp.sum(scaled * mid, axis=-1, keepdims=True) * (1.0 / width)
    dmid = dy_ref[...].astype(F32) + scale * scaled - mid * (scale * scale * scale * mean)
    dmid_ref[...] = dmid
    low = dmid.astype(BF16)
    low_ref[...] = low
    gain_term = jnp.sum(dn * mid * scale, axis=0, keepdims=True)
    high = gain_term.astype(BF16)
    rest = (gain_term - high.astype(F32)).astype(BF16)
    out_ref[:, HD:] = jnp.zeros((out_ref.shape[0], out_ref.shape[1] - HD, out_ref.shape[2]), BF16)
    for h in range(out_ref.shape[0]):
        at = slice(h * HD, (h + 1) * HD)
        out_ref[h, HD : HD + 1, : 2 * HD] = jnp.concatenate([high[:, at], rest[:, at]], axis=1)
    for i in range(tiles):
        w_in[i].wait()
        v = mxu_nt(w_scr[i * rows : (i + 1) * rows, :], low).astype(BF16)
        for j in range(rows // HD):
            out_ref[i * (rows // HD) + j, :HD] = v[j * HD : (j + 1) * HD]


def mid_grad(terms, mid, dy, scale, gain, w):
    tok, width = mid.shape
    owners = w.shape[0] // HD
    return pl.pallas_call(
        mid_grad_kernel,
        in_specs=[VMEM] * 7 + [ANY],
        out_specs=[VMEM] * 3,
        out_shape=[
            jax.ShapeDtypeStruct((tok, width), F32),
            jax.ShapeDtypeStruct((tok, width), BF16),
            jax.ShapeDtypeStruct((owners, HD + 16, tok), BF16),
        ],
        scratch_shapes=[pltpu.VMEM(w.shape, BF16), pltpu.SemaphoreType.DMA((4,))],
        compiler_params=pltpu.CompilerParams(vmem_limit_bytes=60 << 20),
        cost_estimate=pl.CostEstimate(
            flops=2 * tok * width * w.shape[0], bytes_accessed=2 * width * w.shape[0], transcendentals=0
        ),
        name="mid_grad",
    )(*terms, mid, dy, scale, gain, w)


FAR = ("ctx", "row")
NEAR = ("col", "core")


def swap(v, axis):
    return lax.ppermute(v, axis, [(0, 1), (1, 0)])


def shift(v):
    n = lax.axis_size("ctx")
    return lax.ppermute(v, "ctx", [(i, (i + 1) % n) for i in range(n)])


class Flow:
    def __init__(self, steps):
        self.steps = steps
        self.result = None
        self.pending = next(steps)

    def take(self, got):
        try:
            self.pending = self.steps.send(got)
        except StopIteration as end:
            self.pending, self.result = None, end.value

    def run_on(self):
        self.take(self.pending)


def stage(flows, values=(), then=None):
    got, values = lax.optimization_barrier(([f.pending for f in flows], values))
    if then is not None:
        then(values)
    for f, g in zip(flows, got, strict=True):
        f.take(g)
    return values


def spread(v, slots):
    slots[0, 0] = v
    n = lax.axis_size("ctx")
    for c in range(n - 1):
        slots[c + 1, 0], slots[c, 1] = yield shift(slots[c, 0]), swap(slots[c, 0], "row")
    slots[n - 1, 1] = yield swap(slots[n - 1, 0], "row")
    return slots


def spread_late(v, slots):
    slots[0, 0] = v
    n = lax.axis_size("ctx")
    slots[1, 0] = yield shift(v)
    for c in range(1, n - 2):
        slots[c + 1, 0], slots[c - 1, 1] = yield shift(slots[c, 0]), swap(slots[c - 1, 0], "row")
    slots[n - 1, 0], slots[n - 3, 1], slots[n - 2, 1] = yield (
        shift(slots[n - 2, 0]),
        swap(slots[n - 3, 0], "row"),
        swap(slots[n - 2, 0], "row"),
    )
    slots[n - 1, 1] = yield swap(slots[n - 1, 0], "row")
    return slots


def collect(terms, marks, early=False, open_end=False):
    n = lax.axis_size("ctx")
    across = yield swap(terms[1, 1], "row")
    total = terms[1, 0].astype(F32) + across.astype(F32)
    for c in [*range(2, n), 0]:
        send = total.astype(BF16)
        marks.append(send)
        if early and c == 2:
            ahead, across, last = yield (
                shift(send),
                swap(after(terms[c, 1], send), "row"),
                swap(after(terms[0, 1], send), "row"),
            )
        elif early and c == 0:
            ahead, across = (yield shift(send)), last
        else:
            ahead, across = yield shift(send), swap(after(terms[c, 1], send), "row")
        if open_end and c == 0:
            return terms[0, 0], across, ahead
        total = terms[c, 0].astype(F32) + across.astype(F32) + ahead.astype(F32)
    return total


def reduce_near(send, keep):
    got = yield swap(send, "core")
    (give,) = yield for_column(keep, got, 1)
    across = yield swap(give, "col")
    return keep, got, [across]


def for_column(keep, got, pieces):
    rows = keep.shape[1] // pieces
    return [
        (keep[0, p : p + rows].astype(F32) + got[0, p : p + rows].astype(F32)).astype(BF16)
        for p in range(0, keep.shape[1], rows)
    ]


def add_terms(keep, got, across):
    return keep[1].astype(F32) + got[1].astype(F32) + jnp.concatenate(across, axis=0).astype(F32)


def after(v, first):
    return lax.optimization_barrier((v, first))[0]


def beside(v, tok):
    return jnp.pad(v.reshape(*v.shape[:-1], 1, -1), [(0, 0)] * (v.ndim - 1) + [(0, 15), (0, tok - v.shape[-1])])


def by_side(index, mine, theirs):
    return jnp.where(index == 0, mine, theirs), jnp.where(index == 0, theirs, mine)


def to_near(v, col_at, core_at):
    keep, give = by_side(col_at, v[0], v[1])
    got = yield swap(give, "col")
    both = jnp.stack(by_side(col_at, keep, got))
    keep, give = by_side(core_at, both[:, 0], both[:, 1])
    got = yield swap(give, "core")
    return jnp.stack(by_side(core_at, keep, got), axis=1)


def sum_near(give, keep):
    got = yield swap(give, "core")
    other = (keep[1].astype(F32) + got[1].astype(F32)).astype(BF16)
    across = yield swap(other, "col")
    return keep[0].astype(F32) + got[0].astype(F32) + across.astype(F32)


def gather_heads(send):
    mine = yield lax.all_to_all(send, FAR, split_axis=0, concat_axis=0, tiled=True)
    part = mine.shape[0] // 2
    upper, mine_two = yield swap(mine[:part], "col"), swap(mine, "core")
    lower = yield swap(mine[part:], "col")
    other = jnp.concatenate([upper, lower], axis=0)
    other_two = yield swap(other, "core")
    return mine, mine_two, other, other_two


def per_device_split(
    tokens,
    pair_index,
    gain_attn,
    w_query,
    w_key,
    w_value,
    w_out,
    gain_ffn,
    w_gate,
    w_up,
    w_down,
    cotangent,
):
    n_ctx = lax.axis_size("ctx")
    near = lax.axis_size("col") * lax.axis_size("core")
    far = 2 * n_ctx
    tok, width = tokens.shape
    own_in = w_query.shape[0]
    ctx_at, row_at, col_at, core_at = (lax.axis_index(a) for a in ("ctx", "row", "col", "core"))
    near_at = col_at * lax.axis_size("core") + core_at
    blk = near * tok
    rows_here = far * tok
    group = near * HD

    slots = jnp.arange(far, dtype=jnp.int32)
    ctxs = jnp.arange(n_ctx, dtype=jnp.int32)

    def block_of(ctx, row):
        pair = jnp.sum(jnp.where(ctx[:, None] == ctxs[None, :], pair_index[None, :], 0), axis=1)
        return jnp.where(row == 0, pair, far - 1 - pair)

    def place_of_block(block):
        return jnp.sum(jnp.where(block[None, :] == slots[:, None], slots[None, :], 0), axis=1)

    slot_block = block_of((ctx_at - slots % n_ctx + n_ctx) % n_ctx, row_at ^ (slots // n_ctx))
    places = jnp.stack([place_of_block(slot_block), place_of_block(block_of(slots // 2, slots % 2))])
    freq = jnp.exp(jnp.arange(HD // 2, dtype=F32) * (-2.0 * math.log(THETA) / HD))
    token_places = (
        slot_block[:, None] * blk + near_at * tok + jnp.arange(tok, dtype=jnp.int32)[None, :]
    ).reshape(rows_here)
    angle = freq[:, None] * token_places.astype(F32)[None, :]
    cosine, sine = jnp.cos(angle), jnp.sin(angle)
    seq_angle = freq[:, None] * jnp.arange(far * blk, dtype=jnp.int32).astype(F32)[None, :]
    seq_cos, seq_sin = jnp.cos(seq_angle), jnp.sin(seq_angle)

    gain_one = gain_attn.astype(F32)[:, None]
    send = jnp.concatenate(
        [
            (w.astype(F32) * gain_one).astype(BF16).reshape(own_in, far, group)
            for w in (w_query, w_key, w_value)
        ],
        axis=2,
    ).transpose(1, 0, 2)
    x32 = tokens.astype(F32)
    scale_one = lax.rsqrt(jnp.mean(x32 * x32, axis=-1, keepdims=True) + EPS)
    gate_w = lax.all_gather(w_gate, NEAR, axis=0, tiled=True)

    one_flow = Flow(spread((x32 * scale_one).astype(BF16), {}))
    heads_flow = Flow(gather_heads(send))
    w_out = stage([one_flow, heads_flow], w_out)
    out_w = lax.all_gather(w_out, FAR + NEAR, axis=0, tiled=True)
    for _ in range(n_ctx - 3):
        cosine, sine = stage([one_flow, heads_flow], (cosine, sine))
    dy_low = stage([one_flow, heads_flow], cotangent)
    dy_by = {}
    dy_flow = Flow(spread_late(dy_low, dy_by))
    w_rest = stage([one_flow, heads_flow], jnp.concatenate([w_up, w_down], axis=0))
    dy_flow.run_on()
    rest_w = lax.all_gather(w_rest, NEAR, axis=0, tiled=True)
    slot_names = [(c, r) for r in range(2) for c in range(n_ctx)]
    qkv, rows_one, w_heads = qkv_of(
        near_at.reshape(1),
        [one_flow.result[k] for k in slot_names],
        heads_flow.result,
        cosine,
        sine,
    )
    qkv_head, gate_w, seq_cos, seq_sin = stage(
        [dy_flow],
        (
            lax.all_to_all(qkv, NEAR, split_axis=0, concat_axis=0, tiled=True),
            gate_w,
            seq_cos,
            seq_sin,
        ),
    )
    (attn_head, o32, lse, seq), out_w = stage(
        [dy_flow], (attn_fwd(places, qkv_head, beside(gain_ffn, tok), far), out_w)
    )
    attn = stage(
        [dy_flow], lax.all_to_all(attn_head, FAR + NEAR, split_axis=0, concat_axis=0, tiled=True)
    )
    gain_two = attn[:, HD, :own_in].reshape(1, width).astype(F32)
    attn_all = attn[:, :HD]
    attn = attn_all.reshape(width, tok)

    mid = x32 + jnp.einsum("et,ed->td", attn, out_w, preferred_element_type=F32)
    scale_two = lax.rsqrt(jnp.mean(mid * mid, axis=-1, keepdims=True) + EPS)
    normed_two = (mid * scale_two * gain_two).astype(BF16)
    side_flow = Flow(
        to_near(attn_all.reshape(far, 2, 2, HD, tok).transpose(1, 2, 0, 3, 4), col_at, core_at)
    )

    two, dn_by, br_by, kept = {}, {}, {}, []
    two_flow = Flow(spread(normed_two, two))

    def feed(cs, first=()):
        names = [(c, r) for c in cs for r in range(2)]
        rows = after([two[k] for k in names], first)
        dn, br, lefts = ffn(rows, [dy_by[k] for k in names], gate_w, rest_w, near)
        return dict(zip(names, dn, strict=True)), dict(zip(names, br, strict=True)), lefts

    def fed(results):
        dn, br, lefts = results
        dn_by.update(dn)
        br_by.update(br)
        kept.append(lefts)

    stage([two_flow])
    stage([two_flow], feed([0]), fed)
    for c in range(1, n_ctx - 2):
        stage([two_flow], feed([c]), fed)
    marks = []
    dn_flow = Flow(collect(dn_by, marks, open_end=True))
    stage([two_flow, dn_flow, side_flow], feed([n_ctx - 2]), fed)
    last = feed([n_ctx - 1], marks[-1])
    stage([dn_flow, side_flow], last, fed)
    names = [(c, r) for c in range(n_ctx) for r in range(2)]
    two_rows, dy_rows = [two[k] for k in names], [dy_by[k] for k in names]
    tiles = near_at ^ jnp.array([3, 1, 2, 0], jnp.int32)
    lefts = [[k[i] for k in kept] for i in range(3)]
    for _ in range(n_ctx - 4):
        stage([dn_flow])
    gate_terms = outer(tiles, *after((lefts[1], two_rows), marks[-1]))
    gate_flow = Flow(reduce_near(*stage([dn_flow], gate_terms)))
    up_terms = outer(tiles, *after((lefts[2], two_rows), marks[-1]))
    up_terms, br_by = stage([dn_flow, gate_flow], (up_terms, br_by))
    up_send, up_keep = up_terms
    dmid, dmid_low, dattn = mid_grad(dn_flow.result, mid, cotangent, scale_two, gain_two, out_w)
    dmid_near = lax.all_gather(dmid_low, NEAR, axis=0, tiled=True)
    br_marks = []
    br_flow = Flow(collect(br_by, br_marks, early=True, open_end=True))
    down_terms = outer(tiles, *after((lefts[0], dy_rows), dattn))
    gate_flow.pending = after(gate_flow.pending, dattn)
    attn_side = after(side_flow.result, dattn).transpose(2, 3, 0, 1, 4).reshape(far, HD, blk)
    out_term = jnp.einsum("gft,td->gfd", attn_side, dmid_near, preferred_element_type=F32)
    dattn_head, down_terms, out_term, up_got = stage(
        [gate_flow, br_flow],
        (
            lax.all_to_all(dattn, FAR + NEAR, split_axis=0, concat_axis=0, tiled=True),
            down_terms,
            out_term.astype(BF16),
            swap(up_send, "core"),
        ),
    )
    out_grad = lax.psum_scatter(
        out_term.reshape(far * HD, width), FAR, scatter_dimension=0, tiled=True
    )
    down_send, down_keep = down_terms
    gain_parts = dattn_head[:, HD, : 2 * own_in].astype(F32)
    dqkv_head, down_got = stage(
        [gate_flow, br_flow],
        (
            attn_bwd(places, seq, o32, lse, dattn_head, seq_cos, seq_sin, far),
            swap(down_send, "core"),
        ),
    )
    exchange = lax.all_to_all(dqkv_head, NEAR, split_axis=0, concat_axis=0, tiled=True)
    up_give = for_column(*after((up_keep, up_got), br_marks[-1]), 2)
    (down_keep, down_got) = after((down_keep, down_got), br_marks[-1])
    dqkv, up_give, down_give = stage(
        [br_flow], (exchange, up_give, for_column(down_keep, down_got, 1)[0])
    )
    dx = {(1, 1): input_rows(dqkv, w_heads, slot_names.index((1, 1)), tok)}
    dx_flow = Flow(collect(dx, marks))
    up_first, up_second = up_give
    rest = [i for i in range(far) if slot_names[i] != (1, 1)]

    def add_rows(values):
        dx.update({slot_names[i]: v for i, v in zip(rest, values[1], strict=True)})

    heads_terms, _, up_first = stage(
        [dx_flow, br_flow],
        (*heads_back(near_at.reshape(1), after(dqkv, dx[1, 1]), rows_one, w_heads, rest, tok), swap(up_first, "col")),
        add_rows,
    )
    heads_flow = Flow(sum_near(*heads_terms))
    stage([heads_flow])
    gate_terms, out_grad, up_second = stage(
        [dx_flow, heads_flow], (gate_flow.result, out_grad, up_second)
    )
    back = lax.all_to_all(
        heads_flow.result.astype(BF16), FAR, split_axis=0, concat_axis=0, tiled=True
    )
    gate_terms, down_give, up_second, branch = stage(
        [dx_flow], (gate_terms, down_give, swap(up_second, "col"), br_flow.result)
    )
    up_terms = up_keep, up_got, [up_first, up_second]
    gate_terms, up_terms, branch = after((gate_terms, up_terms, branch), marks[-1])
    gate_grad, up_grad = add_terms(*gate_terms), add_terms(*up_terms)
    down_across = stage([dx_flow], swap(down_give, "col"))
    down_grad = add_terms(down_keep, down_got, [down_across])
    scaled_one = dx_flow.result
    input_grad = (
        dmid
        + scale_one * scaled_one
        - x32 * scale_one**3 * jnp.mean(scaled_one * x32, axis=-1, keepdims=True)
    )
    back, input_grad, down_grad = lax.optimization_barrier((back, input_grad, down_grad))
    back = back.astype(F32)
    raw = [
        back[:, :, i * group : (i + 1) * group].transpose(1, 0, 2).reshape(own_in, -1)
        for i in range(3)
    ]
    gain_attn_grad = sum(
        jnp.sum(w.astype(F32) * g, axis=1)
        for w, g in zip((w_query, w_key, w_value), raw, strict=True)
    )
    query_grad, key_grad, value_grad = (g * gain_one for g in raw)
    gain_ffn_grad = jnp.sum(gain_parts[:, :own_in] + gain_parts[:, own_in:], axis=0)
    return (
        (mid + sum(v.astype(F32) for v in branch)).astype(BF16),
        input_grad,
        gain_attn_grad,
        query_grad,
        key_grad,
        value_grad,
        out_grad.astype(F32),
        gain_ffn_grad,
        gate_grad,
        up_grad,
        down_grad,
    )


def solution(mesh):
    n_ctx, n_fsdp = mesh.shape["ctx"], mesh.shape["fsdp"]

    def step(*args):
        if n_fsdp == 8 and n_ctx == 4 and n_ctx * n_fsdp * HD == args[3].shape[1]:
            body, axes = per_device_split, FAR + NEAR
            over = Mesh(np.asarray(mesh.devices).reshape(n_ctx, 2, 2, 2), axes)
        else:
            body, axes, over = per_device_any, ("ctx", "fsdp"), mesh
        rows, line = P(axes, None), P(axes)
        return jax.shard_map(
            body,
            mesh=over,
            in_specs=(rows, P(), line, rows, rows, rows, rows, line, rows, rows, rows, rows),
            out_specs=(rows, rows, line, rows, rows, rows, rows, line, rows, rows, rows),
            check_vma=False,
        )(*args)

    return step
```
